32 devices in a mesh: slab: 4 (over z), blk: 8 (over y, x, core).
Axes of the slice: x: 2, y: 2, z: 4, core: 2. Of those that a mesh axis runs over, the one named last changes fastest.
Arguments:
- fixed_image: bfloat16 [256, 128, 128], P('blk', 'slab'), may hold values from -6 to 6
- moving_image: bfloat16 [256, 128, 128], P('blk', 'slab'), may hold values from -6 to 6
- fetch_owner: int32 [8, 4, 4, 4], P('blk', 'slab'), may hold values from 0 to 7, as said below
- fetch_block: int32 [8, 4, 4, 4], P('blk', 'slab'), may hold values from 0 to 3
- fetch_count: int32 [8, 4, 4], P('blk', 'slab'), may hold values from 1 to 4, as said below
- interp_level: int32 [8, 4, 4, 3, 4], P('blk', 'slab'), may hold values from 0 to 7
- block_mask: int32 [8, 4, 4], P('blk', 'slab'), may hold values 0 or 1
Outputs:
- update: float32 [3, 256, 128, 128], P(None, 'blk', 'slab')
The draws below stay inside these ranges and needn't reach their ends.
Inputs may be any that keep to these rules, and one draw needn't show every extreme that they name: `fetch_owner`: entries k < fetch_count of one device's lists name any one owner at most 2 times in all; in every draw some owner is named exactly 2 times by every device of its slab. Entries k >= fetch_count are not read. `fetch_count`: every device has a block whose list holds 4 entries.
All inputs are finite; a program needn't handle non-finite values. No bound on the sum of `block_mask` on one device may be relied on, other than what follows from the above.
Results may differ from the reference program's by a relative error of at most 0.006.
Values may be sent and summed in bfloat16 or wider, within the bound.
A program may use at most 64 MiB of HBM per device.

```python
import math
import jax
import jax.numpy as jnp
from jax import lax

BLOCK_SIDE = 32
BLOCKS_DEV = 4
MAX_LIST = 4
LEVELS = 8
BOX_RADIUS = 2
SMOOTH_RADIUS = 3
PEER_SLOTS = 2
WIDTH_X = 256
WIDTH_Z = 128
WIDTH_Y = 128
N_SLAB = 4
N_BLK = 8


def list_layout(key):
    base_key = jax.random.fold_in(key, 4101)
    key_count, key_full, key_hot, key_order, key_owner = jax.random.split(base_key, 5)
    entry_total = BLOCKS_DEV * MAX_LIST
    counts = jax.random.randint(key_count, (N_BLK, N_SLAB, BLOCKS_DEV), 1, MAX_LIST + 1)
    full_at = jax.random.randint(key_full, (N_BLK, N_SLAB, 1), 0, BLOCKS_DEV)
    counts = jnp.where(jnp.arange(BLOCKS_DEV)[None, None, :] == full_at, MAX_LIST, counts).astype(jnp.int32)
    in_list = (jnp.arange(MAX_LIST)[None, None, None, :] < counts[..., None]).reshape(N_BLK, N_SLAB, entry_total)
    scores = jax.random.randint(key_order, (N_BLK, N_SLAB, entry_total), 0, 2 ** 20) * entry_total + jnp.arange(entry_total)[None, None, :]
    scores = jnp.where(in_list, scores, scores + 2 ** 30)
    order_pos = jnp.argsort(scores, axis=-1)
    list_rank = jnp.argsort(order_pos, axis=-1).astype(jnp.int32)
    hot_owner = jax.random.randint(key_hot, (N_SLAB,), 0, N_BLK)
    owner_scores = jax.random.randint(key_owner, (N_BLK, N_SLAB, N_BLK), 0, 2 ** 20) * N_BLK + jnp.arange(N_BLK)[None, None, :]
    owner_scores = jnp.where(jnp.arange(N_BLK)[None, None, :] == hot_owner[None, :, None], 2 ** 30, owner_scores)
    owner_order = jnp.argsort(owner_scores, axis=-1).astype(jnp.int32)
    other_pos = jnp.mod(jnp.maximum(list_rank - PEER_SLOTS, 0), N_BLK - 1)
    other_owner = jnp.take_along_axis(owner_order, other_pos, axis=-1)
    owners = jnp.where(list_rank < PEER_SLOTS, hot_owner[None, :, None], other_owner)
    return (owners.reshape(N_BLK, N_SLAB, BLOCKS_DEV, MAX_LIST).astype(jnp.int32), counts)


def draw_fetch_owner(key, part):
    return list_layout(key)[0]


def draw_fetch_count(key, part):
    return list_layout(key)[1]


def plant(drawn, rng, low, top_value):
    dims = drawn.shape
    index_at = [jax.random.randint(jax.random.fold_in(rng, axis), (), 0, dims[axis]) for axis in range(len(dims))]
    drawn = drawn.at[tuple(index_at)].set(low)
    longest = dims.index(max(dims))
    index_at[longest] = (index_at[longest] + 1) % dims[longest]
    return drawn.at[tuple(index_at)].set(top_value)


def level_of(own_key, shape, shards, low, high):
    def one(axis_at, shards_of):
        heights = jax.random.uniform(jax.random.fold_in(jax.random.fold_in(own_key, 6), axis_at), (shards_of,), jnp.float32, low / len(shards), high / len(shards))
        return jnp.repeat(jnp.exp(heights), shape[axis_at] // shards_of).reshape((-1,) + (1,) * (len(shape) - axis_at - 1))

    loudness = one(*shards[0])
    for cut in shards[1:]:
        loudness = loudness * one(*cut)
    return loudness


def noise(own_key, shape, deviation, most, shards=(), held_as=jnp.bfloat16):
    loudness = level_of(own_key, shape, shards, -0.22, 0.18) if shards else 1.0
    entries = jax.random.normal(own_key, shape, jnp.float32) * deviation * loudness
    return jnp.minimum(jnp.maximum(entries, -most), most).astype(held_as)


def setup_inputs(seed: int = 0) -> dict:
    key_of = jax.random.split(jax.random.key(seed), 8)
    return {
        "fixed_image": noise(key_of[0], (WIDTH_X, WIDTH_Z, WIDTH_Y), 1.0, 6.0, ((0, 8), (1, 4))),
        "moving_image": noise(key_of[1], (WIDTH_X, WIDTH_Z, WIDTH_Y), 1.0, 6.0, ((0, 8), (1, 4))),
        "fetch_owner": draw_fetch_owner(jax.random.fold_in(key_of[7], 71), 0),
        "fetch_block": plant(jax.random.randint(key_of[3], (N_BLK, N_SLAB, BLOCKS_DEV, MAX_LIST), 0, BLOCKS_DEV), jax.random.fold_in(key_of[3], 1), 0, BLOCKS_DEV - 1).astype(jnp.int32),
        "fetch_count": draw_fetch_count(jax.random.fold_in(key_of[7], 71), 0),
        "interp_level": plant(jax.random.randint(key_of[5], (N_BLK, N_SLAB, BLOCKS_DEV, 3, MAX_LIST), 0, LEVELS), jax.random.fold_in(key_of[5], 1), 0, LEVELS - 1).astype(jnp.int32),
        "block_mask": plant((jax.random.randint(key_of[6], (N_BLK, N_SLAB, BLOCKS_DEV), 0, 4) < 3).astype(jnp.int32), jax.random.fold_in(key_of[6], 1), 0, 1),
    }


sigma_smooth = 1.5
step_length = 2.0
var_eps = 1e-05
peak_eps = 1e-06

def smooth_weights(radius):
    weights_raw = [math.exp(-(offset * offset) / (2.0 * sigma_smooth * sigma_smooth)) for offset in range(-radius, radius + 1)]
    weights_total = sum(weights_raw)
    return [weight_one / weights_total for weight_one in weights_raw]

def window_sum(volume, axis_pos, length, weights):
    result = weights[0] * lax.slice_in_dim(volume, 0, length, axis=axis_pos)
    for offset in range(1, len(weights)):
        result = result + weights[offset] * lax.slice_in_dim(volume, offset, offset + length, axis=axis_pos)
    return result

def resample(blocks, fractions):
    for axis_step in range(3):
        axis_now = blocks.ndim - 3 + axis_step
        side_len = blocks.shape[axis_now]
        shifted = jnp.concatenate([lax.slice_in_dim(blocks, 1, side_len, axis=axis_now), lax.slice_in_dim(blocks, side_len - 1, side_len, axis=axis_now)], axis=axis_now)
        factor = fractions[..., axis_step][..., None, None, None]
        blocks = (1.0 - factor) * blocks + factor * shifted
    return blocks

def reference(fixed_image, moving_image, fetch_owner, fetch_block, fetch_count, interp_level, block_mask):
    block_side = BLOCK_SIDE
    blocks_all = moving_image.reshape(N_BLK, block_side, N_SLAB, block_side, BLOCKS_DEV, block_side).transpose(2, 0, 4, 1, 3, 5)
    packed_all = (blocks_all, fetch_owner.transpose(1, 0, 2, 3), fetch_block.transpose(1, 0, 2, 3), fetch_count.transpose(1, 0, 2), interp_level.transpose(1, 0, 2, 3, 4))

    def one_slab(packed):
        slab_blocks, owners, indices, counts, levels = packed
        sources = slab_blocks[owners, indices].astype(jnp.float32)
        fractions = jnp.swapaxes(levels.astype(jnp.float32) / LEVELS, -1, -2)
        resampled = resample(sources, fractions)
        in_list = jnp.arange(MAX_LIST)[None, None, :] < counts[:, :, None]
        weights = jnp.where(in_list, 1.0, 0.0) / counts[:, :, None].astype(jnp.float32)
        return lax.optimization_barrier(jnp.sum(resampled * weights[..., None, None, None], axis=2))
    warped_blocks = lax.map(one_slab, packed_all)
    warped = warped_blocks.astype(jnp.bfloat16).transpose(1, 3, 0, 4, 2, 5).reshape(WIDTH_X, WIDTH_Z, WIDTH_Y)
    warped = lax.optimization_barrier(warped)
    radius = BOX_RADIUS
    box_ones = [1.0] * (2 * radius + 1)
    count_box = float((2 * radius + 1) ** 3)

    def boxed(volume):
        padded = jnp.pad(volume, radius)
        result = window_sum(padded, 0, WIDTH_X, box_ones)
        result = window_sum(result, 1, WIDTH_Z, box_ones)
        return window_sum(result, 2, WIDTH_Y, box_ones)
    fixed_f = fixed_image.astype(jnp.float32)
    moving_f = warped.astype(jnp.float32)
    mean_fixed = boxed(fixed_f) / count_box
    mean_moving = boxed(moving_f) / count_box
    var_fixed = boxed(fixed_f * fixed_f) / count_box - mean_fixed * mean_fixed + var_eps
    var_moving = boxed(moving_f * moving_f) / count_box - mean_moving * mean_moving + var_eps
    covariance = boxed(fixed_f * moving_f) / count_box - mean_fixed * mean_moving
    padded_m = jnp.pad(moving_f, 1)
    grad_x = (padded_m[2:, 1:-1, 1:-1] - padded_m[:-2, 1:-1, 1:-1]) * 0.5
    grad_z = (padded_m[1:-1, 2:, 1:-1] - padded_m[1:-1, :-2, 1:-1]) * 0.5
    grad_y = (padded_m[1:-1, 1:-1, 2:] - padded_m[1:-1, 1:-1, :-2]) * 0.5
    mask_voxel = jnp.broadcast_to(block_mask.astype(jnp.float32)[:, None, :, None, :, None], (N_BLK, block_side, N_SLAB, block_side, BLOCKS_DEV, block_side)).reshape(WIDTH_X, WIDTH_Z, WIDTH_Y)
    scalar_term = mask_voxel * 2.0 * covariance / (var_fixed * var_moving) * (fixed_f - mean_fixed - covariance / var_moving * (moving_f - mean_moving))
    forces = jnp.stack([scalar_term * grad_x, scalar_term * grad_z, scalar_term * grad_y]).astype(jnp.bfloat16)
    forces = lax.optimization_barrier(forces)
    smooth_taps = smooth_weights(SMOOTH_RADIUS)
    reach = SMOOTH_RADIUS
    padded_s = jnp.pad(forces.astype(jnp.float32), ((0, 0), (reach, reach), (reach, reach), (reach, reach)))
    smoothed = window_sum(padded_s, 1, WIDTH_X, smooth_taps)
    smoothed = window_sum(smoothed, 2, WIDTH_Z, smooth_taps)
    smoothed = window_sum(smoothed, 3, WIDTH_Y, smooth_taps)
    norms = jnp.sqrt(smoothed[0] * smoothed[0] + smoothed[1] * smoothed[1] + smoothed[2] * smoothed[2])
    peak_norm = jnp.max(norms)
    return step_length * smoothed / (peak_norm + peak_eps)
```

```python
import functools
import math

import jax
import jax.numpy as jnp
from jax import lax
from jax.experimental import pallas as pl
from jax.experimental.pallas import tpu as pltpu
from jax.sharding import PartitionSpec as P

LEVELS = 8
BOX_RADIUS = 2
SMOOTH_RADIUS = 3
HALO = BOX_RADIUS + SMOOTH_RADIUS

sigma_smooth = 1.5
step_length = 2.0
var_eps = 1e-05
peak_eps = 1e-06

SIDE = 32
LANES = 128
PLANES = SIDE + 2 * HALO
ROWS = 48
FIRST = 8
FPLANES = SIDE + 2 * SMOOTH_RADIUS
FROWS = 40
F32 = jnp.float32
BF16 = jnp.bfloat16
MESH = pl.DeviceIdType.MESH
DIRECTIONS = ((1, 0), (-1, 0), (0, 1), (0, -1), (1, 1), (1, -1), (-1, 1), (-1, -1))


def smooth_weights(radius):
    weights_raw = [
        math.exp(-(offset * offset) / (2.0 * sigma_smooth * sigma_smooth))
        for offset in range(-radius, radius + 1)
    ]
    weights_total = sum(weights_raw)
    return [weight_one / weights_total for weight_one in weights_raw]


def kernel(
    n_slab,
    n_blk,
    fixed_ref,
    moving_ref,
    owner_ref,
    block_ref,
    count_ref,
    level_ref,
    mask_ref,
    out_ref,
    scale_ref,
    gath,
    select,
    acc,
    f_ext,
    m_ext,
    ybuf,
    zbox,
    f_mean,
    f_inv,
    f_dev,
    grad_y,
    forces,
    ysm,
    zsm,
    mask_pl,
    band_m,
    band_2,
    band_s,
    fx_send,
    fz_send,
    fx_recv,
    fz_recv,
    fc_recv,
    mx_send,
    mz_send,
    mx_recv,
    mz_recv,
    mc_recv,
    pk_send,
    pk_blk,
    pk_slab,
    ag_ssem,
    ag_rsem,
    f_ssem,
    f_rsem,
    m_ssem,
    m_rsem,
    pb_ssem,
    pb_rsem,
    ps_ssem,
    ps_rsem,
):
    me_s = lax.axis_index("slab")
    me_b = lax.axis_index("blk")
    chips = n_blk // 2
    chip = me_b // 2
    core = me_b % 2
    taps = smooth_weights(SMOOTH_RADIUS)

    def there(dx, dz):
        ok = None
        for d, me, n in ((dx, me_b, n_blk), (dz, me_s, n_slab)):
            if d == 0:
                continue
            now = me + d < n if d > 0 else me + d >= 0
            ok = now if ok is None else jnp.logical_and(ok, now)
        return ok

    barrier = pltpu.get_barrier_semaphore()
    for d in range(1, n_blk):
        pl.semaphore_signal(
            barrier, inc=1, device_id=(me_s, (me_b + d) % n_blk), device_id_type=MESH
        )
    for d in range(1, n_slab):
        pl.semaphore_signal(
            barrier, inc=1, device_id=((me_s + d) % n_slab, me_b), device_id_type=MESH
        )
    for dx, dz in DIRECTIONS[4:]:

        @pl.when(there(dx, dz))
        def _():
            pl.semaphore_signal(
                barrier, inc=1, device_id=(me_s + dz, me_b + dx), device_id_type=MESH
            )

    wide_x = jnp.where(me_b > 0, 1, 0) + jnp.where(me_b < n_blk - 1, 1, 0)
    wide_z = jnp.where(me_s > 0, 1, 0) + jnp.where(me_s < n_slab - 1, 1, 0)
    pl.semaphore_wait(barrier, n_blk - 1 + n_slab - 1 + wide_x * wide_z)

    def spread(e):
        return pltpu.make_async_remote_copy(
            src_ref=moving_ref,
            dst_ref=gath.at[2 * e],
            send_sem=ag_ssem.at[2 * e],
            recv_sem=ag_rsem.at[2 * e],
            device_id=(me_s, 2 * ((chip + e) % chips) + core),
            device_id_type=MESH,
        )

    def to_sibling(e):
        return pltpu.make_async_remote_copy(
            src_ref=moving_ref if e == 0 else gath.at[2 * e],
            dst_ref=gath.at[2 * e + 1],
            send_sem=ag_ssem.at[2 * e + 1],
            recv_sem=ag_rsem.at[2 * e + 1],
            device_id=(me_s, 2 * chip + 1 - core),
            device_id_type=MESH,
        )

    for e in range(1, chips):
        spread(e).start()
    to_sibling(0).start()

    def rim_copies(x_send, z_send, x_recv, z_recv, c_recv, ssem, rsem):
        copies = []
        for i, (dx, dz) in enumerate(DIRECTIONS):
            if dz == 0:
                src, dst = x_send.at[(dx + 1) // 2], x_recv.at[(dx + 1) // 2]
            elif dx == 0:
                src, dst = z_send.at[(dz + 1) // 2], z_recv.at[(dz + 1) // 2]
            else:
                src = z_send.at[(dz + 1) // 2, :, pl.ds(16 if dx > 0 else 0, 16), :]
                dst = c_recv.at[i - 4]
            copies.append(
                pltpu.make_async_remote_copy(
                    src_ref=src,
                    dst_ref=dst,
                    send_sem=ssem.at[i],
                    recv_sem=rsem.at[i],
                    device_id=(me_s + dz, me_b + dx),
                    device_id_type=MESH,
                )
            )
        return copies

    def start_all(copies):
        for (dx, dz), copy in zip(DIRECTIONS, copies):
            pl.when(there(dx, dz))(copy.start)

    def finish_all(copies):
        for (dx, dz), copy in zip(DIRECTIONS, copies):
            pl.when(there(dx, dz))(copy.wait_send)

    def pack_rims(ext, x_send, z_send):
        flat = ext.reshape(PLANES * ROWS, LANES)
        for j in range(HALO):
            for side, at in ((0, j), (1, SIDE - HALO + j)):
                z_send[side, j] = flat[
                    pl.ds(HALO * ROWS + FIRST + at, SIDE, stride=ROWS), :
                ].astype(BF16)
                x_send[side, j] = ext[HALO + at, FIRST : FIRST + SIDE, :].astype(BF16)

    def fill_rims(copies, ext, x_recv, z_recv, c_recv, mask):
        flat = ext.reshape(PLANES * ROWS, LANES)
        for i, (dx, dz) in enumerate(DIRECTIONS):
            at_x = 0 if dx > 0 else HALO + SIDE
            at_z = FIRST - HALO if dz > 0 else FIRST + SIDE
            region = {1: 0, 0: 1, -1: 2}[dx]
            row_at = {1: 0, 0: SMOOTH_RADIUS, -1: SMOOTH_RADIUS + SIDE}[dz]
            row_n = SIDE if dz == 0 else SMOOTH_RADIUS

            @pl.when(there(-dx, -dz))
            def _():
                copies[i].wait_recv()
                side_x, side_z = (dx + 1) // 2, (dz + 1) // 2
                for j in range(HALO):
                    if dz == 0:
                        ext[at_x + j, FIRST : FIRST + SIDE, :] = x_recv[side_x, j].astype(F32)
                    elif dx == 0:
                        flat[pl.ds(HALO * ROWS + at_z + j, SIDE, stride=ROWS), :] = z_recv[
                            side_z, j
                        ].astype(F32)
                    else:
                        rows = c_recv[i - 4, j].astype(F32)
                        rows = rows[16 - HALO :] if dx > 0 else rows[:HALO]
                        flat[pl.ds(at_x * ROWS + at_z + j, HALO, stride=ROWS), :] = rows
                if mask:
                    if dz == 0:
                        plane = x_recv[side_x, HALO].astype(F32)
                    elif dx == 0:
                        plane = z_recv[side_z, HALO].astype(F32)
                    else:
                        plane = c_recv[i - 4, HALO].astype(F32)
                    mask_pl[region, row_at : row_at + row_n, :] = plane[:row_n]

    lane = lax.broadcasted_iota(jnp.int32, (1, LANES), 1)

    def by_block(scalars):
        vec = jnp.full((1, LANES), scalars[3], jnp.int32)
        for g in range(3):
            vec = jnp.where(lane // SIDE == g, scalars[g], vec)
        return vec

    for ext in (f_ext, m_ext):

        @pl.loop(0, PLANES)
        def _(x):
            ext[x] = jnp.zeros((ROWS, LANES), F32)

    mask_pl[...] = jnp.zeros_like(mask_pl)
    own_mask = by_block([mask_ref[0, 0, g] for g in range(4)]).astype(F32)
    mask_rows = jnp.broadcast_to(own_mask, (SIDE, LANES))
    mask_pl[1, SMOOTH_RADIUS : SMOOTH_RADIUS + SIDE, :] = mask_rows

    @pl.loop(0, SIDE)
    def _(x):
        f_ext[HALO + x, FIRST : FIRST + SIDE, :] = fixed_ref[x].astype(F32)

    pack_rims(f_ext, fx_send, fz_send)
    for side in range(2):
        fx_send[side, HALO] = mask_rows.astype(BF16)
        fz_send[side, HALO] = mask_rows.astype(BF16)
    f_copies = rim_copies(fx_send, fz_send, fx_recv, fz_recv, fc_recv, f_ssem, f_rsem)
    start_all(f_copies)

    place, frac_x, frac_y, frac_z, weight = [], [], [], [], []
    counts = by_block([count_ref[0, 0, g] for g in range(4)])
    for k in range(4):
        fracs = [
            by_block([level_ref[0, 0, g, a, k] for g in range(4)]).astype(F32) / LEVELS
            for a in range(3)
        ]
        frac_x.append(fracs[0])
        frac_z.append(fracs[1])
        frac_y.append(fracs[2])
        place.append(
            by_block([owner_ref[0, 0, g, k] for g in range(4)]) * LANES
            + by_block([block_ref[0, 0, g, k] for g in range(4)]) * SIDE
            + lane % SIDE
        )
        weight.append(jnp.where(counts > k, 1.0, 0.0) / counts.astype(F32))
    sub = lax.broadcasted_iota(jnp.int32, (LANES, LANES), 0)
    for e in range(chips):
        for p in range(2):
            base = (2 * ((chip + chips - e) % chips) + (core if p == 0 else 1 - core)) * LANES
            for k in range(4):
                first = place[k] - base
                second = first + jnp.where(lane % SIDE == SIDE - 1, 0, 1)
                f_y = frac_y[k]
                select[e, p * LANES : (p + 1) * LANES, k * LANES : (k + 1) * LANES] = (
                    jnp.where(sub == first, 1.0 - f_y, 0.0) + jnp.where(sub == second, f_y, 0.0)
                ).astype(BF16)

    off = sub - lax.broadcasted_iota(jnp.int32, (LANES, LANES), 1)
    band = jnp.where(jnp.abs(off) <= BOX_RADIUS, 1.0, 0.0).astype(BF16)
    band_m[:, :LANES] = band
    band_m[:, LANES:] = (
        jnp.where(off == 1, 0.5, 0.0) - jnp.where(off == -1, 0.5, 0.0)
    ).astype(BF16)
    band_2[:LANES] = band
    band_2[LANES:] = band
    bell = jnp.zeros((LANES, LANES), F32)
    for t in range(2 * SMOOTH_RADIUS + 1):
        bell = jnp.where(off == t - SMOOTH_RADIUS, taps[t], bell)
    bell_hi = bell.astype(BF16)
    band_s[:, :LANES] = bell_hi
    band_s[:, LANES:] = (bell - bell_hi.astype(F32)).astype(BF16)

    def halves(product):
        high = product.astype(BF16)
        return jnp.concatenate([high, (product - high.astype(F32)).astype(BF16)], axis=1)

    def z_sum(ref, q, j):
        total = ref[q, j, 3 : 3 + FROWS, :]
        for t in range(1, 5):
            total = total + ref[q, j, 3 + t : 3 + t + FROWS, :]
        return total

    def x_sum(q, i):
        total = zbox[q, i]
        for t in range(1, 5):
            total = total + zbox[q, i + t]
        return total

    count_box = float((2 * BOX_RADIUS + 1) ** 3)
    group = 7

    fill_rims(f_copies, f_ext, fx_recv, fz_recv, fc_recv, True)

    @pl.loop(0, PLANES // group)
    def _(step):
        planes = f_ext[pl.ds(step * group, group)].reshape(group * ROWS, LANES)
        y_f = jnp.dot(planes.astype(BF16), band, preferred_element_type=F32)
        y_ff = jnp.dot(halves(planes * planes), band_2[...], preferred_element_type=F32)
        ybuf[0] = y_f.reshape(group, ROWS, LANES)
        ybuf[1] = y_ff.reshape(group, ROWS, LANES)
        for j in range(group):
            for q in range(2):
                zbox[q, step * group + j] = z_sum(ybuf, q, j)

    @pl.loop(0, FPLANES)
    def _(i):
        mean = x_sum(0, i) / count_box
        var = x_sum(1, i) / count_box - mean * mean + var_eps
        f_mean[i] = mean
        f_inv[i] = 1.0 / var
        f_dev[i] = f_ext[i + 2, 5 : 5 + FROWS, :] - mean

    @pl.loop(0, SIDE)
    def _(x):
        gath[0, x] = moving_ref[x]

    for e in range(chips):
        if e > 0:
            spread(e).wait_recv()
            to_sibling(e).start()
    for e in range(chips):
        to_sibling(e).wait_recv()

        @pl.loop(0, 4)
        def _(part):
            at = pl.ds(part * 8, 8)
            pair = jnp.concatenate(
                [gath[2 * e, at].reshape(256, LANES), gath[2 * e + 1, at].reshape(256, LANES)],
                axis=1,
            )
            got = jnp.dot(pair, select[e], preferred_element_type=F32)
            rows = pl.ds(part * 256, 256)
            if e == 0:
                acc[rows, :] = got
            else:
                acc[rows, :] = acc[rows, :] + got

    last_row = lax.broadcasted_iota(jnp.int32, (SIDE, LANES), 0) == SIDE - 1

    @pl.loop(0, SIDE)
    def _(x):
        here = pl.ds(pl.multiple_of(x * SIDE, SIDE), SIDE)
        after = pl.ds(pl.multiple_of(jnp.minimum(x + 1, SIDE - 1) * SIDE, SIDE), SIDE)
        stay = jnp.zeros((SIDE, LANES), F32)
        move = jnp.zeros((SIDE, LANES), F32)
        for k in range(4):
            cols = slice(k * LANES, (k + 1) * LANES)
            mixed = (1.0 - frac_x[k]) * acc[here, cols] + frac_x[k] * acc[after, cols]
            stay = stay + (weight[k] * (1.0 - frac_z[k])) * mixed
            move = move + (weight[k] * frac_z[k]) * mixed
        moved = jnp.where(last_row, move, pltpu.roll(move, SIDE - 1, 0))
        m_ext[HALO + x, FIRST : FIRST + SIDE, :] = (stay + moved).astype(BF16).astype(F32)

    pack_rims(m_ext, mx_send, mz_send)
    m_copies = rim_copies(mx_send, mz_send, mx_recv, mz_recv, mc_recv, m_ssem, m_rsem)
    start_all(m_copies)
    fill_rims(m_copies, m_ext, mx_recv, mz_recv, mc_recv, False)

    @pl.loop(0, PLANES // group)
    def _(step):
        at = pl.ds(step * group, group)
        m_now = m_ext[at].reshape(group * ROWS, LANES)
        f_now = f_ext[at].reshape(group * ROWS, LANES)
        y_m = jnp.dot(m_now.astype(BF16), band_m[...], preferred_element_type=F32)
        products = jnp.concatenate([halves(m_now * m_now), halves(f_now * m_now)], axis=0)
        y_p = jnp.dot(products, band_2[...], preferred_element_type=F32)
        ybuf[0] = y_m[:, :LANES].reshape(group, ROWS, LANES)
        ybuf[1] = y_p[: group * ROWS].reshape(group, ROWS, LANES)
        ybuf[2] = y_p[group * ROWS :].reshape(group, ROWS, LANES)
        grad_y[at] = y_m[:, LANES:].reshape(group, ROWS, LANES)
        for j in range(group):
            for q in range(3):
                zbox[q, step * group + j] = z_sum(ybuf, q, j)

    @pl.loop(0, FPLANES)
    def _(i):
        mean = x_sum(0, i) / count_box
        var = x_sum(1, i) / count_box - mean * mean + var_eps
        cov = x_sum(2, i) / count_box - f_mean[i] * mean
        inv = 1.0 / var
        slope = cov * inv
        center = m_ext[i + 2, 5 : 5 + FROWS, :]
        term = 2.0 * slope * f_inv[i] * (f_dev[i] - slope * (center - mean))
        region = jnp.where(i >= SMOOTH_RADIUS, 1, 0) + jnp.where(i >= SMOOTH_RADIUS + SIDE, 1, 0)
        term = jnp.where(mask_pl[region] > 0.5, term, 0.0)
        half = 0.5 * term
        forces[i, 0] = half * (
            m_ext[i + 3, 5 : 5 + FROWS, :] - m_ext[i + 1, 5 : 5 + FROWS, :]
        )
        forces[i, 1] = half * (
            m_ext[i + 2, 6 : 6 + FROWS, :] - m_ext[i + 2, 4 : 4 + FROWS, :]
        )
        forces[i, 2] = term * grad_y[i + 2, 5 : 5 + FROWS, :]

    @pl.loop(0, FPLANES // 2)
    def _(step):
        at = pl.ds(step * 2, 2)
        rows = forces[at].reshape(6 * FROWS, LANES).astype(BF16)
        both = jnp.dot(rows, band_s[...], preferred_element_type=F32)
        ysm[at] = (both[:, :LANES] + both[:, LANES:]).reshape(2, 3, FROWS, LANES)

    def bell_sum(load):
        total = taps[3] * load(3)
        for t in range(3):
            total = total + taps[t] * (load(t) + load(6 - t))
        return total

    @pl.loop(0, FPLANES)
    def _(i):
        for c in range(3):
            zsm[c, i] = bell_sum(lambda t: ysm[i, c, t : t + SIDE, :])

    def last_pass(x, top):
        square = jnp.zeros((SIDE, LANES), F32)
        for c in range(3):
            value = bell_sum(lambda t: zsm[c, x + t])
            out_ref[c, x] = value
            square = square + value * value
        return jnp.maximum(top, square)

    top = lax.fori_loop(0, SIDE, last_pass, jnp.zeros((SIDE, LANES), F32))
    top = jnp.max(top.reshape(4, 8, LANES), axis=0)

    def all_peak(top, n, slots, ssem, rsem, device):
        pk = pk_send.at[0 if slots is pk_blk else 1]
        pk[...] = top
        copies = []
        for d in range(1, n):
            copies.append(
                pltpu.make_async_remote_copy(
                    src_ref=pk,
                    dst_ref=slots.at[d],
                    send_sem=ssem.at[d],
                    recv_sem=rsem.at[d],
                    device_id=device(d),
                    device_id_type=MESH,
                )
            )
        for copy in copies:
            copy.start()
        for d, copy in enumerate(copies):
            copy.wait_recv()
            top = jnp.maximum(top, slots[d + 1])
        return top, copies

    top, blk_copies = all_peak(
        top, n_blk, pk_blk, pb_ssem, pb_rsem, lambda d: (me_s, (me_b + d) % n_blk)
    )
    top, slab_copies = all_peak(
        top, n_slab, pk_slab, ps_ssem, ps_rsem, lambda d: ((me_s + d) % n_slab, me_b)
    )
    peak = jnp.sqrt(jnp.max(top, axis=(0, 1), keepdims=True))
    scale_ref[...] = jnp.broadcast_to(step_length / (peak + peak_eps), (8, LANES))

    for e in range(1, chips):
        spread(e).wait_send()
    for e in range(chips):
        to_sibling(e).wait_send()
    finish_all(f_copies)
    finish_all(m_copies)
    for copy in blk_copies + slab_copies:
        copy.wait_send()


def per_device(
    n_slab,
    n_blk,
    fixed_image,
    moving_image,
    fetch_owner,
    fetch_block,
    fetch_count,
    interp_level,
    block_mask,
):
    chips = n_blk // 2
    vmem = pl.BlockSpec(memory_space=pltpu.VMEM)
    smem = pl.BlockSpec(memory_space=pltpu.SMEM)
    rim = lambda planes, rows, n: pltpu.VMEM((n, planes, rows, LANES), BF16)
    sems = lambda n: pltpu.SemaphoreType.DMA((n,))
    smoothed, scale = pl.pallas_call(
        functools.partial(kernel, n_slab, n_blk),
        out_shape=(
            jax.ShapeDtypeStruct((3, SIDE, SIDE, LANES), F32),
            jax.ShapeDtypeStruct((8, LANES), F32),
        ),
        in_specs=[vmem, vmem, smem, smem, smem, smem, smem],
        out_specs=(vmem, vmem),
        scratch_shapes=[
            pltpu.VMEM((n_blk, SIDE, SIDE, LANES), BF16),
            pltpu.VMEM((chips, 2 * LANES, 4 * LANES), BF16),
            pltpu.VMEM((SIDE * SIDE, 4 * LANES), F32),
            pltpu.VMEM((PLANES, ROWS, LANES), F32),
            pltpu.VMEM((PLANES, ROWS, LANES), F32),
            pltpu.VMEM((3, 7, ROWS, LANES), F32),
            pltpu.VMEM((3, PLANES, FROWS, LANES), F32),
            pltpu.VMEM((FPLANES, FROWS, LANES), F32),
            pltpu.VMEM((FPLANES, FROWS, LANES), F32),
            pltpu.VMEM((FPLANES, FROWS, LANES), F32),
            pltpu.VMEM((PLANES, ROWS, LANES), F32),
            pltpu.VMEM((FPLANES, 3, FROWS, LANES), F32),
            pltpu.VMEM((FPLANES, 3, FROWS, LANES), F32),
            pltpu.VMEM((3, FPLANES, SIDE, LANES), F32),
            pltpu.VMEM((3, FROWS, LANES), F32),
            pltpu.VMEM((LANES, 2 * LANES), BF16),
            pltpu.VMEM((2 * LANES, LANES), BF16),
            pltpu.VMEM((LANES, 2 * LANES), BF16),
            rim(HALO + 1, SIDE, 2),
            rim(HALO + 1, SIDE, 2),
            rim(HALO + 1, SIDE, 2),
            rim(HALO + 1, SIDE, 2),
            rim(HALO + 1, 16, 4),
            rim(HALO, SIDE, 2),
            rim(HALO, SIDE, 2),
            rim(HALO, SIDE, 2),
            rim(HALO, SIDE, 2),
            rim(HALO, 16, 4),
            pltpu.VMEM((2, 8, LANES), F32),
            pltpu.VMEM((n_blk, 8, LANES), F32),
            pltpu.VMEM((n_slab, 8, LANES), F32),
            sems(n_blk),
            sems(n_blk),
            sems(8),
            sems(8),
            sems(8),
            sems(8),
            sems(n_blk),
            sems(n_blk),
            sems(n_slab),
            sems(n_slab),
        ],
        compiler_params=pltpu.CompilerParams(
            collective_id=0, has_side_effects=True, vmem_limit_bytes=48 * 1024 * 1024
        ),
        name="syn_step",
    )(
        fixed_image,
        moving_image,
        fetch_owner,
        fetch_block,
        fetch_count,
        interp_level,
        block_mask,
    )
    return smoothed * scale[0, 0]


def solution(mesh):
    in_specs = (
        P("blk", "slab", None),
        P("blk", "slab", None),
        P("blk", "slab", None, None),
        P("blk", "slab", None, None),
        P("blk", "slab", None),
        P("blk", "slab", None, None, None),
        P("blk", "slab", None),
    )
    out_specs = P(None, "blk", "slab", None)
    return jax.shard_map(
        functools.partial(per_device, mesh.shape["slab"], mesh.shape["blk"]),
        mesh=mesh,
        in_specs=in_specs,
        out_specs=out_specs,
        check_vma=False,
    )
```

```python
import functools
import math

import jax
import jax.numpy as jnp
from jax import lax
from jax.experimental import pallas as pl
from jax.experimental.pallas import tpu as pltpu
from jax.sharding import PartitionSpec as P

LEVELS = 8
BOX_RADIUS = 2
SMOOTH_RADIUS = 3
HALO = BOX_RADIUS + SMOOTH_RADIUS

sigma_smooth = 1.5
step_length = 2.0
var_eps = 1e-05
peak_eps = 1e-06

SIDE = 32
LANES = 128
PLANES = SIDE + 2 * HALO
ROWS = 48
FIRST = 8
FPLANES = SIDE + 2 * SMOOTH_RADIUS
FROWS = 40
F32 = jnp.float32
BF16 = jnp.bfloat16
MESH = pl.DeviceIdType.MESH
DIRECTIONS = ((1, 0), (-1, 0), (0, 1), (0, -1), (1, 1), (1, -1), (-1, 1), (-1, -1))


def smooth_weights(radius):
    weights_raw = [
        math.exp(-(offset * offset) / (2.0 * sigma_smooth * sigma_smooth))
        for offset in range(-radius, radius + 1)
    ]
    weights_total = sum(weights_raw)
    return [weight_one / weights_total for weight_one in weights_raw]


def kernel(
    n_slab,
    n_blk,
    fixed_hbm,
    moving_hbm,
    owner_hbm,
    block_hbm,
    count_hbm,
    level_hbm,
    mask_hbm,
    out_ref,
    scale_ref,
    fixed_ref,
    owner_ref,
    block_ref,
    count_ref,
    level_ref,
    mask_ref,
    in_sem,
    gath,
    select,
    acc,
    f_ext,
    m_ext,
    ybox,
    zbox,
    f_mean,
    f_inv,
    f_dev,
    grad_y,
    forces,
    ysm,
    zsm,
    mask_pl,
    band_m,
    band_2,
    band_s,
    fx_send,
    fz_send,
    fx_recv,
    fz_recv,
    fc_recv,
    mx_send,
    mz_send,
    mx_recv,
    mz_recv,
    mc_recv,
    pk_send,
    pk_blk,
    pk_slab,
    ag_ssem,
    ag_rsem,
    f_ssem,
    f_rsem,
    m_ssem,
    m_rsem,
    pb_ssem,
    pb_rsem,
    ps_ssem,
    ps_rsem,
):
    me_s = lax.axis_index("slab")
    me_b = lax.axis_index("blk")
    chips = n_blk // 2
    chip = me_b // 2
    core = me_b % 2
    taps = smooth_weights(SMOOTH_RADIUS)

    def there(dx, dz):
        ok = None
        for d, me, n in ((dx, me_b, n_blk), (dz, me_s, n_slab)):
            if d == 0:
                continue
            now = me + d < n if d > 0 else me + d >= 0
            ok = now if ok is None else jnp.logical_and(ok, now)
        return ok

    loads = [
        pltpu.make_async_copy(src, dst, in_sem.at[i])
        for i, (src, dst) in enumerate(
            (
                (fixed_hbm, fixed_ref),
                (moving_hbm, gath.at[0]),
                (owner_hbm, owner_ref),
                (block_hbm, block_ref),
                (count_hbm, count_ref),
                (level_hbm, level_ref),
                (mask_hbm, mask_ref),
            )
        )
    ]
    for load in loads:
        load.start()

    barrier = pltpu.get_barrier_semaphore()
    for d in range(1, n_blk):
        pl.semaphore_signal(
            barrier, inc=1, device_id=(me_s, (me_b + d) % n_blk), device_id_type=MESH
        )
    for d in range(1, n_slab):
        pl.semaphore_signal(
            barrier, inc=1, device_id=((me_s + d) % n_slab, me_b), device_id_type=MESH
        )
    for dx, dz in DIRECTIONS[4:]:

        @pl.when(there(dx, dz))
        def _():
            pl.semaphore_signal(
                barrier, inc=1, device_id=(me_s + dz, me_b + dx), device_id_type=MESH
            )

    wide_x = jnp.where(me_b > 0, 1, 0) + jnp.where(me_b < n_blk - 1, 1, 0)
    wide_z = jnp.where(me_s > 0, 1, 0) + jnp.where(me_s < n_slab - 1, 1, 0)
    pl.semaphore_wait(barrier, n_blk - 1 + n_slab - 1 + wide_x * wide_z)

    if chips == 4:
        flip_x = chip + 1 - 2 * (chip % 2)
        flip_y = chip + 2 - 4 * (chip // 2)
        away = [chip, flip_x, flip_y, 3 - chip]
    else:
        away = [(chip + chips - e) % chips for e in range(chips)]
    half = SIDE // 2

    def remote(src, dst, at, device):
        return pltpu.make_async_remote_copy(
            src_ref=src,
            dst_ref=dst,
            send_sem=ag_ssem.at[at],
            recv_sem=ag_rsem.at[at],
            device_id=device,
            device_id_type=MESH,
        )

    def piece(e, h):
        rows = pl.ds(h * half, half)
        at = 4 * e + 2 * h
        if chips != 4:
            target = (chip + e) % chips
            src = moving_hbm.at[rows]
        elif e < 3:
            target = away[e]
            src = moving_hbm.at[rows]
        else:
            target = away[2 - h]
            src = gath.at[2 * (1 + h), rows]
        return remote(src, gath.at[2 * e, rows], at, (me_s, 2 * target + core))

    def passed(e, h):
        rows = pl.ds(h * half, half)
        src = moving_hbm.at[rows] if e == 0 else gath.at[2 * e, rows]
        return remote(
            src, gath.at[2 * e + 1, rows], 4 * e + 2 * h + 1, (me_s, 2 * chip + 1 - core)
        )

    if chips == 4:
        for e, h in ((1, 0), (2, 1), (1, 1), (2, 0)):
            piece(e, h).start()
    else:
        for e in range(1, chips):
            for h in range(2):
                piece(e, h).start()
    for h in range(2):
        passed(0, h).start()

    def take(e, h):
        piece(e, h).wait_recv()
        if chips == 4 and (e, h) in ((1, 0), (2, 1)):
            piece(3, h).start()
        passed(e, h).start()

    def rim_copies(x_send, z_send, x_recv, z_recv, c_recv, ssem, rsem):
        copies = []
        for i, (dx, dz) in enumerate(DIRECTIONS):
            if dz == 0:
                src, dst = x_send.at[(dx + 1) // 2], x_recv.at[(dx + 1) // 2]
            elif dx == 0:
                src, dst = z_send.at[(dz + 1) // 2], z_recv.at[(dz + 1) // 2]
            else:
                src = z_send.at[(dz + 1) // 2, :, pl.ds(16 if dx > 0 else 0, 16), :]
                dst = c_recv.at[i - 4]
            copies.append(
                pltpu.make_async_remote_copy(
                    src_ref=src,
                    dst_ref=dst,
                    send_sem=ssem.at[i],
                    recv_sem=rsem.at[i],
                    device_id=(me_s + dz, me_b + dx),
                    device_id_type=MESH,
                )
            )
        return copies

    def start_all(copies):
        for (dx, dz), copy in zip(DIRECTIONS, copies):
            pl.when(there(dx, dz))(copy.start)

    def finish_all(copies):
        for (dx, dz), copy in zip(DIRECTIONS, copies):
            pl.when(there(dx, dz))(copy.wait_send)

    def pack_rims(ext, x_send, z_send):
        flat = ext.reshape(PLANES * ROWS, LANES)
        for j in range(HALO):
            for side, at in ((0, j), (1, SIDE - HALO + j)):
                z_send[side, j] = flat[
                    pl.ds(HALO * ROWS + FIRST + at, SIDE, stride=ROWS), :
                ].astype(BF16)
                x_send[side, j] = ext[HALO + at, FIRST : FIRST + SIDE, :].astype(BF16)

    def fill_rims(copies, ext, x_recv, z_recv, c_recv, mask):
        flat = ext.reshape(PLANES * ROWS, LANES)
        for i, (dx, dz) in enumerate(DIRECTIONS):
            at_x = 0 if dx > 0 else HALO + SIDE
            at_z = FIRST - HALO if dz > 0 else FIRST + SIDE
            region = {1: 0, 0: 1, -1: 2}[dx]
            row_at = {1: 0, 0: SMOOTH_RADIUS, -1: SMOOTH_RADIUS + SIDE}[dz]
            row_n = SIDE if dz == 0 else SMOOTH_RADIUS

            @pl.when(there(-dx, -dz))
            def _():
                copies[i].wait_recv()
                side_x, side_z = (dx + 1) // 2, (dz + 1) // 2
                for j in range(HALO):
                    if dz == 0:
                        ext[at_x + j, FIRST : FIRST + SIDE, :] = x_recv[side_x, j].astype(F32)
                    elif dx == 0:
                        flat[pl.ds(HALO * ROWS + at_z + j, SIDE, stride=ROWS), :] = z_recv[
                            side_z, j
                        ].astype(F32)
                    else:
                        rows = c_recv[i - 4, j].astype(F32)
                        rows = rows[16 - HALO :] if dx > 0 else rows[:HALO]
                        flat[pl.ds(at_x * ROWS + at_z + j, HALO, stride=ROWS), :] = rows
                if mask:
                    if dz == 0:
                        plane = x_recv[side_x, HALO].astype(F32)
                    elif dx == 0:
                        plane = z_recv[side_z, HALO].astype(F32)
                    else:
                        plane = c_recv[i - 4, HALO].astype(F32)
                    mask_pl[region, row_at : row_at + row_n, :] = plane[:row_n]

    lane = lax.broadcasted_iota(jnp.int32, (1, LANES), 1)

    def by_block(scalars):
        vec = jnp.full((1, LANES), scalars[3], jnp.int32)
        for g in range(3):
            vec = jnp.where(lane // SIDE == g, scalars[g], vec)
        return vec

    nought = me_b // n_blk
    for ext in (f_ext, m_ext):

        @pl.loop(0, PLANES // 7)
        def _(x):
            ext[pl.ds(x * 7, 7)] = jnp.zeros((7, ROWS, LANES), F32)

    for load in loads:
        load.wait()

    mask_pl[...] = jnp.zeros_like(mask_pl)
    own_mask = by_block([mask_ref[0, 0, g] for g in range(4)]).astype(F32)
    mask_rows = jnp.broadcast_to(own_mask, (SIDE, LANES))
    mask_pl[1, SMOOTH_RADIUS : SMOOTH_RADIUS + SIDE, :] = mask_rows

    @pl.loop(0, SIDE // 4)
    def _(x):
        at = pl.ds(HALO + x * 4, 4)
        f_ext[at, FIRST : FIRST + SIDE, :] = fixed_ref[pl.ds(x * 4, 4)].astype(F32)

    pack_rims(f_ext, fx_send, fz_send)
    for side in range(2):
        fx_send[side, HALO] = mask_rows.astype(BF16)
        fz_send[side, HALO] = mask_rows.astype(BF16)
    f_copies = rim_copies(fx_send, fz_send, fx_recv, fz_recv, fc_recv, f_ssem, f_rsem)
    start_all(f_copies)

    place, frac_x, frac_y, frac_z, weight = [], [], [], [], []
    counts = by_block([count_ref[0, 0, g] for g in range(4)])
    for k in range(4):
        fracs = [
            by_block([level_ref[0, 0, a, g, k] for g in range(4)]).astype(F32) / LEVELS
            for a in range(3)
        ]
        frac_x.append(fracs[0])
        frac_z.append(fracs[1])
        frac_y.append(fracs[2])
        place.append(
            by_block([owner_ref[0, 0, g, k] for g in range(4)]) * LANES
            + by_block([block_ref[0, 0, g, k] for g in range(4)]) * SIDE
            + lane % SIDE
        )
        weight.append(jnp.where(counts > k, 1.0, 0.0) / counts.astype(F32))
    sub = lax.broadcasted_iota(jnp.int32, (LANES, LANES), 0)
    for e in range(chips):
        for p in range(2):
            base = (2 * away[e] + (core if p == 0 else 1 - core)) * LANES
            for k in range(4):
                first = place[k] - base
                second = first + jnp.where(lane % SIDE == SIDE - 1, 0, 1)
                f_y = frac_y[k]
                select[e, p * LANES : (p + 1) * LANES, k * LANES : (k + 1) * LANES] = (
                    jnp.where(sub == first, 1.0 - f_y, 0.0) + jnp.where(sub == second, f_y, 0.0)
                ).astype(BF16)

    off = sub - lax.broadcasted_iota(jnp.int32, (LANES, LANES), 1)
    band = jnp.where(jnp.abs(off) <= BOX_RADIUS, 1.0, 0.0).astype(BF16)
    band_m[:, :LANES] = band
    band_m[:, LANES:] = (
        jnp.where(off == 1, 0.5, 0.0) - jnp.where(off == -1, 0.5, 0.0)
    ).astype(BF16)
    band_2[:LANES] = band
    band_2[LANES:] = band
    bell = jnp.zeros((LANES, LANES), F32)
    for t in range(2 * SMOOTH_RADIUS + 1):
        bell = jnp.where(off == t - SMOOTH_RADIUS, taps[t], bell)
    bell_hi = bell.astype(BF16)
    band_s[:, :LANES] = bell_hi
    band_s[:, LANES:] = (bell - bell_hi.astype(F32)).astype(BF16)

    def halves(product):
        high = product.astype(BF16)
        return jnp.concatenate([high, (product - high.astype(F32)).astype(BF16)], axis=1)

    def shifted(ref, lead, start, rows):
        return ref[(*lead, pl.ds(nought + start, rows), slice(None))]

    def z_sum(ref, q, j):
        total = shifted(ref, (q, j), 3, FROWS)
        for t in range(1, 5):
            total = total + shifted(ref, (q, j), 3 + t, FROWS)
        return total

    def x_sums(q, i):
        v = [zbox[q, i + t] for t in range(6)]
        shared = (v[1] + v[2]) + (v[3] + v[4])
        return v[0] + shared, shared + v[5]

    per_box = 1.0 / float((2 * BOX_RADIUS + 1) ** 3)

    def resample(e):
        @pl.loop(0, 4)
        def _(part):
            at = pl.ds(part * 8, 8)
            pair = jnp.concatenate(
                [gath[2 * e, at].reshape(256, LANES), gath[2 * e + 1, at].reshape(256, LANES)],
                axis=1,
            )
            got = jnp.dot(pair, select[e], preferred_element_type=F32)
            rows = pl.ds(part * 256, 256)
            if e == 0:
                acc[rows, :] = got
            else:
                acc[rows, :] = acc[rows, :] + got

    if chips == 4:
        take(1, 0)
        take(2, 1)

    fill_rims(f_copies, f_ext, fx_recv, fz_recv, fc_recv, True)

    @pl.loop(0, PLANES // 7)
    def _(step):
        at = pl.ds(step * 7, 7)
        planes = f_ext[at].reshape(7 * ROWS, LANES)
        y_f = jnp.dot(planes.astype(BF16), band, preferred_element_type=F32)
        y_ff = jnp.dot(halves(planes * planes), band_2[...], preferred_element_type=F32)
        ybox[0, at] = y_f.reshape(7, ROWS, LANES)
        ybox[1, at] = y_ff.reshape(7, ROWS, LANES)

    if chips == 4:
        take(1, 1)
        take(2, 0)

    @pl.loop(0, PLANES // 2)
    def _(step):
        for j in range(2):
            for q in range(2):
                zbox[q, 2 * step + j] = z_sum(ybox, q, 2 * step + j)

    @pl.loop(0, FPLANES // 2)
    def _(step):
        i = 2 * step
        sums = x_sums(0, i), x_sums(1, i)
        for j in range(2):
            mean = sums[0][j] * per_box
            var = sums[1][j] * per_box - mean * mean + var_eps
            f_mean[i + j] = mean
            f_inv[i + j] = 1.0 / var
            f_dev[i + j] = shifted(f_ext, (i + j + 2,), 5, FROWS) - mean

    for h in range(2):
        passed(0, h).wait_recv()
    resample(0)
    if chips != 4:
        for e in range(1, chips):
            for h in range(2):
                take(e, h)
    for e in range(1, chips):
        for h in range(2):
            if chips == 4 and e == 2:
                take(3, h)
            passed(e, h).wait_recv()
        resample(e)

    last_row = lax.broadcasted_iota(jnp.int32, (SIDE, LANES), 0) == SIDE - 1

    @pl.loop(0, SIDE, unroll=2)
    def _(x):
        here = pl.ds(pl.multiple_of(x * SIDE, SIDE), SIDE)
        after = pl.ds(pl.multiple_of(jnp.minimum(x + 1, SIDE - 1) * SIDE, SIDE), SIDE)
        stay = jnp.zeros((SIDE, LANES), F32)
        move = jnp.zeros((SIDE, LANES), F32)
        for k in range(4):
            cols = slice(k * LANES, (k + 1) * LANES)
            mixed = (1.0 - frac_x[k]) * acc[here, cols] + frac_x[k] * acc[after, cols]
            stay = stay + (weight[k] * (1.0 - frac_z[k])) * mixed
            move = move + (weight[k] * frac_z[k]) * mixed
        moved = jnp.where(last_row, move, pltpu.roll(move, SIDE - 1, 0))
        m_ext[HALO + x, FIRST : FIRST + SIDE, :] = (stay + moved).astype(BF16).astype(F32)

    pack_rims(m_ext, mx_send, mz_send)
    m_copies = rim_copies(mx_send, mz_send, mx_recv, mz_recv, mc_recv, m_ssem, m_rsem)
    start_all(m_copies)

    def y_pass(planes, rows, shape):
        count = shape[0] * shape[1]
        m_now = m_ext[planes, rows].reshape(count, LANES)
        f_now = f_ext[planes, rows].reshape(count, LANES)
        y_m = jnp.dot(m_now.astype(BF16), band_m[...], preferred_element_type=F32)
        products = jnp.concatenate([halves(m_now * m_now), halves(f_now * m_now)], axis=0)
        y_p = jnp.dot(products, band_2[...], preferred_element_type=F32)
        ybox[0, planes, rows] = y_m[:, :LANES].reshape(*shape, LANES)
        grad_y[planes, rows] = y_m[:, LANES:].reshape(*shape, LANES)
        ybox[1, planes, rows] = y_p[:count].reshape(*shape, LANES)
        ybox[2, planes, rows] = y_p[count:].reshape(*shape, LANES)

    @pl.loop(0, 4)
    def _(part):
        y_pass(pl.ds(HALO + part * 8, 8), slice(FIRST, FIRST + SIDE), (8, SIDE))

    fill_rims(m_copies, m_ext, mx_recv, mz_recv, mc_recv, False)
    y_pass(slice(0, HALO), slice(None), (HALO, ROWS))
    y_pass(slice(HALO + SIDE, PLANES), slice(None), (HALO, ROWS))
    y_pass(slice(HALO, HALO + SIDE), slice(0, FIRST), (SIDE, FIRST))
    y_pass(slice(HALO, HALO + SIDE), slice(FIRST + SIDE, ROWS), (SIDE, ROWS - FIRST - SIDE))

    @pl.loop(0, PLANES // 2)
    def _(step):
        for j in range(2):
            for q in range(3):
                zbox[q, 2 * step + j] = z_sum(ybox, q, 2 * step + j)

    def bell_sum(values):
        total = taps[3] * values[3]
        for t in range(3):
            total = total + taps[t] * (values[t] + values[6 - t])
        return total

    pairs = FPLANES // 2

    @pl.loop(0, pairs + 2)
    def _(step):
        old = jnp.maximum(step - 2, 0)
        for j in range(2):
            for c in range(3):
                zsm[c, 2 * old + j] = bell_sum(
                    [shifted(ysm, (old, 3 * j + c), t, SIDE) for t in range(7)]
                )
        mid = jnp.minimum(jnp.maximum(step - 1, 0), pairs - 1)
        both = jnp.dot(forces[mid].astype(BF16), band_s[...], preferred_element_type=F32)
        ysm[mid] = (both[:, :LANES] + both[:, LANES:]).reshape(6, FROWS, LANES)
        now = jnp.minimum(step, pairs - 1)
        i = 2 * now
        sums = [x_sums(q, i) for q in range(3)]
        for j in range(2):
            at = i + j
            mean = sums[0][j] * per_box
            var = sums[1][j] * per_box - mean * mean + var_eps
            cov = sums[2][j] * per_box - f_mean[at] * mean
            slope = cov / var
            center = shifted(m_ext, (at + 2,), 5, FROWS)
            term = slope * f_inv[at] * (f_dev[at] - slope * (center - mean))
            region = jnp.where(at >= SMOOTH_RADIUS, 1, 0) + jnp.where(
                at >= SMOOTH_RADIUS + SIDE, 1, 0
            )
            term = jnp.where(mask_pl[region] > 0.5, term, 0.0)
            base = 3 * j * FROWS
            forces[now, base : base + FROWS] = term * (
                shifted(m_ext, (at + 3,), 5, FROWS) - shifted(m_ext, (at + 1,), 5, FROWS)
            )
            forces[now, base + FROWS : base + 2 * FROWS] = term * (
                shifted(m_ext, (at + 2,), 6, FROWS) - shifted(m_ext, (at + 2,), 4, FROWS)
            )
            forces[now, base + 2 * FROWS : base + 3 * FROWS] = (
                2.0 * term * shifted(grad_y, (at + 2,), 5, FROWS)
            )

    def last_pass(step, top):
        x = 2 * step
        squares = [jnp.zeros((SIDE, LANES), F32) for _ in range(2)]
        for c in range(3):
            values = [zsm[c, x + t] for t in range(8)]
            for j in range(2):
                value = bell_sum(values[j : j + 7])
                out_ref[c, x + j] = value
                squares[j] = squares[j] + value * value
        return jnp.maximum(top, jnp.maximum(squares[0], squares[1]))

    top = lax.fori_loop(0, SIDE // 2, last_pass, jnp.zeros((SIDE, LANES), F32))
    top = jnp.max(top.reshape(4, 8, LANES), axis=0)

    def all_peak(top, n, slots, ssem, rsem, device):
        pk = pk_send.at[0 if slots is pk_blk else 1]
        pk[...] = top
        copies = []
        for d in range(1, n):
            copies.append(
                pltpu.make_async_remote_copy(
                    src_ref=pk,
                    dst_ref=slots.at[d],
                    send_sem=ssem.at[d],
                    recv_sem=rsem.at[d],
                    device_id=device(d),
                    device_id_type=MESH,
                )
            )
        for copy in copies:
            copy.start()
        for d, copy in enumerate(copies):
            copy.wait_recv()
            top = jnp.maximum(top, slots[d + 1])
        return top, copies

    top, blk_copies = all_peak(
        top, n_blk, pk_blk, pb_ssem, pb_rsem, lambda d: (me_s, (me_b + d) % n_blk)
    )
    top, slab_copies = all_peak(
        top, n_slab, pk_slab, ps_ssem, ps_rsem, lambda d: ((me_s + d) % n_slab, me_b)
    )
    peak = jnp.sqrt(jnp.max(top, axis=(0, 1), keepdims=True))
    scale_ref[...] = jnp.broadcast_to(step_length / (peak + peak_eps), (1, LANES))

    for e in range(chips):
        for h in range(2):
            if e > 0:
                piece(e, h).wait_send()
            passed(e, h).wait_send()
    finish_all(f_copies)
    finish_all(m_copies)
    for copy in blk_copies + slab_copies:
        copy.wait_send()


def per_device(
    n_slab,
    n_blk,
    fixed_image,
    moving_image,
    fetch_owner,
    fetch_block,
    fetch_count,
    interp_level,
    block_mask,
):
    chips = n_blk // 2
    interp_level = jnp.swapaxes(interp_level, 2, 3)
    vmem = pl.BlockSpec(memory_space=pltpu.VMEM)
    small = [fetch_owner, fetch_block, fetch_count, interp_level, block_mask]
    rim = lambda planes, rows, n: pltpu.VMEM((n, planes, rows, LANES), BF16)
    sems = lambda n: pltpu.SemaphoreType.DMA((n,))
    smoothed, scale = pl.pallas_call(
        functools.partial(kernel, n_slab, n_blk),
        out_shape=(
            jax.ShapeDtypeStruct((3, SIDE, SIDE, LANES), F32),
            jax.ShapeDtypeStruct((1, LANES), F32),
        ),
        in_specs=[pl.BlockSpec(memory_space=pl.ANY)] * 7,
        out_specs=(vmem, vmem),
        scratch_shapes=[
            pltpu.VMEM((SIDE, SIDE, LANES), BF16),
            *[pltpu.SMEM(one.shape, jnp.int32) for one in small],
            sems(7),
            pltpu.VMEM((n_blk, SIDE, SIDE, LANES), BF16),
            pltpu.VMEM((chips, 2 * LANES, 4 * LANES), BF16),
            pltpu.VMEM((SIDE * SIDE, 4 * LANES), F32),
            pltpu.VMEM((PLANES, ROWS, LANES), F32),
            pltpu.VMEM((PLANES, ROWS, LANES), F32),
            pltpu.VMEM((3, PLANES, ROWS, LANES), F32),
            pltpu.VMEM((3, PLANES, FROWS, LANES), F32),
            pltpu.VMEM((FPLANES, FROWS, LANES), F32),
            pltpu.VMEM((FPLANES, FROWS, LANES), F32),
            pltpu.VMEM((FPLANES, FROWS, LANES), F32),
            pltpu.VMEM((PLANES, ROWS, LANES), F32),
            pltpu.VMEM((FPLANES // 2, 6 * FROWS, LANES), F32),
            pltpu.VMEM((FPLANES // 2, 6, FROWS, LANES), F32),
            pltpu.VMEM((3, FPLANES, SIDE, LANES), F32),
            pltpu.VMEM((3, FROWS, LANES), F32),
            pltpu.VMEM((LANES, 2 * LANES), BF16),
            pltpu.VMEM((2 * LANES, LANES), BF16),
            pltpu.VMEM((LANES, 2 * LANES), BF16),
            rim(HALO + 1, SIDE, 2),
            rim(HALO + 1, SIDE, 2),
            rim(HALO + 1, SIDE, 2),
            rim(HALO + 1, SIDE, 2),
            rim(HALO + 1, 16, 4),
            rim(HALO, SIDE, 2),
            rim(HALO, SIDE, 2),
            rim(HALO, SIDE, 2),
            rim(HALO, SIDE, 2),
            rim(HALO, 16, 4),
            pltpu.VMEM((2, 8, LANES), F32),
            pltpu.VMEM((n_blk, 8, LANES), F32),
            pltpu.VMEM((n_slab, 8, LANES), F32),
            sems(2 * n_blk),
            sems(2 * n_blk),
            sems(8),
            sems(8),
            sems(8),
            sems(8),
            sems(n_blk),
            sems(n_blk),
            sems(n_slab),
            sems(n_slab),
        ],
        compiler_params=pltpu.CompilerParams(
            collective_id=0, has_side_effects=True, vmem_limit_bytes=48 * 1024 * 1024
        ),
        name="syn_step",
    )(
        fixed_image,
        moving_image,
        fetch_owner,
        fetch_block,
        fetch_count,
        interp_level,
        block_mask,
    )
    return smoothed * scale.reshape(1, 1, 1, LANES)


def solution(mesh):
    in_specs = (
        P("blk", "slab", None),
        P("blk", "slab", None),
        P("blk", "slab", None, None),
        P("blk", "slab", None, None),
        P("blk", "slab", None),
        P("blk", "slab", None, None, None),
        P("blk", "slab", None),
    )
    out_specs = P(None, "blk", "slab", None)
    return jax.shard_map(
        functools.partial(per_device, mesh.shape["slab"], mesh.shape["blk"]),
        mesh=mesh,
        in_specs=in_specs,
        out_specs=out_specs,
        check_vma=False,
    )
```

```python
import functools
import math

import jax
import jax.numpy as jnp
from jax import lax
from jax.experimental import pallas as pl
from jax.experimental.pallas import tpu as pltpu
from jax.sharding import PartitionSpec as P

LEVELS = 8
BOX_RADIUS = 2
SMOOTH_RADIUS = 3
HALO = BOX_RADIUS + SMOOTH_RADIUS

sigma_smooth = 1.5
step_length = 2.0
var_eps = 1e-05
peak_eps = 1e-06

SIDE = 32
LANES = 128
PLANES = SIDE + 2 * HALO
ROWS = 48
FIRST = 8
FPLANES = SIDE + 2 * SMOOTH_RADIUS
FROWS = 40
F32 = jnp.float32
BF16 = jnp.bfloat16
MESH = pl.DeviceIdType.MESH
DIRECTIONS = ((1, 0), (-1, 0), (0, 1), (0, -1), (1, 1), (1, -1), (-1, 1), (-1, -1))


def smooth_weights(radius):
    weights_raw = [
        math.exp(-(offset * offset) / (2.0 * sigma_smooth * sigma_smooth))
        for offset in range(-radius, radius + 1)
    ]
    weights_total = sum(weights_raw)
    return [weight_one / weights_total for weight_one in weights_raw]


def kernel(
    n_slab,
    n_blk,
    fixed_hbm,
    moving_hbm,
    owner_hbm,
    block_hbm,
    count_hbm,
    level_hbm,
    mask_hbm,
    out_hbm,
    scale_ref,
    out_ref,
    out_sem,
    fixed_ref,
    owner_ref,
    block_ref,
    count_ref,
    level_ref,
    mask_ref,
    in_sem,
    gath,
    select,
    acc,
    f_ext,
    m_ext,
    ybox,
    zbox,
    f_mean,
    f_inv,
    f_dev,
    grad_y,
    forces,
    ysm,
    zsm,
    mask_pl,
    band_m,
    band_2,
    band_s,
    fx_send,
    fz_send,
    fx_recv,
    fz_recv,
    fc_recv,
    mx_send,
    mz_send,
    mx_recv,
    mz_recv,
    mc_recv,
    pk_send,
    pk_blk,
    pk_slab,
    ag_ssem,
    ag_rsem,
    f_ssem,
    f_rsem,
    m_ssem,
    m_rsem,
    pb_ssem,
    pb_rsem,
    ps_ssem,
    ps_rsem,
):
    me_s = lax.axis_index("slab")
    me_b = lax.axis_index("blk")
    chips = n_blk // 2
    chip = me_b // 2
    core = me_b % 2
    taps = smooth_weights(SMOOTH_RADIUS)

    def there(dx, dz):
        ok = None
        for d, me, n in ((dx, me_b, n_blk), (dz, me_s, n_slab)):
            if d == 0:
                continue
            now = me + d < n if d > 0 else me + d >= 0
            ok = now if ok is None else jnp.logical_and(ok, now)
        return ok

    loads = [
        pltpu.make_async_copy(src, dst, in_sem.at[i])
        for i, (src, dst) in enumerate(
            (
                (fixed_hbm, fixed_ref),
                (moving_hbm, gath.at[0]),
                (owner_hbm, owner_ref),
                (block_hbm, block_ref),
                (count_hbm, count_ref),
                (level_hbm, level_ref),
                (mask_hbm, mask_ref),
            )
        )
    ]
    for load in loads:
        load.start()

    barrier = pltpu.get_barrier_semaphore()
    for d in range(1, n_blk):
        pl.semaphore_signal(
            barrier, inc=1, device_id=(me_s, (me_b + d) % n_blk), device_id_type=MESH
        )
    for d in range(1, n_slab):
        pl.semaphore_signal(
            barrier, inc=1, device_id=((me_s + d) % n_slab, me_b), device_id_type=MESH
        )
    for dx, dz in DIRECTIONS[4:]:

        @pl.when(there(dx, dz))
        def _():
            pl.semaphore_signal(
                barrier, inc=1, device_id=(me_s + dz, me_b + dx), device_id_type=MESH
            )

    def rim_copies(x_send, z_send, x_recv, z_recv, c_recv, ssem, rsem):
        copies = []
        for i, (dx, dz) in enumerate(DIRECTIONS):
            if dz == 0:
                src, dst = x_send.at[(dx + 1) // 2], x_recv.at[(dx + 1) // 2]
            elif dx == 0:
                src, dst = z_send.at[(dz + 1) // 2], z_recv.at[(dz + 1) // 2]
            else:
                src = z_send.at[(dz + 1) // 2, :, pl.ds(16 if dx > 0 else 0, 16), :]
                dst = c_recv.at[i - 4]
            copies.append(
                pltpu.make_async_remote_copy(
                    src_ref=src,
                    dst_ref=dst,
                    send_sem=ssem.at[i],
                    recv_sem=rsem.at[i],
                    device_id=(me_s + dz, me_b + dx),
                    device_id_type=MESH,
                )
            )
        return copies

    def start_all(copies):
        for (dx, dz), copy in zip(DIRECTIONS, copies):
            pl.when(there(dx, dz))(copy.start)

    def finish_all(copies):
        for (dx, dz), copy in zip(DIRECTIONS, copies):
            pl.when(there(dx, dz))(copy.wait_send)

    def pack_rims(ext, x_send, z_send):
        flat = ext.reshape(PLANES * ROWS, LANES)
        for j in range(HALO):
            for side, at in ((0, j), (1, SIDE - HALO + j)):
                z_send[side, j] = flat[
                    pl.ds(HALO * ROWS + FIRST + at, SIDE, stride=ROWS), :
                ].astype(BF16)
                x_send[side, j] = ext[HALO + at, FIRST : FIRST + SIDE, :].astype(BF16)

    def fill_rims(copies, ext, x_recv, z_recv, c_recv, mask):
        flat = ext.reshape(PLANES * ROWS, LANES)
        for i, (dx, dz) in enumerate(DIRECTIONS):
            at_x = 0 if dx > 0 else HALO + SIDE
            at_z = FIRST - HALO if dz > 0 else FIRST + SIDE
            region = {1: 0, 0: 1, -1: 2}[dx]
            row_at = {1: 0, 0: SMOOTH_RADIUS, -1: SMOOTH_RADIUS + SIDE}[dz]
            row_n = SIDE if dz == 0 else SMOOTH_RADIUS

            @pl.when(there(-dx, -dz))
            def _():
                copies[i].wait_recv()
                side_x, side_z = (dx + 1) // 2, (dz + 1) // 2
                for j in range(HALO):
                    if dz == 0:
                        ext[at_x + j, FIRST : FIRST + SIDE, :] = x_recv[side_x, j].astype(F32)
                    elif dx == 0:
                        flat[pl.ds(HALO * ROWS + at_z + j, SIDE, stride=ROWS), :] = z_recv[
                            side_z, j
                        ].astype(F32)
                    else:
                        rows = c_recv[i - 4, j].astype(F32)
                        rows = rows[16 - HALO :] if dx > 0 else rows[:HALO]
                        flat[pl.ds(at_x * ROWS + at_z + j, HALO, stride=ROWS), :] = rows
                if mask:
                    if dz == 0:
                        plane = x_recv[side_x, HALO].astype(F32)
                    elif dx == 0:
                        plane = z_recv[side_z, HALO].astype(F32)
                    else:
                        plane = c_recv[i - 4, HALO].astype(F32)
                    mask_pl[region, row_at : row_at + row_n, :] = plane[:row_n]

    lane = lax.broadcasted_iota(jnp.int32, (1, LANES), 1)

    def by_block(scalars):
        vec = jnp.full((1, LANES), scalars[3], jnp.int32)
        for g in range(3):
            vec = jnp.where(lane // SIDE == g, scalars[g], vec)
        return vec

    nought = me_b // n_blk
    for ext in (f_ext, m_ext):

        @pl.loop(0, PLANES // 7)
        def _(x):
            ext[pl.ds(x * 7, 7)] = jnp.zeros((7, ROWS, LANES), F32)

    loads[0].wait()
    loads[6].wait()

    mask_pl[...] = jnp.zeros_like(mask_pl)
    own_mask = by_block([mask_ref[0, 0, g] for g in range(4)]).astype(F32)
    mask_rows = jnp.broadcast_to(own_mask, (SIDE, LANES))
    mask_pl[1, SMOOTH_RADIUS : SMOOTH_RADIUS + SIDE, :] = mask_rows

    @pl.loop(0, SIDE // 4)
    def _(x):
        at = pl.ds(HALO + x * 4, 4)
        f_ext[at, FIRST : FIRST + SIDE, :] = fixed_ref[pl.ds(x * 4, 4)].astype(F32)

    pack_rims(f_ext, fx_send, fz_send)
    for side in range(2):
        fx_send[side, HALO] = mask_rows.astype(BF16)
        fz_send[side, HALO] = mask_rows.astype(BF16)
    wide_x = jnp.where(me_b > 0, 1, 0) + jnp.where(me_b < n_blk - 1, 1, 0)
    wide_z = jnp.where(me_s > 0, 1, 0) + jnp.where(me_s < n_slab - 1, 1, 0)
    pl.semaphore_wait(barrier, n_blk - 1 + n_slab - 1 + wide_x * wide_z)

    f_copies = rim_copies(fx_send, fz_send, fx_recv, fz_recv, fc_recv, f_ssem, f_rsem)
    start_all(f_copies)

    if chips == 4:
        flip_x = chip + 1 - 2 * (chip % 2)
        flip_y = chip + 2 - 4 * (chip // 2)
        away = [chip, flip_x, flip_y, 3 - chip]
    else:
        away = [(chip + chips - e) % chips for e in range(chips)]
    half = SIDE // 2

    def remote(src, dst, at, device):
        return pltpu.make_async_remote_copy(
            src_ref=src,
            dst_ref=dst,
            send_sem=ag_ssem.at[at],
            recv_sem=ag_rsem.at[at],
            device_id=device,
            device_id_type=MESH,
        )

    def piece(e, h):
        rows = pl.ds(h * half, half)
        at = 4 * e + 2 * h
        if chips != 4:
            target = (chip + e) % chips
            src = moving_hbm.at[rows]
        elif e < 3:
            target = away[e]
            src = moving_hbm.at[rows]
        else:
            target = away[2 - h]
            src = gath.at[2 * (1 + h), rows]
        return remote(src, gath.at[2 * e, rows], at, (me_s, 2 * target + core))

    def passed(e, h):
        rows = pl.ds(h * half, half)
        src = moving_hbm.at[rows] if e == 0 else gath.at[2 * e, rows]
        return remote(
            src, gath.at[2 * e + 1, rows], 4 * e + 2 * h + 1, (me_s, 2 * chip + 1 - core)
        )

    if chips == 4:
        for e, h in ((1, 0), (2, 1), (1, 1), (2, 0)):
            piece(e, h).start()
    else:
        for e in range(1, chips):
            for h in range(2):
                piece(e, h).start()
    for h in range(2):
        passed(0, h).start()

    def take(e, h):
        piece(e, h).wait_recv()
        if chips == 4 and (e, h) in ((1, 0), (2, 1)):
            piece(3, h).start()
        passed(e, h).start()

    for load in loads[2:6]:
        load.wait()
    places, mixes = [], []
    counts = by_block([count_ref[0, 0, g] for g in range(4)])
    at_end = lane % SIDE == SIDE - 1
    for k in range(4):
        f_x, f_z, f_y = [
            by_block([level_ref[0, 0, a, g, k] for g in range(4)]).astype(F32) / LEVELS
            for a in range(3)
        ]
        places.append(
            by_block([owner_ref[0, 0, g, k] for g in range(4)]) * LANES
            + by_block([block_ref[0, 0, g, k] for g in range(4)]) * SIDE
            + lane % SIDE
        )
        listed = jnp.where(counts > k, 1.0, 0.0)
        mixes.append(
            (
                jnp.where(at_end, 1.0, 1.0 - f_y),
                jnp.where(at_end, 0.0, f_y),
                [
                    listed * (f_x if mx else 1.0 - f_x) * (f_z if mz else 1.0 - f_z)
                    for mx, mz in ((0, 0), (1, 0), (0, 1), (1, 1))
                ],
            )
        )
    share = 1.0 / counts.astype(F32)
    sub = lax.broadcasted_iota(jnp.int32, (LANES, LANES), 0)

    @pl.loop(0, LANES // SIDE)
    def _(part):
        row = lax.broadcasted_iota(jnp.int32, (SIDE, LANES), 0) + part * SIDE
        for e in range(chips):
            for p in range(2):
                base = (2 * away[e] + (core if p == 0 else 1 - core)) * LANES
                totals = [None] * 4
                for k in range(4):
                    first = places[k] - base
                    y_stay, y_move, mix = mixes[k]
                    taken = jnp.where(
                        row == first, y_stay, jnp.where(row == first + 1, y_move, 0.0)
                    )
                    for c in range(4):
                        term = taken * mix[c]
                        totals[c] = term if k == 0 else totals[c] + term
                for c in range(4):
                    cols = slice(c * LANES, (c + 1) * LANES)
                    high = totals[c].astype(BF16)
                    low = (totals[c] - high.astype(F32)).astype(BF16)
                    at = pl.multiple_of(p * LANES + part * SIDE, SIDE)
                    select[e, pl.ds(at, SIDE), cols] = high
                    select[e, pl.ds(at + 2 * LANES, SIDE), cols] = low

    off = sub - lax.broadcasted_iota(jnp.int32, (LANES, LANES), 1)
    band = jnp.where(jnp.abs(off) <= BOX_RADIUS, 1.0, 0.0).astype(BF16)
    band_m[:, :LANES] = band
    band_m[:, LANES:] = (
        jnp.where(off == 1, 0.5, 0.0) - jnp.where(off == -1, 0.5, 0.0)
    ).astype(BF16)
    band_2[:LANES] = band
    band_2[LANES:] = band
    bell = jnp.zeros((LANES, LANES), F32)
    for t in range(2 * SMOOTH_RADIUS + 1):
        bell = jnp.where(off == t - SMOOTH_RADIUS, taps[t], bell)
    bell_hi = bell.astype(BF16)
    band_s[:, :LANES] = bell_hi
    band_s[:, LANES:] = (bell - bell_hi.astype(F32)).astype(BF16)

    def halves(product):
        high = product.astype(BF16)
        return jnp.concatenate([high, (product - high.astype(F32)).astype(BF16)], axis=1)

    def shifted(ref, lead, start, rows):
        return ref[(*lead, pl.ds(nought + start, rows), slice(None))]

    def z_sum(ref, q, j):
        total = shifted(ref, (q, j), 3, FROWS)
        for t in range(1, 5):
            total = total + shifted(ref, (q, j), 3 + t, FROWS)
        return total

    def x_sums(q, i):
        v = [zbox[q, i + t] for t in range(6)]
        shared = (v[1] + v[2]) + (v[3] + v[4])
        return v[0] + shared, shared + v[5]

    def inverse(value):
        guess = pltpu.reciprocal(value, approx=True)
        return guess * (2.0 - value * guess)

    per_box = 1.0 / float((2 * BOX_RADIUS + 1) ** 3)

    def resample(e):
        @pl.loop(0, 4)
        def _(part):
            at = pl.ds(part * 8, 8)
            pair = jnp.concatenate(
                [gath[2 * e, at].reshape(256, LANES), gath[2 * e + 1, at].reshape(256, LANES)],
                axis=1,
            )
            pair = jnp.concatenate([pair, pair], axis=1)
            got = jnp.dot(pair, select[e], preferred_element_type=F32)
            rows = pl.ds(part * 256, 256)
            if e == 0:
                acc[rows, :] = got
            else:
                acc[rows, :] = acc[rows, :] + got

    if chips == 4:
        take(1, 0)
        take(2, 1)

    fill_rims(f_copies, f_ext, fx_recv, fz_recv, fc_recv, True)

    @pl.loop(0, PLANES // 7)
    def _(step):
        at = pl.ds(step * 7, 7)
        planes = f_ext[at].reshape(7 * ROWS, LANES)
        y_f = jnp.dot(planes.astype(BF16), band, preferred_element_type=F32)
        y_ff = jnp.dot(halves(planes * planes), band_2[...], preferred_element_type=F32)
        ybox[0, at] = y_f.reshape(7, ROWS, LANES)
        ybox[1, at] = y_ff.reshape(7, ROWS, LANES)

    if chips == 4:
        take(1, 1)
        take(2, 0)

    @pl.loop(0, PLANES // 2)
    def _(step):
        for j in range(2):
            for q in range(2):
                zbox[q, 2 * step + j] = z_sum(ybox, q, 2 * step + j)

    loads[1].wait()
    for h in range(2):
        passed(0, h).wait_recv()
    resample(0)

    @pl.loop(0, FPLANES // 2)
    def _(step):
        i = 2 * step
        sums = x_sums(0, i), x_sums(1, i)
        for j in range(2):
            mean = sums[0][j] * per_box
            var = sums[1][j] * per_box - mean * mean + var_eps
            f_mean[i + j] = mean
            f_inv[i + j] = inverse(var)
            f_dev[i + j] = shifted(f_ext, (i + j + 2,), 5, FROWS) - mean

    if chips != 4:
        for e in range(1, chips):
            for h in range(2):
                take(e, h)
    for e in range(1, chips):
        for h in range(2):
            if chips == 4 and e == 2:
                take(3, h)
            passed(e, h).wait_recv()
        resample(e)

    last_row = lax.broadcasted_iota(jnp.int32, (SIDE, LANES), 0) == SIDE - 1

    @pl.loop(0, SIDE, unroll=4)
    def _(x):
        here = pl.ds(pl.multiple_of(x * SIDE, SIDE), SIDE)
        after = pl.ds(pl.multiple_of(jnp.minimum(x + 1, SIDE - 1) * SIDE, SIDE), SIDE)
        stay = acc[here, :LANES] + acc[after, LANES : 2 * LANES]
        move = acc[here, 2 * LANES : 3 * LANES] + acc[after, 3 * LANES :]
        moved = jnp.where(last_row, move, pltpu.roll(move, SIDE - 1, 0))
        warped = ((stay + moved) * share).astype(BF16).astype(F32)
        m_ext[HALO + x, FIRST : FIRST + SIDE, :] = warped

    pack_rims(m_ext, mx_send, mz_send)
    m_copies = rim_copies(mx_send, mz_send, mx_recv, mz_recv, mc_recv, m_ssem, m_rsem)
    start_all(m_copies)

    def y_pass(planes, rows, shape):
        count = shape[0] * shape[1]
        m_now = m_ext[planes, rows].reshape(count, LANES)
        f_now = f_ext[planes, rows].reshape(count, LANES)
        y_m = jnp.dot(m_now.astype(BF16), band_m[...], preferred_element_type=F32)
        products = jnp.concatenate([halves(m_now * m_now), halves(f_now * m_now)], axis=0)
        y_p = jnp.dot(products, band_2[...], preferred_element_type=F32)
        ybox[0, planes, rows] = y_m[:, :LANES].reshape(*shape, LANES)
        grad_y[planes, rows] = y_m[:, LANES:].reshape(*shape, LANES)
        ybox[1, planes, rows] = y_p[:count].reshape(*shape, LANES)
        ybox[2, planes, rows] = y_p[count:].reshape(*shape, LANES)

    @pl.loop(0, 4)
    def _(part):
        y_pass(pl.ds(HALO + part * 8, 8), slice(FIRST, FIRST + SIDE), (8, SIDE))

    fill_rims(m_copies, m_ext, mx_recv, mz_recv, mc_recv, False)
    y_pass(slice(0, HALO), slice(None), (HALO, ROWS))
    y_pass(slice(HALO + SIDE, PLANES), slice(None), (HALO, ROWS))
    y_pass(slice(HALO, HALO + SIDE), slice(0, FIRST), (SIDE, FIRST))
    y_pass(slice(HALO, HALO + SIDE), slice(FIRST + SIDE, ROWS), (SIDE, ROWS - FIRST - SIDE))

    @pl.loop(0, PLANES // 2)
    def _(step):
        for j in range(2):
            for q in range(3):
                zbox[q, 2 * step + j] = z_sum(ybox, q, 2 * step + j)

    def bell_sum(values):
        total = taps[3] * values[3]
        for t in range(3):
            total = total + taps[t] * (values[t] + values[6 - t])
        return total

    pairs = FPLANES // 2

    @pl.loop(0, pairs + 2)
    def _(step):
        old = jnp.maximum(step - 2, 0)
        for j in range(2):
            for c in range(3):
                zsm[c, 2 * old + j] = bell_sum(
                    [shifted(ysm, (old, 3 * j + c), t, SIDE) for t in range(7)]
                )
        mid = jnp.minimum(jnp.maximum(step - 1, 0), pairs - 1)
        both = jnp.dot(forces[mid].astype(BF16), band_s[...], preferred_element_type=F32)
        ysm[mid] = (both[:, :LANES] + both[:, LANES:]).reshape(6, FROWS, LANES)
        now = jnp.minimum(step, pairs - 1)
        i = 2 * now
        sums = [x_sums(q, i) for q in range(3)]
        for j in range(2):
            at = i + j
            mean = sums[0][j] * per_box
            var = sums[1][j] * per_box - mean * mean + var_eps
            cov = sums[2][j] * per_box - f_mean[at] * mean
            slope = cov * inverse(var)
            center = shifted(m_ext, (at + 2,), 5, FROWS)
            term = slope * f_inv[at] * (f_dev[at] - slope * (center - mean))
            region = jnp.where(at >= SMOOTH_RADIUS, 1, 0) + jnp.where(
                at >= SMOOTH_RADIUS + SIDE, 1, 0
            )
            term = jnp.where(mask_pl[region] > 0.5, term, 0.0)
            base = 3 * j * FROWS
            forces[now, base : base + FROWS] = term * (
                shifted(m_ext, (at + 3,), 5, FROWS) - shifted(m_ext, (at + 1,), 5, FROWS)
            )
            forces[now, base + FROWS : base + 2 * FROWS] = term * (
                shifted(m_ext, (at + 2,), 6, FROWS) - shifted(m_ext, (at + 2,), 4, FROWS)
            )
            forces[now, base + 2 * FROWS : base + 3 * FROWS] = (
                2.0 * term * shifted(grad_y, (at + 2,), 5, FROWS)
            )

    def last_pass(step, top):
        x = 2 * step
        squares = [jnp.zeros((SIDE, LANES), F32) for _ in range(2)]
        for c in range(3):
            values = [zsm[c, x + t] for t in range(8)]
            for j in range(2):
                value = bell_sum(values[j : j + 7])
                out_ref[c, x + j] = value
                squares[j] = squares[j] + value * value
        return jnp.maximum(top, jnp.maximum(squares[0], squares[1]))

    top = lax.fori_loop(0, SIDE // 2, last_pass, jnp.zeros((SIDE, LANES), F32))
    top = jnp.max(top.reshape(4, 8, LANES), axis=0)
    write = pltpu.make_async_copy(out_ref, out_hbm, out_sem)
    write.start()

    def all_peak(top, n, slots, ssem, rsem, device):
        pk = pk_send.at[0 if slots is pk_blk else 1]
        pk[...] = top
        copies = []
        for d in range(1, n):
            copies.append(
                pltpu.make_async_remote_copy(
                    src_ref=pk,
                    dst_ref=slots.at[d],
                    send_sem=ssem.at[d],
                    recv_sem=rsem.at[d],
                    device_id=device(d),
                    device_id_type=MESH,
                )
            )
        for copy in copies:
            copy.start()
        for d, copy in enumerate(copies):
            copy.wait_recv()
            top = jnp.maximum(top, slots[d + 1])
        return top, copies

    top, blk_copies = all_peak(
        top, n_blk, pk_blk, pb_ssem, pb_rsem, lambda d: (me_s, (me_b + d) % n_blk)
    )
    top, slab_copies = all_peak(
        top, n_slab, pk_slab, ps_ssem, ps_rsem, lambda d: ((me_s + d) % n_slab, me_b)
    )
    peak = jnp.sqrt(jnp.max(top, axis=(0, 1), keepdims=True))
    scale_ref[...] = jnp.broadcast_to(step_length / (peak + peak_eps), (1, LANES))

    for e in range(chips):
        for h in range(2):
            if e > 0:
                piece(e, h).wait_send()
            passed(e, h).wait_send()
    write.wait()
    finish_all(f_copies)
    finish_all(m_copies)
    for copy in blk_copies + slab_copies:
        copy.wait_send()


def per_device(
    n_slab,
    n_blk,
    fixed_image,
    moving_image,
    fetch_owner,
    fetch_block,
    fetch_count,
    interp_level,
    block_mask,
):
    chips = n_blk // 2
    interp_level = jnp.swapaxes(interp_level, 2, 3)
    vmem = pl.BlockSpec(memory_space=pltpu.VMEM)
    small = [fetch_owner, fetch_block, fetch_count, interp_level, block_mask]
    rim = lambda planes, rows, n: pltpu.VMEM((n, planes, rows, LANES), BF16)
    sems = lambda n: pltpu.SemaphoreType.DMA((n,))
    smoothed, scale = pl.pallas_call(
        functools.partial(kernel, n_slab, n_blk),
        out_shape=(
            jax.ShapeDtypeStruct((3, SIDE, SIDE, LANES), F32),
            jax.ShapeDtypeStruct((1, LANES), F32),
        ),
        in_specs=[pl.BlockSpec(memory_space=pltpu.HBM)] * 7,
        out_specs=(pl.BlockSpec(memory_space=pltpu.HBM), vmem),
        scratch_shapes=[
            pltpu.VMEM((3, SIDE, SIDE, LANES), F32),
            pltpu.SemaphoreType.DMA,
            pltpu.VMEM((SIDE, SIDE, LANES), BF16),
            *[pltpu.SMEM(one.shape, jnp.int32) for one in small],
            sems(7),
            pltpu.VMEM((n_blk, SIDE, SIDE, LANES), BF16),
            pltpu.VMEM((chips, 4 * LANES, 4 * LANES), BF16),
            pltpu.VMEM((SIDE * SIDE, 4 * LANES), F32),
            pltpu.VMEM((PLANES, ROWS, LANES), F32),
            pltpu.VMEM((PLANES, ROWS, LANES), F32),
            pltpu.VMEM((3, PLANES, ROWS, LANES), F32),
            pltpu.VMEM((3, PLANES, FROWS, LANES), F32),
            pltpu.VMEM((FPLANES, FROWS, LANES), F32),
            pltpu.VMEM((FPLANES, FROWS, LANES), F32),
            pltpu.VMEM((FPLANES, FROWS, LANES), F32),
            pltpu.VMEM((PLANES, ROWS, LANES), F32),
            pltpu.VMEM((FPLANES // 2, 6 * FROWS, LANES), F32),
            pltpu.VMEM((FPLANES // 2, 6, FROWS, LANES), F32),
            pltpu.VMEM((3, FPLANES, SIDE, LANES), F32),
            pltpu.VMEM((3, FROWS, LANES), F32),
            pltpu.VMEM((LANES, 2 * LANES), BF16),
            pltpu.VMEM((2 * LANES, LANES), BF16),
            pltpu.VMEM((LANES, 2 * LANES), BF16),
            rim(HALO + 1, SIDE, 2),
            rim(HALO + 1, SIDE, 2),
            rim(HALO + 1, SIDE, 2),
            rim(HALO + 1, SIDE, 2),
            rim(HALO + 1, 16, 4),
            rim(HALO, SIDE, 2),
            rim(HALO, SIDE, 2),
            rim(HALO, SIDE, 2),
            rim(HALO, SIDE, 2),
            rim(HALO, 16, 4),
            pltpu.VMEM((2, 8, LANES), F32),
            pltpu.VMEM((n_blk, 8, LANES), F32),
            pltpu.VMEM((n_slab, 8, LANES), F32),
            sems(2 * n_blk),
            sems(2 * n_blk),
            sems(8),
            sems(8),
            sems(8),
            sems(8),
            sems(n_blk),
            sems(n_blk),
            sems(n_slab),
            sems(n_slab),
        ],
        compiler_params=pltpu.CompilerParams(
            collective_id=0, has_side_effects=True, vmem_limit_bytes=64 * 1024 * 1024
        ),
        name="syn_step",
    )(
        fixed_image,
        moving_image,
        fetch_owner,
        fetch_block,
        fetch_count,
        interp_level,
        block_mask,
    )
    return smoothed * scale.reshape(1, 1, 1, LANES)


def solution(mesh):
    in_specs = (
        P("blk", "slab", None),
        P("blk", "slab", None),
        P("blk", "slab", None, None),
        P("blk", "slab", None, None),
        P("blk", "slab", None),
        P("blk", "slab", None, None, None),
        P("blk", "slab", None),
    )
    out_specs = P(None, "blk", "slab", None)
    return jax.shard_map(
        functools.partial(per_device, mesh.shape["slab"], mesh.shape["blk"]),
        mesh=mesh,
        in_specs=in_specs,
        out_specs=out_specs,
        check_vma=False,
    )
```

```python
import functools
import math

import jax
import jax.numpy as jnp
from jax import lax
from jax.experimental import pallas as pl
from jax.experimental.pallas import tpu as pltpu
from jax.sharding import PartitionSpec as P

LEVELS = 8
BOX_RADIUS = 2
SMOOTH_RADIUS = 3
HALO = BOX_RADIUS + SMOOTH_RADIUS

sigma_smooth = 1.5
step_length = 2.0
var_eps = 1e-05
peak_eps = 1e-06

SIDE = 32
LANES = 128
PLANES = SIDE + 2 * HALO
ROWS = 48
FIRST = 8
FPLANES = SIDE + 2 * SMOOTH_RADIUS
FROWS = 40
F32 = jnp.float32
BF16 = jnp.bfloat16
MESH = pl.DeviceIdType.MESH
DIRECTIONS = ((1, 0), (-1, 0), (0, 1), (0, -1), (1, 1), (1, -1), (-1, 1), (-1, -1))


def smooth_weights(radius):
    weights_raw = [
        math.exp(-(offset * offset) / (2.0 * sigma_smooth * sigma_smooth))
        for offset in range(-radius, radius + 1)
    ]
    weights_total = sum(weights_raw)
    return [weight_one / weights_total for weight_one in weights_raw]


def kernel(
    n_slab,
    n_blk,
    fixed_hbm,
    moving_hbm,
    owner_hbm,
    block_hbm,
    count_hbm,
    level_hbm,
    mask_hbm,
    out_hbm,
    scale_ref,
    out_ref,
    out_sem,
    fixed_ref,
    owner_ref,
    block_ref,
    count_ref,
    level_ref,
    mask_ref,
    in_sem,
    gath,
    select,
    acc,
    f_ext,
    m_ext,
    ybox,
    zbox,
    f_mean,
    f_inv,
    f_dev,
    grad_y,
    forces,
    ysm,
    zsm,
    mask_pl,
    band_m,
    band_2,
    band_s,
    fx_send,
    fz_send,
    fx_recv,
    fz_recv,
    fc_recv,
    mx_send,
    mz_send,
    mx_recv,
    mz_recv,
    mc_recv,
    pk_send,
    pk_blk,
    pk_slab,
    ag_ssem,
    ag_rsem,
    f_ssem,
    f_rsem,
    m_ssem,
    m_rsem,
    pb_ssem,
    pb_rsem,
    ps_ssem,
    ps_rsem,
):
    me_s = lax.axis_index("slab")
    me_b = lax.axis_index("blk")
    chips = n_blk // 2
    chip = me_b // 2
    core = me_b % 2
    taps = smooth_weights(SMOOTH_RADIUS)

    def there(dx, dz):
        ok = None
        for d, me, n in ((dx, me_b, n_blk), (dz, me_s, n_slab)):
            if d == 0:
                continue
            now = me + d < n if d > 0 else me + d >= 0
            ok = now if ok is None else jnp.logical_and(ok, now)
        return ok

    loads = [
        pltpu.make_async_copy(src, dst, in_sem.at[i])
        for i, (src, dst) in enumerate(
            (
                (fixed_hbm, fixed_ref),
                (moving_hbm, gath.at[0]),
                (owner_hbm, owner_ref),
                (block_hbm, block_ref),
                (count_hbm, count_ref),
                (level_hbm, level_ref),
                (mask_hbm, mask_ref),
            )
        )
    ]
    for load in loads:
        load.start()

    barrier = pltpu.get_barrier_semaphore()
    for d in range(1, n_blk):
        pl.semaphore_signal(
            barrier, inc=1, device_id=(me_s, (me_b + d) % n_blk), device_id_type=MESH
        )
    for d in range(1, n_slab):
        pl.semaphore_signal(
            barrier, inc=1, device_id=((me_s + d) % n_slab, me_b), device_id_type=MESH
        )
    for dx, dz in DIRECTIONS[4:]:

        @pl.when(there(dx, dz))
        def _():
            pl.semaphore_signal(
                barrier, inc=1, device_id=(me_s + dz, me_b + dx), device_id_type=MESH
            )

    def rim_copies(x_send, z_send, x_recv, z_recv, c_recv, ssem, rsem):
        copies = []
        for i, (dx, dz) in enumerate(DIRECTIONS):
            if dz == 0:
                src, dst = x_send.at[(dx + 1) // 2], x_recv.at[(dx + 1) // 2]
            elif dx == 0:
                src, dst = z_send.at[(dz + 1) // 2], z_recv.at[(dz + 1) // 2]
            else:
                src = z_send.at[(dz + 1) // 2, :, pl.ds(16 if dx > 0 else 0, 16), :]
                dst = c_recv.at[i - 4]
            copies.append(
                pltpu.make_async_remote_copy(
                    src_ref=src,
                    dst_ref=dst,
                    send_sem=ssem.at[i],
                    recv_sem=rsem.at[i],
                    device_id=(me_s + dz, me_b + dx),
                    device_id_type=MESH,
                )
            )
        return copies

    def start_all(copies):
        for (dx, dz), copy in zip(DIRECTIONS, copies):
            pl.when(there(dx, dz))(copy.start)

    def finish_all(copies):
        for (dx, dz), copy in zip(DIRECTIONS, copies):
            pl.when(there(dx, dz))(copy.wait_send)

    def pack_rims(ext, x_send, z_send):
        flat = ext.reshape(PLANES * ROWS, LANES)
        for j in range(HALO):
            for side, at in ((0, j), (1, SIDE - HALO + j)):
                z_send[side, j] = flat[
                    pl.ds(HALO * ROWS + FIRST + at, SIDE, stride=ROWS), :
                ].astype(BF16)
                x_send[side, j] = ext[HALO + at, FIRST : FIRST + SIDE, :].astype(BF16)

    def fill_rims(copies, ext, x_recv, z_recv, c_recv, mask):
        flat = ext.reshape(PLANES * ROWS, LANES)
        for i, (dx, dz) in enumerate(DIRECTIONS):
            at_x = 0 if dx > 0 else HALO + SIDE
            at_z = FIRST - HALO if dz > 0 else FIRST + SIDE
            region = {1: 0, 0: 1, -1: 2}[dx]
            row_at = {1: 0, 0: SMOOTH_RADIUS, -1: SMOOTH_RADIUS + SIDE}[dz]
            row_n = SIDE if dz == 0 else SMOOTH_RADIUS

            @pl.when(there(-dx, -dz))
            def _():
                copies[i].wait_recv()
                side_x, side_z = (dx + 1) // 2, (dz + 1) // 2
                for j in range(HALO):
                    if dz == 0:
                        ext[at_x + j, FIRST : FIRST + SIDE, :] = x_recv[side_x, j].astype(F32)
                    elif dx == 0:
                        flat[pl.ds(HALO * ROWS + at_z + j, SIDE, stride=ROWS), :] = z_recv[
                            side_z, j
                        ].astype(F32)
                    else:
                        rows = c_recv[i - 4, j].astype(F32)
                        rows = rows[16 - HALO :] if dx > 0 else rows[:HALO]
                        flat[pl.ds(at_x * ROWS + at_z + j, HALO, stride=ROWS), :] = rows
                if mask:
                    if dz == 0:
                        plane = x_recv[side_x, HALO].astype(F32)
                    elif dx == 0:
                        plane = z_recv[side_z, HALO].astype(F32)
                    else:
                        plane = c_recv[i - 4, HALO].astype(F32)
                    mask_pl[region, row_at : row_at + row_n, :] = plane[:row_n]

    lane = lax.broadcasted_iota(jnp.int32, (1, LANES), 1)

    def by_block(scalars):
        vec = jnp.full((1, LANES), scalars[3], jnp.int32)
        for g in range(3):
            vec = jnp.where(lane // SIDE == g, scalars[g], vec)
        return vec

    nought = me_b // n_blk
    for ext in (f_ext, m_ext):

        @pl.loop(0, PLANES // 7)
        def _(x):
            ext[pl.ds(x * 7, 7)] = jnp.zeros((7, ROWS, LANES), F32)

    loads[0].wait()
    loads[6].wait()

    mask_pl[...] = jnp.zeros_like(mask_pl)
    own_mask = by_block([mask_ref[0, 0, g] for g in range(4)]).astype(F32)
    mask_rows = jnp.broadcast_to(own_mask, (SIDE, LANES))
    mask_pl[1, SMOOTH_RADIUS : SMOOTH_RADIUS + SIDE, :] = mask_rows

    @pl.loop(0, SIDE // 4)
    def _(x):
        at = pl.ds(HALO + x * 4, 4)
        f_ext[at, FIRST : FIRST + SIDE, :] = fixed_ref[pl.ds(x * 4, 4)].astype(F32)

    pack_rims(f_ext, fx_send, fz_send)
    for side in range(2):
        fx_send[side, HALO] = mask_rows.astype(BF16)
        fz_send[side, HALO] = mask_rows.astype(BF16)
    wide_x = jnp.where(me_b > 0, 1, 0) + jnp.where(me_b < n_blk - 1, 1, 0)
    wide_z = jnp.where(me_s > 0, 1, 0) + jnp.where(me_s < n_slab - 1, 1, 0)
    pl.semaphore_wait(barrier, n_blk - 1 + n_slab - 1 + wide_x * wide_z)

    f_copies = rim_copies(fx_send, fz_send, fx_recv, fz_recv, fc_recv, f_ssem, f_rsem)
    start_all(f_copies)

    if chips == 4:
        flip_x = chip + 1 - 2 * (chip % 2)
        flip_y = chip + 2 - 4 * (chip // 2)
        away = [chip, flip_x, flip_y, 3 - chip]
    else:
        away = [(chip + chips - e) % chips for e in range(chips)]
    half = SIDE // 2

    def remote(src, dst, at, device):
        return pltpu.make_async_remote_copy(
            src_ref=src,
            dst_ref=dst,
            send_sem=ag_ssem.at[at],
            recv_sem=ag_rsem.at[at],
            device_id=device,
            device_id_type=MESH,
        )

    def piece(e, h):
        rows = pl.ds(h * half, half)
        at = 4 * e + 2 * h
        if chips != 4:
            target = (chip + e) % chips
            src = moving_hbm.at[rows]
        elif e < 3:
            target = away[e]
            src = moving_hbm.at[rows]
        else:
            target = away[2 - h]
            src = gath.at[2 * (1 + h), rows]
        return remote(src, gath.at[2 * e, rows], at, (me_s, 2 * target + core))

    def passed(e, h):
        rows = pl.ds(h * half, half)
        src = moving_hbm.at[rows] if e == 0 else gath.at[2 * e, rows]
        return remote(
            src, gath.at[2 * e + 1, rows], 4 * e + 2 * h + 1, (me_s, 2 * chip + 1 - core)
        )

    if chips == 4:
        for e, h in ((1, 0), (2, 1), (1, 1), (2, 0)):
            piece(e, h).start()
    else:
        for e in range(1, chips):
            for h in range(2):
                piece(e, h).start()
    for h in range(2):
        passed(0, h).start()

    def take(e, h):
        piece(e, h).wait_recv()
        if chips == 4 and (e, h) in ((1, 0), (2, 1)):
            piece(3, h).start()
        passed(e, h).start()

    for load in loads[2:6]:
        load.wait()
    places, mixes = [], []
    counts = by_block([count_ref[0, 0, g] for g in range(4)])
    at_end = lane % SIDE == SIDE - 1
    for k in range(4):
        f_x, f_z, f_y = [
            by_block([level_ref[0, 0, a, g, k] for g in range(4)]).astype(F32) / LEVELS
            for a in range(3)
        ]
        places.append(
            by_block([owner_ref[0, 0, g, k] for g in range(4)]) * LANES
            + by_block([block_ref[0, 0, g, k] for g in range(4)]) * SIDE
            + lane % SIDE
        )
        listed = jnp.where(counts > k, 1.0, 0.0)
        mixes.append(
            (
                jnp.where(at_end, 1.0, 1.0 - f_y),
                jnp.where(at_end, 0.0, f_y),
                [
                    listed * (f_x if mx else 1.0 - f_x) * (f_z if mz else 1.0 - f_z)
                    for mx, mz in ((0, 0), (1, 0), (0, 1), (1, 1))
                ],
            )
        )
    share = 1.0 / counts.astype(F32)
    sub = lax.broadcasted_iota(jnp.int32, (LANES, LANES), 0)

    @pl.loop(0, LANES // SIDE)
    def _(part):
        row = lax.broadcasted_iota(jnp.int32, (SIDE, LANES), 0) + part * SIDE
        for e in range(chips):
            for p in range(2):
                base = (2 * away[e] + (core if p == 0 else 1 - core)) * LANES
                totals = [None] * 4
                for k in range(4):
                    first = places[k] - base
                    y_stay, y_move, mix = mixes[k]
                    taken = jnp.where(
                        row == first, y_stay, jnp.where(row == first + 1, y_move, 0.0)
                    )
                    for c in range(4):
                        term = taken * mix[c]
                        totals[c] = term if k == 0 else totals[c] + term
                for c in range(4):
                    cols = slice(c * LANES, (c + 1) * LANES)
                    high = totals[c].astype(BF16)
                    low = (totals[c] - high.astype(F32)).astype(BF16)
                    at = pl.multiple_of(p * LANES + part * SIDE, SIDE)
                    select[e, pl.ds(at, SIDE), cols] = high
                    select[e, pl.ds(at + 2 * LANES, SIDE), cols] = low

    off = sub - lax.broadcasted_iota(jnp.int32, (LANES, LANES), 1)
    band = jnp.where(jnp.abs(off) <= BOX_RADIUS, 1.0, 0.0).astype(BF16)
    band_m[:, :LANES] = band
    band_m[:, LANES:] = (
        jnp.where(off == 1, 0.5, 0.0) - jnp.where(off == -1, 0.5, 0.0)
    ).astype(BF16)
    band_2[:LANES] = band
    band_2[LANES:] = band
    bell = jnp.zeros((LANES, LANES), F32)
    for t in range(2 * SMOOTH_RADIUS + 1):
        bell = jnp.where(off == t - SMOOTH_RADIUS, taps[t], bell)
    bell_hi = bell.astype(BF16)
    band_s[:, :LANES] = bell_hi
    band_s[:, LANES:] = (bell - bell_hi.astype(F32)).astype(BF16)

    def halves(product):
        high = product.astype(BF16)
        return jnp.concatenate([high, (product - high.astype(F32)).astype(BF16)], axis=1)

    def shifted(ref, lead, start, rows):
        return ref[(*lead, pl.ds(nought + start, rows), slice(None))]

    def z_sum(q, j, first=0, rows=FROWS):
        total = shifted(ybox, (q, j), first + 3, rows)
        for t in range(1, 5):
            total = total + shifted(ybox, (q, j), first + 3 + t, rows)
        zbox[q, j, first : first + rows] = total

    def x_sums(q, i, first=0, rows=FROWS):
        v = [zbox[q, i + t, first : first + rows] for t in range(6)]
        shared = (v[1] + v[2]) + (v[3] + v[4])
        return v[0] + shared, shared + v[5]

    def inverse(value):
        guess = pltpu.reciprocal(value, approx=True)
        return guess * (2.0 - value * guess)

    per_box = 1.0 / float((2 * BOX_RADIUS + 1) ** 3)

    def resample(e, begin=0, end=4):
        @pl.loop(begin, end)
        def _(part):
            at = pl.ds(part * 8, 8)
            pair = jnp.concatenate(
                [gath[2 * e, at].reshape(256, LANES), gath[2 * e + 1, at].reshape(256, LANES)],
                axis=1,
            )
            pair = jnp.concatenate([pair, pair], axis=1)
            got = jnp.dot(pair, select[e], preferred_element_type=F32)
            rows = pl.ds(part * 256, 256)
            if e == 0:
                acc[rows, :] = got
            else:
                acc[rows, :] = acc[rows, :] + got

    if chips == 4:
        take(1, 0)
        take(2, 1)

    fill_rims(f_copies, f_ext, fx_recv, fz_recv, fc_recv, True)

    @pl.loop(0, PLANES // 7)
    def _(step):
        at = pl.ds(step * 7, 7)
        planes = f_ext[at].reshape(7 * ROWS, LANES)
        y_f = jnp.dot(planes.astype(BF16), band, preferred_element_type=F32)
        y_ff = jnp.dot(halves(planes * planes), band_2[...], preferred_element_type=F32)
        ybox[0, at] = y_f.reshape(7, ROWS, LANES)
        ybox[1, at] = y_ff.reshape(7, ROWS, LANES)

    if chips == 4:
        take(1, 1)
        take(2, 0)

    @pl.loop(0, PLANES // 2)
    def _(step):
        for j in range(2):
            for q in range(2):
                z_sum(q, 2 * step + j)

    loads[1].wait()
    for h in range(2):
        passed(0, h).wait_recv()
    resample(0)

    @pl.loop(0, FPLANES // 2)
    def _(step):
        i = 2 * step
        sums = x_sums(0, i), x_sums(1, i)
        for j in range(2):
            mean = sums[0][j] * per_box
            var = sums[1][j] * per_box - mean * mean + var_eps
            f_mean[i + j] = mean
            f_inv[i + j] = inverse(var)
            f_dev[i + j] = shifted(f_ext, (i + j + 2,), 5, FROWS) - mean

    if chips != 4:
        for e in range(1, chips):
            for h in range(2):
                take(e, h)
    for e in range(1, chips):
        for h in range(2):
            if chips == 4 and e == 2:
                take(3, h)
            passed(e, h).wait_recv()
            if e == chips - 1:
                resample(e, 2 * h, 2 * h + 2)
        if e < chips - 1:
            resample(e)

    last_row = lax.broadcasted_iota(jnp.int32, (SIDE, LANES), 0) == SIDE - 1

    @pl.loop(0, SIDE, unroll=4)
    def _(x):
        here = pl.ds(pl.multiple_of(x * SIDE, SIDE), SIDE)
        after = pl.ds(pl.multiple_of(jnp.minimum(x + 1, SIDE - 1) * SIDE, SIDE), SIDE)
        stay = acc[here, :LANES] + acc[after, LANES : 2 * LANES]
        move = acc[here, 2 * LANES : 3 * LANES] + acc[after, 3 * LANES :]
        moved = jnp.where(last_row, move, pltpu.roll(move, SIDE - 1, 0))
        warped = ((stay + moved) * share).astype(BF16).astype(F32)
        m_ext[HALO + x, FIRST : FIRST + SIDE, :] = warped

    pack_rims(m_ext, mx_send, mz_send)
    m_copies = rim_copies(mx_send, mz_send, mx_recv, mz_recv, mc_recv, m_ssem, m_rsem)
    start_all(m_copies)

    def y_pass(planes, rows, shape):
        count = shape[0] * shape[1]
        m_now = m_ext[planes, rows].reshape(count, LANES)
        f_now = f_ext[planes, rows].reshape(count, LANES)
        y_m = jnp.dot(m_now.astype(BF16), band_m[...], preferred_element_type=F32)
        products = jnp.concatenate([halves(m_now * m_now), halves(f_now * m_now)], axis=0)
        y_p = jnp.dot(products, band_2[...], preferred_element_type=F32)
        ybox[0, planes, rows] = y_m[:, :LANES].reshape(*shape, LANES)
        grad_y[planes, rows] = y_m[:, LANES:].reshape(*shape, LANES)
        ybox[1, planes, rows] = y_p[:count].reshape(*shape, LANES)
        ybox[2, planes, rows] = y_p[count:].reshape(*shape, LANES)

    @pl.loop(0, 4)
    def _(part):
        y_pass(pl.ds(HALO + part * 8, 8), slice(FIRST, FIRST + SIDE), (8, SIDE))

    edge = 3
    inner = slice(8, 32)
    outer = (slice(0, 8), slice(32, FROWS))

    def force_rows(now, rows):
        first, n = rows.start, rows.stop - rows.start
        i = 2 * now
        sums = [x_sums(q, i, first, n) for q in range(3)]
        for j in range(2):
            at = i + j
            mean = sums[0][j] * per_box
            var = sums[1][j] * per_box - mean * mean + var_eps
            cov = sums[2][j] * per_box - f_mean[at, rows] * mean
            slope = cov * inverse(var)
            center = shifted(m_ext, (at + 2,), 5 + first, n)
            term = slope * f_inv[at, rows] * (f_dev[at, rows] - slope * (center - mean))
            region = jnp.where(at >= SMOOTH_RADIUS, 1, 0) + jnp.where(
                at >= SMOOTH_RADIUS + SIDE, 1, 0
            )
            term = jnp.where(mask_pl[region, rows] > 0.5, term, 0.0)
            steps = (
                shifted(m_ext, (at + 3,), 5 + first, n) - shifted(m_ext, (at + 1,), 5 + first, n),
                shifted(m_ext, (at + 2,), 6 + first, n) - shifted(m_ext, (at + 2,), 4 + first, n),
                2.0 * shifted(grad_y, (at + 2,), 5 + first, n),
            )
            for c in range(3):
                base = (3 * j + c) * FROWS + first
                forces[now, base : base + n] = term * steps[c]

    @pl.loop(0, SIDE // 2)
    def _(step):
        for j in range(2):
            for q in range(3):
                z_sum(q, HALO + 2 * step + j, 8, 24)

    pairs = FPLANES // 2

    @pl.loop(edge, pairs - edge)
    def _(now):
        force_rows(now, inner)

    fill_rims(m_copies, m_ext, mx_recv, mz_recv, mc_recv, False)
    y_pass(slice(0, HALO), slice(None), (HALO, ROWS))
    y_pass(slice(HALO + SIDE, PLANES), slice(None), (HALO, ROWS))
    y_pass(slice(HALO, HALO + SIDE), slice(0, FIRST), (SIDE, FIRST))
    y_pass(slice(HALO, HALO + SIDE), slice(FIRST + SIDE, ROWS), (SIDE, ROWS - FIRST - SIDE))

    @pl.loop(0, HALO)
    def _(step):
        for at in (step, HALO + SIDE + step):
            for q in range(3):
                z_sum(q, at)

    @pl.loop(0, SIDE // 4)
    def _(step):
        for j in range(4):
            for q in range(3):
                for rows in outer:
                    z_sum(q, HALO + 4 * step + j, rows.start, 8)

    def bell_sum(values):
        total = taps[3] * values[3]
        for t in range(3):
            total = total + taps[t] * (values[t] + values[6 - t])
        return total

    def stages(step, row_sets):
        old = jnp.maximum(step - 2, 0)
        for j in range(2):
            for c in range(3):
                zsm[c, 2 * old + j] = bell_sum(
                    [shifted(ysm, (old, 3 * j + c), t, SIDE) for t in range(7)]
                )
        mid = jnp.minimum(jnp.maximum(step - 1, 0), pairs - 1)
        both = jnp.dot(forces[mid].astype(BF16), band_s[...], preferred_element_type=F32)
        ysm[mid] = (both[:, :LANES] + both[:, LANES:]).reshape(6, FROWS, LANES)
        for rows in row_sets:
            force_rows(step, rows)

    for begin, end, row_sets in (
        (0, edge, (slice(0, FROWS),)),
        (edge, pairs - edge, outer),
        (pairs - edge, pairs, (slice(0, FROWS),)),
        (pairs, pairs + 2, ()),
    ):

        @pl.loop(begin, end)
        def _(step):
            stages(step, row_sets)

    def last_pass(step, top):
        x = 2 * step
        squares = [jnp.zeros((SIDE, LANES), F32) for _ in range(2)]
        for c in range(3):
            values = [zsm[c, x + t] for t in range(8)]
            for j in range(2):
                value = bell_sum(values[j : j + 7])
                out_ref[c, x + j] = value
                squares[j] = squares[j] + value * value
        return jnp.maximum(top, jnp.maximum(squares[0], squares[1]))

    top = lax.fori_loop(0, SIDE // 2, last_pass, jnp.zeros((SIDE, LANES), F32))
    top = jnp.max(top.reshape(4, 8, LANES), axis=0)
    write = pltpu.make_async_copy(out_ref, out_hbm, out_sem)
    write.start()

    def all_peak(top, n, slots, ssem, rsem, device):
        pk = pk_send.at[0 if slots is pk_blk else 1]
        pk[...] = top
        copies = []
        for d in range(1, n):
            copies.append(
                pltpu.make_async_remote_copy(
                    src_ref=pk,
                    dst_ref=slots.at[d],
                    send_sem=ssem.at[d],
                    recv_sem=rsem.at[d],
                    device_id=device(d),
                    device_id_type=MESH,
                )
            )
        for copy in copies:
            copy.start()
        for d, copy in enumerate(copies):
            copy.wait_recv()
            top = jnp.maximum(top, slots[d + 1])
        return top, copies

    top, blk_copies = all_peak(
        top, n_blk, pk_blk, pb_ssem, pb_rsem, lambda d: (me_s, (me_b + d) % n_blk)
    )
    top, slab_copies = all_peak(
        top, n_slab, pk_slab, ps_ssem, ps_rsem, lambda d: ((me_s + d) % n_slab, me_b)
    )
    peak = jnp.sqrt(jnp.max(top, axis=(0, 1), keepdims=True))
    scale_ref[...] = jnp.broadcast_to(step_length / (peak + peak_eps), (1, LANES))

    for e in range(chips):
        for h in range(2):
            if e > 0:
                piece(e, h).wait_send()
            passed(e, h).wait_send()
    write.wait()
    finish_all(f_copies)
    finish_all(m_copies)
    for copy in blk_copies + slab_copies:
        copy.wait_send()


def scale_kernel(in_hbm, scale_hbm, out_hbm, held, scale_ref, in_sems, out_sems, scale_sem):
    chunks = [(c, pl.ds(h * (SIDE // 2), SIDE // 2)) for c in range(3) for h in range(2)]
    fetch = [
        pltpu.make_async_copy(in_hbm.at[chunk], held.at[chunk], in_sems.at[i])
        for i, chunk in enumerate(chunks)
    ]
    store = [
        pltpu.make_async_copy(held.at[chunk], out_hbm.at[chunk], out_sems.at[i])
        for i, chunk in enumerate(chunks)
    ]
    fetch_scale = pltpu.make_async_copy(scale_hbm, scale_ref, scale_sem)
    fetch_scale.start()
    for copy in fetch:
        copy.start()
    fetch_scale.wait()
    scale = scale_ref[...].reshape(1, 1, LANES)
    for chunk, came, goes in zip(chunks, fetch, store):
        came.wait()
        held[chunk] = held[chunk] * scale
        goes.start()
    for goes in store:
        goes.wait()


def per_device(
    n_slab,
    n_blk,
    fixed_image,
    moving_image,
    fetch_owner,
    fetch_block,
    fetch_count,
    interp_level,
    block_mask,
):
    chips = n_blk // 2
    interp_level = jnp.swapaxes(interp_level, 2, 3)
    vmem = pl.BlockSpec(memory_space=pltpu.VMEM)
    small = [fetch_owner, fetch_block, fetch_count, interp_level, block_mask]
    rim = lambda planes, rows, n: pltpu.VMEM((n, planes, rows, LANES), BF16)
    sems = lambda n: pltpu.SemaphoreType.DMA((n,))
    smoothed, scale = pl.pallas_call(
        functools.partial(kernel, n_slab, n_blk),
        out_shape=(
            jax.ShapeDtypeStruct((3, SIDE, SIDE, LANES), F32),
            jax.ShapeDtypeStruct((1, LANES), F32),
        ),
        in_specs=[pl.BlockSpec(memory_space=pltpu.HBM)] * 7,
        out_specs=(pl.BlockSpec(memory_space=pltpu.HBM), vmem),
        scratch_shapes=[
            pltpu.VMEM((3, SIDE, SIDE, LANES), F32),
            pltpu.SemaphoreType.DMA,
            pltpu.VMEM((SIDE, SIDE, LANES), BF16),
            *[pltpu.SMEM(one.shape, jnp.int32) for one in small],
            sems(7),
            pltpu.VMEM((n_blk, SIDE, SIDE, LANES), BF16),
            pltpu.VMEM((chips, 4 * LANES, 4 * LANES), BF16),
            pltpu.VMEM((SIDE * SIDE, 4 * LANES), F32),
            pltpu.VMEM((PLANES, ROWS, LANES), F32),
            pltpu.VMEM((PLANES, ROWS, LANES), F32),
            pltpu.VMEM((3, PLANES, ROWS, LANES), F32),
            pltpu.VMEM((3, PLANES, FROWS, LANES), F32),
            pltpu.VMEM((FPLANES, FROWS, LANES), F32),
            pltpu.VMEM((FPLANES, FROWS, LANES), F32),
            pltpu.VMEM((FPLANES, FROWS, LANES), F32),
            pltpu.VMEM((PLANES, ROWS, LANES), F32),
            pltpu.VMEM((FPLANES // 2, 6 * FROWS, LANES), F32),
            pltpu.VMEM((FPLANES // 2, 6, FROWS, LANES), F32),
            pltpu.VMEM((3, FPLANES, SIDE, LANES), F32),
            pltpu.VMEM((3, FROWS, LANES), F32),
            pltpu.VMEM((LANES, 2 * LANES), BF16),
            pltpu.VMEM((2 * LANES, LANES), BF16),
            pltpu.VMEM((LANES, 2 * LANES), BF16),
            rim(HALO + 1, SIDE, 2),
            rim(HALO + 1, SIDE, 2),
            rim(HALO + 1, SIDE, 2),
            rim(HALO + 1, SIDE, 2),
            rim(HALO + 1, 16, 4),
            rim(HALO, SIDE, 2),
            rim(HALO, SIDE, 2),
            rim(HALO, SIDE, 2),
            rim(HALO, SIDE, 2),
            rim(HALO, 16, 4),
            pltpu.VMEM((2, 8, LANES), F32),
            pltpu.VMEM((n_blk, 8, LANES), F32),
            pltpu.VMEM((n_slab, 8, LANES), F32),
            sems(2 * n_blk),
            sems(2 * n_blk),
            sems(8),
            sems(8),
            sems(8),
            sems(8),
            sems(n_blk),
            sems(n_blk),
            sems(n_slab),
            sems(n_slab),
        ],
        compiler_params=pltpu.CompilerParams(
            collective_id=0, has_side_effects=True, vmem_limit_bytes=64 * 1024 * 1024
        ),
        name="syn_step",
    )(
        fixed_image,
        moving_image,
        fetch_owner,
        fetch_block,
        fetch_count,
        interp_level,
        block_mask,
    )
    return pl.pallas_call(
        scale_kernel,
        out_shape=jax.ShapeDtypeStruct((3, SIDE, SIDE, LANES), F32),
        in_specs=[pl.BlockSpec(memory_space=pltpu.HBM)] * 2,
        out_specs=pl.BlockSpec(memory_space=pltpu.HBM),
        scratch_shapes=[
            pltpu.VMEM((3, SIDE, SIDE, LANES), F32),
            pltpu.VMEM((1, LANES), F32),
            sems(6),
            sems(6),
            pltpu.SemaphoreType.DMA,
        ],
        compiler_params=pltpu.CompilerParams(vmem_limit_bytes=64 * 1024 * 1024),
        name="scale_step",
    )(smoothed, scale)


def solution(mesh):
    in_specs = (
        P("blk", "slab", None),
        P("blk", "slab", None),
        P("blk", "slab", None, None),
        P("blk", "slab", None, None),
        P("blk", "slab", None),
        P("blk", "slab", None, None, None),
        P("blk", "slab", None),
    )
    out_specs = P(None, "blk", "slab", None)
    return jax.shard_map(
        functools.partial(per_device, mesh.shape["slab"], mesh.shape["blk"]),
        mesh=mesh,
        in_specs=in_specs,
        out_specs=out_specs,
        check_vma=False,
    )
```

```python
import functools
import math

import jax
import jax.numpy as jnp
from jax import lax
from jax.experimental import pallas as pl
from jax.experimental.pallas import tpu as pltpu
from jax.sharding import PartitionSpec as P

LEVELS = 8
BOX_RADIUS = 2
SMOOTH_RADIUS = 3
HALO = BOX_RADIUS + SMOOTH_RADIUS

sigma_smooth = 1.5
step_length = 2.0
var_eps = 1e-05
peak_eps = 1e-06

SIDE = 32
LANES = 128
PLANES = SIDE + 2 * HALO
ROWS = 48
FIRST = 8
FPLANES = SIDE + 2 * SMOOTH_RADIUS
FROWS = 40
F32 = jnp.float32
BF16 = jnp.bfloat16
MESH = pl.DeviceIdType.MESH
DIRECTIONS = ((1, 0), (-1, 0), (0, 1), (0, -1), (1, 1), (1, -1), (-1, 1), (-1, -1))


def smooth_weights(radius):
    weights_raw = [
        math.exp(-(offset * offset) / (2.0 * sigma_smooth * sigma_smooth))
        for offset in range(-radius, radius + 1)
    ]
    weights_total = sum(weights_raw)
    return [weight_one / weights_total for weight_one in weights_raw]


def kernel(
    n_slab,
    n_blk,
    fixed_hbm,
    moving_hbm,
    owner_hbm,
    block_hbm,
    count_hbm,
    level_hbm,
    mask_hbm,
    out_hbm,
    scale_ref,
    out_ref,
    out_sem,
    fixed_ref,
    owner_ref,
    block_ref,
    count_ref,
    level_ref,
    mask_ref,
    in_sem,
    gath,
    select,
    acc,
    f_ext,
    m_ext,
    ybox,
    zbox,
    f_mean,
    f_inv,
    f_dev,
    grad_y,
    forces,
    ysm,
    zsm,
    mask_pl,
    band_m,
    band_2,
    band_s,
    fx_recv,
    fz_recv,
    fc_recv,
    mx_send,
    mz_send,
    mx_recv,
    mz_recv,
    mc_recv,
    pk_send,
    pk_blk,
    pk_slab,
    ag_ssem,
    ag_rsem,
    f_ssem,
    f_rsem,
    m_ssem,
    m_rsem,
    pb_ssem,
    pb_rsem,
    ps_ssem,
    ps_rsem,
):
    me_s = lax.axis_index("slab")
    me_b = lax.axis_index("blk")
    chips = n_blk // 2
    chip = me_b // 2
    core = me_b % 2
    taps = smooth_weights(SMOOTH_RADIUS)

    def there(dx, dz):
        ok = None
        for d, me, n in ((dx, me_b, n_blk), (dz, me_s, n_slab)):
            if d == 0:
                continue
            now = me + d < n if d > 0 else me + d >= 0
            ok = now if ok is None else jnp.logical_and(ok, now)
        return ok

    loads = [
        pltpu.make_async_copy(src, dst, in_sem.at[i])
        for i, (src, dst) in enumerate(
            (
                (fixed_hbm, fixed_ref),
                (moving_hbm, gath.at[0]),
                (owner_hbm, owner_ref),
                (block_hbm, block_ref),
                (count_hbm, count_ref),
                (level_hbm, level_ref),
                (mask_hbm, mask_ref),
            )
        )
    ]
    for load in loads:
        load.start()

    barrier = pltpu.get_barrier_semaphore()
    for d in range(1, n_blk):
        pl.semaphore_signal(
            barrier, inc=1, device_id=(me_s, (me_b + d) % n_blk), device_id_type=MESH
        )
    for d in range(1, n_slab):
        pl.semaphore_signal(
            barrier, inc=1, device_id=((me_s + d) % n_slab, me_b), device_id_type=MESH
        )
    for dx, dz in DIRECTIONS[4:]:

        @pl.when(there(dx, dz))
        def _():
            pl.semaphore_signal(
                barrier, inc=1, device_id=(me_s + dz, me_b + dx), device_id_type=MESH
            )

    def rim_copies(x_send, z_send, x_recv, z_recv, c_recv, ssem, rsem):
        copies = []
        for i, (dx, dz) in enumerate(DIRECTIONS):
            if dz == 0:
                src, dst = x_send.at[(dx + 1) // 2], x_recv.at[(dx + 1) // 2]
            elif dx == 0:
                src, dst = z_send.at[(dz + 1) // 2], z_recv.at[(dz + 1) // 2]
            else:
                src = z_send.at[(dz + 1) // 2, :, pl.ds(16 if dx > 0 else 0, 16), :]
                dst = c_recv.at[i - 4]
            copies.append(
                pltpu.make_async_remote_copy(
                    src_ref=src,
                    dst_ref=dst,
                    send_sem=ssem.at[i],
                    recv_sem=rsem.at[i],
                    device_id=(me_s + dz, me_b + dx),
                    device_id_type=MESH,
                )
            )
        return copies

    def start_all(copies):
        for (dx, dz), copy in zip(DIRECTIONS, copies):
            pl.when(there(dx, dz))(copy.start)

    def finish_all(copies):
        for (dx, dz), copy in zip(DIRECTIONS, copies):
            pl.when(there(dx, dz))(copy.wait_send)

    def pack_rims(ext, x_send, z_send):
        flat = ext.reshape(PLANES * ROWS, LANES)
        for j in range(HALO):
            for side, at in ((0, j), (1, SIDE - HALO + j)):
                z_send[side, j] = flat[
                    pl.ds(HALO * ROWS + FIRST + at, SIDE, stride=ROWS), :
                ].astype(BF16)
                x_send[side, j] = ext[HALO + at, FIRST : FIRST + SIDE, :].astype(BF16)

    def fill_rims(copies, ext, x_recv, z_recv, c_recv):
        flat = ext.reshape(PLANES * ROWS, LANES)
        for i, (dx, dz) in enumerate(DIRECTIONS):
            at_x = 0 if dx > 0 else HALO + SIDE
            at_z = FIRST - HALO if dz > 0 else FIRST + SIDE
            region = {1: 0, 0: 1, -1: 2}[dx]
            row_at = {1: 0, 0: SMOOTH_RADIUS, -1: SMOOTH_RADIUS + SIDE}[dz]
            row_n = SIDE if dz == 0 else SMOOTH_RADIUS

            @pl.when(there(-dx, -dz))
            def _():
                copies[i].wait_recv()
                side_x, side_z = (dx + 1) // 2, (dz + 1) // 2
                for j in range(HALO):
                    if dz == 0:
                        ext[at_x + j, FIRST : FIRST + SIDE, :] = x_recv[side_x, j].astype(F32)
                    elif dx == 0:
                        flat[pl.ds(HALO * ROWS + at_z + j, SIDE, stride=ROWS), :] = z_recv[
                            side_z, j
                        ].astype(F32)
                    else:
                        rows = c_recv[i - 4, j].astype(F32)
                        rows = rows[16 - HALO :] if dx > 0 else rows[:HALO]
                        flat[pl.ds(at_x * ROWS + at_z + j, HALO, stride=ROWS), :] = rows
                if dz == 0:
                    plane = x_recv[side_x, HALO].astype(F32)
                elif dx == 0:
                    plane = z_recv[side_z, HALO].astype(F32)
                else:
                    plane = c_recv[i - 4, HALO].astype(F32)
                mask_pl[region, row_at : row_at + row_n, :] = plane[:row_n]

    lane = lax.broadcasted_iota(jnp.int32, (1, LANES), 1)

    def by_block(scalars):
        vec = jnp.full((1, LANES), scalars[3], jnp.int32)
        for g in range(3):
            vec = jnp.where(lane // SIDE == g, scalars[g], vec)
        return vec

    wide_x = jnp.where(me_b > 0, 1, 0) + jnp.where(me_b < n_blk - 1, 1, 0)
    wide_z = jnp.where(me_s > 0, 1, 0) + jnp.where(me_s < n_slab - 1, 1, 0)
    pl.semaphore_wait(barrier, n_blk - 1 + n_slab - 1 + wide_x * wide_z)

    f_copies = []
    for i, (dx, dz) in enumerate(DIRECTIONS):
        planes = pl.ds(0 if dx < 0 else SIDE - HALO, HALO)
        rows = pl.ds(0 if dz < 0 else SIDE - 16, 16)
        if dz == 0:
            src, dst = fixed_hbm.at[planes], fx_recv.at[(dx + 1) // 2]
        elif dx == 0:
            src, dst = fixed_hbm.at[:, rows], fz_recv.at[(dz + 1) // 2]
        else:
            src, dst = fixed_hbm.at[planes, rows], fc_recv.at[i - 4]
        f_copies.append(
            pltpu.make_async_remote_copy(
                src_ref=src,
                dst_ref=dst,
                send_sem=f_ssem.at[i],
                recv_sem=f_rsem.at[i],
                device_id=(me_s + dz, me_b + dx),
                device_id_type=MESH,
            )
        )
    start_all(f_copies)

    if chips == 4:
        flip_x = chip + 1 - 2 * (chip % 2)
        flip_y = chip + 2 - 4 * (chip // 2)
        away = [chip, flip_x, flip_y, 3 - chip]
    else:
        away = [(chip + chips - e) % chips for e in range(chips)]
    half = SIDE // 2

    def remote(src, dst, at, device):
        return pltpu.make_async_remote_copy(
            src_ref=src,
            dst_ref=dst,
            send_sem=ag_ssem.at[at],
            recv_sem=ag_rsem.at[at],
            device_id=device,
            device_id_type=MESH,
        )

    def piece(e, h):
        rows = pl.ds(h * half, half)
        at = 4 * e + 2 * h
        if chips != 4:
            target = (chip + e) % chips
            src = moving_hbm.at[rows]
        elif e < 3:
            target = away[e]
            src = moving_hbm.at[rows]
        else:
            target = away[2 - h]
            src = gath.at[2 * (1 + h), rows]
        return remote(src, gath.at[2 * e, rows], at, (me_s, 2 * target + core))

    def passed(e, h):
        rows = pl.ds(h * half, half)
        src = moving_hbm.at[rows] if e == 0 else gath.at[2 * e, rows]
        return remote(
            src, gath.at[2 * e + 1, rows], 4 * e + 2 * h + 1, (me_s, 2 * chip + 1 - core)
        )

    if chips == 4:
        for e, h in ((1, 0), (2, 1), (1, 1), (2, 0)):
            piece(e, h).start()
    else:
        for e in range(1, chips):
            for h in range(2):
                piece(e, h).start()
    for h in range(2):
        passed(0, h).start()

    def take(e, h):
        piece(e, h).wait_recv()
        if chips == 4 and (e, h) in ((1, 0), (2, 1)):
            piece(3, h).start()
        passed(e, h).start()

    nought = me_b // n_blk
    for ext in (f_ext, m_ext):

        @pl.loop(0, PLANES // 7)
        def _(x):
            ext[pl.ds(x * 7, 7)] = jnp.zeros((7, ROWS, LANES), F32)

    loads[0].wait()
    loads[6].wait()

    mask_pl[...] = jnp.zeros_like(mask_pl)
    own_mask = by_block([mask_ref[0, 0, g] for g in range(4)]).astype(F32)
    mask_rows = jnp.broadcast_to(own_mask, (SIDE, LANES))
    mask_pl[1, SMOOTH_RADIUS : SMOOTH_RADIUS + SIDE, :] = mask_rows

    @pl.loop(0, SIDE // 4)
    def _(x):
        at = pl.ds(HALO + x * 4, 4)
        f_ext[at, FIRST : FIRST + SIDE, :] = fixed_ref[pl.ds(x * 4, 4)].astype(F32)

    for side in range(2):
        mx_send[side, HALO] = mask_rows.astype(BF16)
        mz_send[side, HALO] = mask_rows.astype(BF16)
    for load in loads[2:6]:
        load.wait()
    places, mixes = [], []
    counts = by_block([count_ref[0, 0, g] for g in range(4)])
    at_end = lane % SIDE == SIDE - 1
    for k in range(4):
        f_x, f_z, f_y = [
            by_block([level_ref[0, 0, a, g, k] for g in range(4)]).astype(F32) / LEVELS
            for a in range(3)
        ]
        places.append(
            by_block([owner_ref[0, 0, g, k] for g in range(4)]) * LANES
            + by_block([block_ref[0, 0, g, k] for g in range(4)]) * SIDE
            + lane % SIDE
        )
        listed = jnp.where(counts > k, 1.0, 0.0)
        mixes.append(
            (
                jnp.where(at_end, 1.0, 1.0 - f_y),
                jnp.where(at_end, 0.0, f_y),
                [
                    listed * (f_x if mx else 1.0 - f_x) * (f_z if mz else 1.0 - f_z)
                    for mx, mz in ((0, 0), (1, 0), (0, 1), (1, 1))
                ],
            )
        )
    share = 1.0 / counts.astype(F32)
    sub = lax.broadcasted_iota(jnp.int32, (LANES, LANES), 0)

    @pl.loop(0, LANES // SIDE)
    def _(part):
        row = lax.broadcasted_iota(jnp.int32, (SIDE, LANES), 0) + part * SIDE
        for e in range(chips):
            for p in range(2):
                base = (2 * away[e] + (core if p == 0 else 1 - core)) * LANES
                totals = [None] * 4
                for k in range(4):
                    first = places[k] - base
                    y_stay, y_move, mix = mixes[k]
                    taken = jnp.where(
                        row == first, y_stay, jnp.where(row == first + 1, y_move, 0.0)
                    )
                    for c in range(4):
                        term = taken * mix[c]
                        totals[c] = term if k == 0 else totals[c] + term
                for c in range(4):
                    cols = slice(c * LANES, (c + 1) * LANES)
                    high = totals[c].astype(BF16)
                    low = (totals[c] - high.astype(F32)).astype(BF16)
                    at = pl.multiple_of(p * LANES + part * SIDE, SIDE)
                    select[e, pl.ds(at, SIDE), cols] = high
                    select[e, pl.ds(at + 2 * LANES, SIDE), cols] = low

    off = sub - lax.broadcasted_iota(jnp.int32, (LANES, LANES), 1)
    band = jnp.where(jnp.abs(off) <= BOX_RADIUS, 1.0, 0.0).astype(BF16)
    band_m[:, :LANES] = band
    band_m[:, LANES:] = (
        jnp.where(off == 1, 0.5, 0.0) - jnp.where(off == -1, 0.5, 0.0)
    ).astype(BF16)
    band_2[:LANES] = band
    band_2[LANES:] = band
    bell = jnp.zeros((LANES, LANES), F32)
    for t in range(2 * SMOOTH_RADIUS + 1):
        bell = jnp.where(off == t - SMOOTH_RADIUS, taps[t], bell)
    bell_hi = bell.astype(BF16)
    band_s[:, :LANES] = bell_hi
    band_s[:, LANES:] = (bell - bell_hi.astype(F32)).astype(BF16)

    def halves(product):
        high = product.astype(BF16)
        return jnp.concatenate([high, (product - high.astype(F32)).astype(BF16)], axis=1)

    def shifted(ref, lead, start, rows):
        return ref[(*lead, pl.ds(nought + start, rows), slice(None))]

    def z_sum(q, j, first=0, rows=FROWS):
        total = shifted(ybox, (q, j), first + 3, rows)
        for t in range(1, 5):
            total = total + shifted(ybox, (q, j), first + 3 + t, rows)
        zbox[q, j, first : first + rows] = total

    def x_sums(q, i, first=0, rows=FROWS):
        v = [zbox[q, i + t, first : first + rows] for t in range(6)]
        shared = (v[1] + v[2]) + (v[3] + v[4])
        return v[0] + shared, shared + v[5]

    def inverse(value):
        guess = pltpu.reciprocal(value, approx=True)
        return guess * (2.0 - value * guess)

    per_box = 1.0 / float((2 * BOX_RADIUS + 1) ** 3)

    def resample(first_e, last_e, h):
        at = slice(h * half, (h + 1) * half)
        rows = slice(h * half * SIDE, (h + 1) * half * SIDE)
        blocks = []
        for e in range(first_e, last_e):
            pair = [gath[2 * e + p, at].reshape(half * SIDE, LANES) for p in range(2)]
            blocks += pair + pair
        got = jnp.dot(
            jnp.concatenate(blocks, axis=1),
            select[first_e:last_e].reshape((last_e - first_e) * 4 * LANES, 4 * LANES),
            preferred_element_type=F32,
        )
        acc[rows, :] = got if first_e == 0 else acc[rows, :] + got

    if chips == 4:
        take(1, 0)
        take(2, 1)

    for i, (dx, dz) in enumerate(DIRECTIONS):
        planes = {1: slice(0, HALO), 0: slice(HALO, HALO + SIDE), -1: slice(HALO + SIDE, PLANES)}[dx]

        @pl.when(there(-dx, -dz))
        def _():
            f_copies[i].wait_recv()
            if dz == 0:
                f_ext[planes, FIRST : FIRST + SIDE] = fx_recv[(dx + 1) // 2].astype(F32)
            else:
                slab = fz_recv[(dz + 1) // 2] if dx == 0 else fc_recv[i - 4]
                slab = slab.astype(F32)
                if dz > 0:
                    f_ext[planes, :FIRST] = slab[:, 8:]
                else:
                    f_ext[planes, FIRST + SIDE :] = slab[:, :8]


    @pl.loop(0, PLANES // 7)
    def _(step):
        at = pl.ds(step * 7, 7)
        planes = f_ext[at].reshape(7 * ROWS, LANES)
        y_f = jnp.dot(planes.astype(BF16), band, preferred_element_type=F32)
        y_ff = jnp.dot(halves(planes * planes), band_2[...], preferred_element_type=F32)
        ybox[0, at] = y_f.reshape(7, ROWS, LANES)
        ybox[1, at] = y_ff.reshape(7, ROWS, LANES)

    if chips == 4:
        take(1, 1)
        take(2, 0)

    @pl.loop(0, PLANES // 2)
    def _(step):
        for j in range(2):
            for q in range(2):
                z_sum(q, 2 * step + j)

    @pl.loop(0, FPLANES // 2)
    def _(step):
        i = 2 * step
        sums = x_sums(0, i), x_sums(1, i)
        for j in range(2):
            mean = sums[0][j] * per_box
            var = sums[1][j] * per_box - mean * mean + var_eps
            f_mean[i + j] = mean
            f_inv[i + j] = inverse(var)
            f_dev[i + j] = shifted(f_ext, (i + j + 2,), 5, FROWS) - mean

    if chips != 4:
        for e in range(1, chips):
            for h in range(2):
                take(e, h)
    loads[1].wait()
    for e in range(chips - 1):
        for h in range(2):
            passed(e, h).wait_recv()
    for h in range(2):
        resample(0, chips - 1, h)
        if chips == 4:
            take(3, h)
    for h in range(2):
        passed(chips - 1, h).wait_recv()
        resample(chips - 1, chips, h)

    last_row = lax.broadcasted_iota(jnp.int32, (SIDE, LANES), 0) == SIDE - 1

    @pl.loop(0, SIDE, unroll=4)
    def _(x):
        here = pl.ds(pl.multiple_of(x * SIDE, SIDE), SIDE)
        after = pl.ds(pl.multiple_of(jnp.minimum(x + 1, SIDE - 1) * SIDE, SIDE), SIDE)
        stay = acc[here, :LANES] + acc[after, LANES : 2 * LANES]
        move = acc[here, 2 * LANES : 3 * LANES] + acc[after, 3 * LANES :]
        moved = jnp.where(last_row, move, pltpu.roll(move, SIDE - 1, 0))
        warped = ((stay + moved) * share).astype(BF16).astype(F32)
        m_ext[HALO + x, FIRST : FIRST + SIDE, :] = warped

    pack_rims(m_ext, mx_send, mz_send)
    m_copies = rim_copies(mx_send, mz_send, mx_recv, mz_recv, mc_recv, m_ssem, m_rsem)
    start_all(m_copies)

    def y_pass(planes, rows, shape):
        count = shape[0] * shape[1]
        m_now = m_ext[planes, rows].reshape(count, LANES)
        f_now = f_ext[planes, rows].reshape(count, LANES)
        y_m = jnp.dot(m_now.astype(BF16), band_m[...], preferred_element_type=F32)
        products = jnp.concatenate([halves(m_now * m_now), halves(f_now * m_now)], axis=0)
        y_p = jnp.dot(products, band_2[...], preferred_element_type=F32)
        ybox[0, planes, rows] = y_m[:, :LANES].reshape(*shape, LANES)
        grad_y[planes, rows] = y_m[:, LANES:].reshape(*shape, LANES)
        ybox[1, planes, rows] = y_p[:count].reshape(*shape, LANES)
        ybox[2, planes, rows] = y_p[count:].reshape(*shape, LANES)

    @pl.loop(0, 4)
    def _(part):
        y_pass(pl.ds(HALO + part * 8, 8), slice(FIRST, FIRST + SIDE), (8, SIDE))

    edge = 3
    inner = slice(8, 32)
    outer = (slice(0, 8), slice(32, FROWS))

    def force_rows(now, rows):
        first, n = rows.start, rows.stop - rows.start
        i = 2 * now
        sums = [x_sums(q, i, first, n) for q in range(3)]
        for j in range(2):
            at = i + j
            mean = sums[0][j] * per_box
            var = sums[1][j] * per_box - mean * mean + var_eps
            cov = sums[2][j] * per_box - f_mean[at, rows] * mean
            slope = cov * inverse(var)
            center = shifted(m_ext, (at + 2,), 5 + first, n)
            term = slope * f_inv[at, rows] * (f_dev[at, rows] - slope * (center - mean))
            region = jnp.where(at >= SMOOTH_RADIUS, 1, 0) + jnp.where(
                at >= SMOOTH_RADIUS + SIDE, 1, 0
            )
            term = jnp.where(mask_pl[region, rows] > 0.5, term, 0.0)
            steps = (
                shifted(m_ext, (at + 3,), 5 + first, n) - shifted(m_ext, (at + 1,), 5 + first, n),
                shifted(m_ext, (at + 2,), 6 + first, n) - shifted(m_ext, (at + 2,), 4 + first, n),
                2.0 * shifted(grad_y, (at + 2,), 5 + first, n),
            )
            for c in range(3):
                base = (3 * j + c) * FROWS + first
                forces[now, base : base + n] = term * steps[c]

    @pl.loop(0, SIDE // 2)
    def _(step):
        for j in range(2):
            for q in range(3):
                z_sum(q, HALO + 2 * step + j, 8, 24)

    pairs = FPLANES // 2

    @pl.loop(edge, pairs - edge)
    def _(now):
        force_rows(now, inner)

    fill_rims(m_copies, m_ext, mx_recv, mz_recv, mc_recv)
    y_pass(slice(0, HALO), slice(None), (HALO, ROWS))
    y_pass(slice(HALO + SIDE, PLANES), slice(None), (HALO, ROWS))
    y_pass(slice(HALO, HALO + SIDE), slice(0, FIRST), (SIDE, FIRST))
    y_pass(slice(HALO, HALO + SIDE), slice(FIRST + SIDE, ROWS), (SIDE, ROWS - FIRST - SIDE))

    @pl.loop(0, HALO)
    def _(step):
        for at in (step, HALO + SIDE + step):
            for q in range(3):
                z_sum(q, at)

    @pl.loop(0, SIDE // 4)
    def _(step):
        for j in range(4):
            for q in range(3):
                for rows in outer:
                    z_sum(q, HALO + 4 * step + j, rows.start, 8)

    def bell_sum(values):
        total = taps[3] * values[3]
        for t in range(3):
            total = total + taps[t] * (values[t] + values[6 - t])
        return total

    def stages(step, row_sets):
        old = jnp.maximum(step - 2, 0)
        for j in range(2):
            for c in range(3):
                zsm[c, 2 * old + j] = bell_sum(
                    [shifted(ysm, (old, 3 * j + c), t, SIDE) for t in range(7)]
                )
        mid = jnp.minimum(jnp.maximum(step - 1, 0), pairs - 1)
        both = jnp.dot(forces[mid].astype(BF16), band_s[...], preferred_element_type=F32)
        ysm[mid] = (both[:, :LANES] + both[:, LANES:]).reshape(6, FROWS, LANES)
        for rows in row_sets:
            force_rows(step, rows)

    for begin, end, row_sets in (
        (0, edge, (slice(0, FROWS),)),
        (edge, pairs - edge, outer),
        (pairs - edge, pairs, (slice(0, FROWS),)),
        (pairs, pairs + 2, ()),
    ):

        @pl.loop(begin, end)
        def _(step):
            stages(step, row_sets)

    def last_pass(step, top):
        x = 2 * step
        squares = [jnp.zeros((SIDE, LANES), F32) for _ in range(2)]
        for c in range(3):
            values = [zsm[c, x + t] for t in range(8)]
            for j in range(2):
                value = bell_sum(values[j : j + 7])
                out_ref[c, x + j] = value
                squares[j] = squares[j] + value * value
        return jnp.maximum(top, jnp.maximum(squares[0], squares[1]))

    top = lax.fori_loop(0, SIDE // 2, last_pass, jnp.zeros((SIDE, LANES), F32))
    top = jnp.max(top.reshape(4, 8, LANES), axis=0)
    write = pltpu.make_async_copy(out_ref, out_hbm, out_sem)
    write.start()

    def all_peak(top, n, slots, ssem, rsem, device):
        pk = pk_send.at[0 if slots is pk_blk else 1]
        pk[...] = top
        copies = []
        for d in range(1, n):
            copies.append(
                pltpu.make_async_remote_copy(
                    src_ref=pk,
                    dst_ref=slots.at[d],
                    send_sem=ssem.at[d],
                    recv_sem=rsem.at[d],
                    device_id=device(d),
                    device_id_type=MESH,
                )
            )
        for copy in copies:
            copy.start()
        for d, copy in enumerate(copies):
            copy.wait_recv()
            top = jnp.maximum(top, slots[d + 1])
        return top, copies

    top, blk_copies = all_peak(
        top, n_blk, pk_blk, pb_ssem, pb_rsem, lambda d: (me_s, (me_b + d) % n_blk)
    )
    top, slab_copies = all_peak(
        top, n_slab, pk_slab, ps_ssem, ps_rsem, lambda d: ((me_s + d) % n_slab, me_b)
    )
    peak = jnp.sqrt(jnp.max(top, axis=(0, 1), keepdims=True))
    scale_ref[...] = jnp.broadcast_to(step_length / (peak + peak_eps), (1, LANES))

    for e in range(chips):
        for h in range(2):
            if e > 0:
                piece(e, h).wait_send()
            passed(e, h).wait_send()
    write.wait()
    finish_all(f_copies)
    finish_all(m_copies)
    for copy in blk_copies + slab_copies:
        copy.wait_send()


def scale_kernel(in_hbm, scale_hbm, out_hbm, held, scale_ref, in_sems, out_sems, scale_sem):
    chunks = [(c, pl.ds(h * (SIDE // 2), SIDE // 2)) for c in range(3) for h in range(2)]
    fetch = [
        pltpu.make_async_copy(in_hbm.at[chunk], held.at[chunk], in_sems.at[i])
        for i, chunk in enumerate(chunks)
    ]
    store = [
        pltpu.make_async_copy(held.at[chunk], out_hbm.at[chunk], out_sems.at[i])
        for i, chunk in enumerate(chunks)
    ]
    fetch_scale = pltpu.make_async_copy(scale_hbm, scale_ref, scale_sem)
    fetch_scale.start()
    for copy in fetch:
        copy.start()
    fetch_scale.wait()
    scale = scale_ref[...].reshape(1, 1, LANES)
    for chunk, came, goes in zip(chunks, fetch, store):
        came.wait()
        held[chunk] = held[chunk] * scale
        goes.start()
    for goes in store:
        goes.wait()


def per_device(
    n_slab,
    n_blk,
    fixed_image,
    moving_image,
    fetch_owner,
    fetch_block,
    fetch_count,
    interp_level,
    block_mask,
):
    chips = n_blk // 2
    interp_level = jnp.swapaxes(interp_level, 2, 3)
    vmem = pl.BlockSpec(memory_space=pltpu.VMEM)
    small = [fetch_owner, fetch_block, fetch_count, interp_level, block_mask]
    rim = lambda planes, rows, n: pltpu.VMEM((n, planes, rows, LANES), BF16)
    sems = lambda n: pltpu.SemaphoreType.DMA((n,))
    smoothed, scale = pl.pallas_call(
        functools.partial(kernel, n_slab, n_blk),
        out_shape=(
            jax.ShapeDtypeStruct((3, SIDE, SIDE, LANES), F32),
            jax.ShapeDtypeStruct((1, LANES), F32),
        ),
        in_specs=[pl.BlockSpec(memory_space=pltpu.HBM)] * 7,
        out_specs=(pl.BlockSpec(memory_space=pltpu.HBM), vmem),
        scratch_shapes=[
            pltpu.VMEM((3, SIDE, SIDE, LANES), F32),
            pltpu.SemaphoreType.DMA,
            pltpu.VMEM((SIDE, SIDE, LANES), BF16),
            *[pltpu.SMEM(one.shape, jnp.int32) for one in small],
            sems(7),
            pltpu.VMEM((n_blk, SIDE, SIDE, LANES), BF16),
            pltpu.VMEM((chips, 4 * LANES, 4 * LANES), BF16),
            pltpu.VMEM((SIDE * SIDE, 4 * LANES), F32),
            pltpu.VMEM((PLANES, ROWS, LANES), F32),
            pltpu.VMEM((PLANES, ROWS, LANES), F32),
            pltpu.VMEM((3, PLANES, ROWS, LANES), F32),
            pltpu.VMEM((3, PLANES, FROWS, LANES), F32),
            pltpu.VMEM((FPLANES, FROWS, LANES), F32),
            pltpu.VMEM((FPLANES, FROWS, LANES), F32),
            pltpu.VMEM((FPLANES, FROWS, LANES), F32),
            pltpu.VMEM((PLANES, ROWS, LANES), F32),
            pltpu.VMEM((FPLANES // 2, 6 * FROWS, LANES), F32),
            pltpu.VMEM((FPLANES // 2, 6, FROWS, LANES), F32),
            pltpu.VMEM((3, FPLANES, SIDE, LANES), F32),
            pltpu.VMEM((3, FROWS, LANES), F32),
            pltpu.VMEM((LANES, 2 * LANES), BF16),
            pltpu.VMEM((2 * LANES, LANES), BF16),
            pltpu.VMEM((LANES, 2 * LANES), BF16),
            rim(HALO, SIDE, 2),
            rim(SIDE, 16, 2),
            rim(HALO, 16, 4),
            rim(HALO + 1, SIDE, 2),
            rim(HALO + 1, SIDE, 2),
            rim(HALO + 1, SIDE, 2),
            rim(HALO + 1, SIDE, 2),
            rim(HALO + 1, 16, 4),
            pltpu.VMEM((2, 8, LANES), F32),
            pltpu.VMEM((n_blk, 8, LANES), F32),
            pltpu.VMEM((n_slab, 8, LANES), F32),
            sems(2 * n_blk),
            sems(2 * n_blk),
            sems(8),
            sems(8),
            sems(8),
            sems(8),
            sems(n_blk),
            sems(n_blk),
            sems(n_slab),
            sems(n_slab),
        ],
        compiler_params=pltpu.CompilerParams(
            collective_id=0, has_side_effects=True, vmem_limit_bytes=64 * 1024 * 1024
        ),
        name="syn_step",
    )(
        fixed_image,
        moving_image,
        fetch_owner,
        fetch_block,
        fetch_count,
        interp_level,
        block_mask,
    )
    return pl.pallas_call(
        scale_kernel,
        out_shape=jax.ShapeDtypeStruct((3, SIDE, SIDE, LANES), F32),
        in_specs=[pl.BlockSpec(memory_space=pltpu.HBM)] * 2,
        out_specs=pl.BlockSpec(memory_space=pltpu.HBM),
        scratch_shapes=[
            pltpu.VMEM((3, SIDE, SIDE, LANES), F32),
            pltpu.VMEM((1, LANES), F32),
            sems(6),
            sems(6),
            pltpu.SemaphoreType.DMA,
        ],
        compiler_params=pltpu.CompilerParams(vmem_limit_bytes=64 * 1024 * 1024),
        name="scale_step",
    )(smoothed, scale)


def solution(mesh):
    in_specs = (
        P("blk", "slab", None),
        P("blk", "slab", None),
        P("blk", "slab", None, None),
        P("blk", "slab", None, None),
        P("blk", "slab", None),
        P("blk", "slab", None, None, None),
        P("blk", "slab", None),
    )
    out_specs = P(None, "blk", "slab", None)
    return jax.shard_map(
        functools.partial(per_device, mesh.shape["slab"], mesh.shape["blk"]),
        mesh=mesh,
        in_specs=in_specs,
        out_specs=out_specs,
        check_vma=False,
    )
```

```python
import functools
import math

import jax
import jax.numpy as jnp
from jax import lax
from jax.experimental import pallas as pl
from jax.experimental.pallas import tpu as pltpu
from jax.sharding import PartitionSpec as P

LEVELS = 8
BOX_RADIUS = 2
SMOOTH_RADIUS = 3
HALO = BOX_RADIUS + SMOOTH_RADIUS

sigma_smooth = 1.5
step_length = 2.0
var_eps = 1e-05
peak_eps = 1e-06

SIDE = 32
LANES = 128
PLANES = SIDE + 2 * HALO
ROWS = 48
FIRST = 8
FPLANES = SIDE + 2 * SMOOTH_RADIUS
FROWS = 40
F32 = jnp.float32
BF16 = jnp.bfloat16
MESH = pl.DeviceIdType.MESH
DIRECTIONS = ((1, 0), (-1, 0), (0, 1), (0, -1), (1, 1), (1, -1), (-1, 1), (-1, -1))


def smooth_weights(radius):
    weights_raw = [
        math.exp(-(offset * offset) / (2.0 * sigma_smooth * sigma_smooth))
        for offset in range(-radius, radius + 1)
    ]
    weights_total = sum(weights_raw)
    return [weight_one / weights_total for weight_one in weights_raw]


def kernel(
    n_slab,
    n_blk,
    fixed_hbm,
    moving_hbm,
    owner_hbm,
    block_hbm,
    count_hbm,
    level_hbm,
    mask_hbm,
    out_hbm,
    scale_ref,
    out_ref,
    out_sem,
    fixed_ref,
    owner_ref,
    block_ref,
    count_ref,
    level_ref,
    mask_ref,
    in_sem,
    gath,
    select,
    acc,
    f_ext,
    m_ext,
    ybox,
    zbox,
    f_mean,
    f_inv,
    f_dev,
    grad_y,
    forces,
    ysm,
    zsm,
    mask_pl,
    band_m,
    band_2,
    band_s,
    band_z,
    fx_recv,
    fz_recv,
    fc_recv,
    mx_send,
    mz_send,
    mx_recv,
    mz_recv,
    mc_recv,
    pk_send,
    pk_blk,
    pk_slab,
    ag_ssem,
    ag_rsem,
    f_ssem,
    f_rsem,
    m_ssem,
    m_rsem,
    pb_ssem,
    pb_rsem,
    ps_ssem,
    ps_rsem,
):
    me_s = lax.axis_index("slab")
    me_b = lax.axis_index("blk")
    chips = n_blk // 2
    chip = me_b // 2
    core = me_b % 2
    taps = smooth_weights(SMOOTH_RADIUS)

    def there(dx, dz):
        ok = None
        for d, me, n in ((dx, me_b, n_blk), (dz, me_s, n_slab)):
            if d == 0:
                continue
            now = me + d < n if d > 0 else me + d >= 0
            ok = now if ok is None else jnp.logical_and(ok, now)
        return ok

    loads = [
        pltpu.make_async_copy(src, dst, in_sem.at[i])
        for i, (src, dst) in enumerate(
            (
                (fixed_hbm, fixed_ref),
                (moving_hbm, gath.at[0]),
                (owner_hbm, owner_ref),
                (block_hbm, block_ref),
                (count_hbm, count_ref),
                (level_hbm, level_ref),
                (mask_hbm, mask_ref),
            )
        )
    ]
    for load in loads:
        load.start()

    barrier = pltpu.get_barrier_semaphore()
    for d in range(1, n_blk):
        pl.semaphore_signal(
            barrier, inc=1, device_id=(me_s, (me_b + d) % n_blk), device_id_type=MESH
        )
    for d in range(1, n_slab):
        pl.semaphore_signal(
            barrier, inc=1, device_id=((me_s + d) % n_slab, me_b), device_id_type=MESH
        )
    for dx, dz in DIRECTIONS[4:]:

        @pl.when(there(dx, dz))
        def _():
            pl.semaphore_signal(
                barrier, inc=1, device_id=(me_s + dz, me_b + dx), device_id_type=MESH
            )

    def rim_copies(x_send, z_send, x_recv, z_recv, c_recv, ssem, rsem):
        copies = []
        for i, (dx, dz) in enumerate(DIRECTIONS):
            if dz == 0:
                src, dst = x_send.at[(dx + 1) // 2], x_recv.at[(dx + 1) // 2]
            elif dx == 0:
                src, dst = z_send.at[(dz + 1) // 2], z_recv.at[(dz + 1) // 2]
            else:
                src = z_send.at[(dz + 1) // 2, :, pl.ds(16 if dx > 0 else 0, 16), :]
                dst = c_recv.at[i - 4]
            copies.append(
                pltpu.make_async_remote_copy(
                    src_ref=src,
                    dst_ref=dst,
                    send_sem=ssem.at[i],
                    recv_sem=rsem.at[i],
                    device_id=(me_s + dz, me_b + dx),
                    device_id_type=MESH,
                )
            )
        return copies

    def start_all(copies):
        for (dx, dz), copy in zip(DIRECTIONS, copies):
            pl.when(there(dx, dz))(copy.start)

    def finish_all(copies):
        for (dx, dz), copy in zip(DIRECTIONS, copies):
            pl.when(there(dx, dz))(copy.wait_send)

    def pack_rims(ext, x_send, z_send):
        flat = ext.reshape(PLANES * ROWS, LANES)
        for j in range(HALO):
            for side, at in ((0, j), (1, SIDE - HALO + j)):
                z_send[side, j] = flat[
                    pl.ds(HALO * ROWS + FIRST + at, SIDE, stride=ROWS), :
                ].astype(BF16)
                x_send[side, j] = ext[HALO + at, FIRST : FIRST + SIDE, :].astype(BF16)

    def fill_rims(copies, ext, x_recv, z_recv, c_recv):
        flat = ext.reshape(PLANES * ROWS, LANES)
        for i, (dx, dz) in enumerate(DIRECTIONS):
            at_x = 0 if dx > 0 else HALO + SIDE
            at_z = FIRST - HALO if dz > 0 else FIRST + SIDE
            region = {1: 0, 0: 1, -1: 2}[dx]
            row_at = {1: 0, 0: SMOOTH_RADIUS, -1: SMOOTH_RADIUS + SIDE}[dz]
            row_n = SIDE if dz == 0 else SMOOTH_RADIUS

            @pl.when(there(-dx, -dz))
            def _():
                copies[i].wait_recv()
                side_x, side_z = (dx + 1) // 2, (dz + 1) // 2
                for j in range(HALO):
                    if dz == 0:
                        ext[at_x + j, FIRST : FIRST + SIDE, :] = x_recv[side_x, j].astype(F32)
                    elif dx == 0:
                        flat[pl.ds(HALO * ROWS + at_z + j, SIDE, stride=ROWS), :] = z_recv[
                            side_z, j
                        ].astype(F32)
                    else:
                        rows = c_recv[i - 4, j].astype(F32)
                        rows = rows[16 - HALO :] if dx > 0 else rows[:HALO]
                        flat[pl.ds(at_x * ROWS + at_z + j, HALO, stride=ROWS), :] = rows
                if dz == 0:
                    plane = x_recv[side_x, HALO].astype(F32)
                elif dx == 0:
                    plane = z_recv[side_z, HALO].astype(F32)
                else:
                    plane = c_recv[i - 4, HALO].astype(F32)
                mask_pl[region, row_at : row_at + row_n, :] = plane[:row_n]

    lane = lax.broadcasted_iota(jnp.int32, (1, LANES), 1)

    def by_block(scalars):
        vec = jnp.full((1, LANES), scalars[3], jnp.int32)
        for g in range(3):
            vec = jnp.where(lane // SIDE == g, scalars[g], vec)
        return vec

    wide_x = jnp.where(me_b > 0, 1, 0) + jnp.where(me_b < n_blk - 1, 1, 0)
    wide_z = jnp.where(me_s > 0, 1, 0) + jnp.where(me_s < n_slab - 1, 1, 0)
    pl.semaphore_wait(barrier, n_blk - 1 + n_slab - 1 + wide_x * wide_z)

    f_copies = []
    for i, (dx, dz) in enumerate(DIRECTIONS):
        planes = pl.ds(0 if dx < 0 else SIDE - HALO, HALO)
        rows = pl.ds(0 if dz < 0 else SIDE - 16, 16)
        if dz == 0:
            src, dst = fixed_hbm.at[planes], fx_recv.at[(dx + 1) // 2]
        elif dx == 0:
            src, dst = fixed_hbm.at[:, rows], fz_recv.at[(dz + 1) // 2]
        else:
            src, dst = fixed_hbm.at[planes, rows], fc_recv.at[i - 4]
        f_copies.append(
            pltpu.make_async_remote_copy(
                src_ref=src,
                dst_ref=dst,
                send_sem=f_ssem.at[i],
                recv_sem=f_rsem.at[i],
                device_id=(me_s + dz, me_b + dx),
                device_id_type=MESH,
            )
        )
    start_all(f_copies)

    if chips == 4:
        flip_x = chip + 1 - 2 * (chip % 2)
        flip_y = chip + 2 - 4 * (chip // 2)
        away = [chip, flip_x, flip_y, 3 - chip]
    else:
        away = [(chip + chips - e) % chips for e in range(chips)]
    half = SIDE // 2

    def remote(src, dst, at, device):
        return pltpu.make_async_remote_copy(
            src_ref=src,
            dst_ref=dst,
            send_sem=ag_ssem.at[at],
            recv_sem=ag_rsem.at[at],
            device_id=device,
            device_id_type=MESH,
        )

    def piece(e, h):
        rows = pl.ds(h * half, half)
        at = 4 * e + 2 * h
        if chips != 4:
            target = (chip + e) % chips
            src = moving_hbm.at[rows]
        elif e < 3:
            target = away[e]
            src = moving_hbm.at[rows]
        else:
            target = away[2 - h]
            src = gath.at[2 * (1 + h), rows]
        return remote(src, gath.at[2 * e, rows], at, (me_s, 2 * target + core))

    def passed(e, h):
        rows = pl.ds(h * half, half)
        src = moving_hbm.at[rows] if e == 0 else gath.at[2 * e, rows]
        return remote(
            src, gath.at[2 * e + 1, rows], 4 * e + 2 * h + 1, (me_s, 2 * chip + 1 - core)
        )

    if chips == 4:
        for e, h in ((1, 0), (2, 1), (1, 1), (2, 0)):
            piece(e, h).start()
    else:
        for e in range(1, chips):
            for h in range(2):
                piece(e, h).start()
    for h in range(2):
        passed(0, h).start()

    def take(e, h):
        piece(e, h).wait_recv()
        if chips == 4 and (e, h) in ((1, 0), (2, 1)):
            piece(3, h).start()
        passed(e, h).start()

    nought = me_b // n_blk
    for ext in (f_ext, m_ext):

        @pl.loop(0, PLANES // 7)
        def _(x):
            ext[pl.ds(x * 7, 7)] = jnp.zeros((7, ROWS, LANES), F32)

    loads[0].wait()
    loads[6].wait()

    mask_pl[...] = jnp.zeros_like(mask_pl)
    own_mask = by_block([mask_ref[0, 0, g] for g in range(4)]).astype(F32)
    mask_rows = jnp.broadcast_to(own_mask, (SIDE, LANES))
    mask_pl[1, SMOOTH_RADIUS : SMOOTH_RADIUS + SIDE, :] = mask_rows

    @pl.loop(0, SIDE // 4)
    def _(x):
        at = pl.ds(HALO + x * 4, 4)
        f_ext[at, FIRST : FIRST + SIDE, :] = fixed_ref[pl.ds(x * 4, 4)].astype(F32)

    for side in range(2):
        mx_send[side, HALO] = mask_rows.astype(BF16)
        mz_send[side, HALO] = mask_rows.astype(BF16)
    for load in loads[2:6]:
        load.wait()
    places, mixes = [], []
    counts = by_block([count_ref[0, 0, g] for g in range(4)])
    at_end = lane % SIDE == SIDE - 1
    for k in range(4):
        f_x, f_z, f_y = [
            by_block([level_ref[0, 0, a, g, k] for g in range(4)]).astype(F32) / LEVELS
            for a in range(3)
        ]
        places.append(
            by_block([owner_ref[0, 0, g, k] for g in range(4)]) * LANES
            + by_block([block_ref[0, 0, g, k] for g in range(4)]) * SIDE
            + lane % SIDE
        )
        listed = jnp.where(counts > k, 1.0, 0.0)
        mixes.append(
            (
                jnp.where(at_end, 1.0, 1.0 - f_y),
                jnp.where(at_end, 0.0, f_y),
                [
                    listed * (f_x if mx else 1.0 - f_x) * (f_z if mz else 1.0 - f_z)
                    for mx, mz in ((0, 0), (1, 0), (0, 1), (1, 1))
                ],
            )
        )
    share = 1.0 / counts.astype(F32)
    sub = lax.broadcasted_iota(jnp.int32, (LANES, LANES), 0)

    @pl.loop(0, LANES // SIDE)
    def _(part):
        row = lax.broadcasted_iota(jnp.int32, (SIDE, LANES), 0) + part * SIDE
        for e in range(chips):
            for p in range(2):
                base = (2 * away[e] + (core if p == 0 else 1 - core)) * LANES
                totals = [None] * 4
                for k in range(4):
                    first = places[k] - base
                    y_stay, y_move, mix = mixes[k]
                    taken = jnp.where(
                        row == first, y_stay, jnp.where(row == first + 1, y_move, 0.0)
                    )
                    for c in range(4):
                        term = taken * mix[c]
                        totals[c] = term if k == 0 else totals[c] + term
                for c in range(4):
                    cols = slice(c * LANES, (c + 1) * LANES)
                    high = totals[c].astype(BF16)
                    low = (totals[c] - high.astype(F32)).astype(BF16)
                    at = pl.multiple_of(p * LANES + part * SIDE, SIDE)
                    select[e, pl.ds(at, SIDE), cols] = high
                    select[e, pl.ds(at + 2 * LANES, SIDE), cols] = low

    off = sub - lax.broadcasted_iota(jnp.int32, (LANES, LANES), 1)
    band = jnp.where(jnp.abs(off) <= BOX_RADIUS, 1.0, 0.0).astype(BF16)
    band_m[:, :LANES] = band
    band_m[:, LANES:] = (
        jnp.where(off == 1, 0.5, 0.0) - jnp.where(off == -1, 0.5, 0.0)
    ).astype(BF16)
    band_2[:LANES] = band
    band_2[LANES:] = band
    bell = jnp.zeros((LANES, LANES), F32)
    for t in range(2 * SMOOTH_RADIUS + 1):
        bell = jnp.where(off == t - SMOOTH_RADIUS, taps[t], bell)
    bell_hi = bell.astype(BF16)
    for part in range(2):
        rows = slice(part * LANES, (part + 1) * LANES)
        band_s[rows, :LANES] = bell_hi
        band_s[rows, LANES:] = (bell - bell_hi.astype(F32)).astype(BF16)
    ahead = lax.broadcasted_iota(jnp.int32, (SIDE, 2 * LANES), 1) - lax.broadcasted_iota(
        jnp.int32, (SIDE, 2 * LANES), 0
    )
    for b in range(6):
        bell = jnp.zeros((SIDE, 2 * LANES), F32)
        for t in range(2 * SMOOTH_RADIUS + 1):
            bell = jnp.where(ahead == FROWS * b + t, taps[t], bell)
        bell_hi = bell.astype(BF16)
        band_z[SIDE * b : SIDE * (b + 1)] = bell_hi
        band_z[SIDE * (6 + b) : SIDE * (7 + b)] = (bell - bell_hi.astype(F32)).astype(BF16)
    forces[:, 6 * FROWS :] = jnp.zeros((FPLANES // 2, 2 * LANES - 6 * FROWS, LANES), F32)

    def halves(product):
        high = product.astype(BF16)
        return jnp.concatenate([high, (product - high.astype(F32)).astype(BF16)], axis=1)

    def shifted(ref, lead, start, rows):
        return ref[(*lead, pl.ds(nought + start, rows), slice(None))]

    def z_sum(q, j, first=0, rows=FROWS):
        total = shifted(ybox, (q, j), first + 3, rows)
        for t in range(1, 5):
            total = total + shifted(ybox, (q, j), first + 3 + t, rows)
        zbox[q, j, first : first + rows] = total

    def x_sums(q, i, first=0, rows=FROWS):
        v = [zbox[q, i + t, first : first + rows] for t in range(6)]
        shared = (v[1] + v[2]) + (v[3] + v[4])
        return v[0] + shared, shared + v[5]

    def inverse(value):
        guess = pltpu.reciprocal(value, approx=True)
        return guess * (2.0 - value * guess)

    per_box = 1.0 / float((2 * BOX_RADIUS + 1) ** 3)

    def resample(first_e, last_e, h):
        at = slice(h * half, (h + 1) * half)
        rows = slice(h * half * SIDE, (h + 1) * half * SIDE)
        blocks = []
        for e in range(first_e, last_e):
            pair = [gath[2 * e + p, at].reshape(half * SIDE, LANES) for p in range(2)]
            blocks += pair + pair
        got = jnp.dot(
            jnp.concatenate(blocks, axis=1),
            select[first_e:last_e].reshape((last_e - first_e) * 4 * LANES, 4 * LANES),
            preferred_element_type=F32,
        )
        acc[rows, :] = got if first_e == 0 else acc[rows, :] + got

    if chips == 4:
        take(1, 0)
        take(2, 1)

    for i, (dx, dz) in enumerate(DIRECTIONS):
        planes = {1: slice(0, HALO), 0: slice(HALO, HALO + SIDE), -1: slice(HALO + SIDE, PLANES)}[dx]

        @pl.when(there(-dx, -dz))
        def _():
            f_copies[i].wait_recv()
            if dz == 0:
                f_ext[planes, FIRST : FIRST + SIDE] = fx_recv[(dx + 1) // 2].astype(F32)
            else:
                slab = fz_recv[(dz + 1) // 2] if dx == 0 else fc_recv[i - 4]
                slab = slab.astype(F32)
                if dz > 0:
                    f_ext[planes, :FIRST] = slab[:, 8:]
                else:
                    f_ext[planes, FIRST + SIDE :] = slab[:, :8]


    @pl.loop(0, PLANES // 7)
    def _(step):
        at = pl.ds(step * 7, 7)
        planes = f_ext[at].reshape(7 * ROWS, LANES)
        y_f = jnp.dot(planes.astype(BF16), band, preferred_element_type=F32)
        y_ff = jnp.dot(halves(planes * planes), band_2[...], preferred_element_type=F32)
        ybox[0, at] = y_f.reshape(7, ROWS, LANES)
        ybox[1, at] = y_ff.reshape(7, ROWS, LANES)

    if chips == 4:
        take(1, 1)
        take(2, 0)

    @pl.loop(0, PLANES // 2)
    def _(step):
        for j in range(2):
            for q in range(2):
                z_sum(q, 2 * step + j)

    @pl.loop(0, FPLANES // 2)
    def _(step):
        i = 2 * step
        sums = x_sums(0, i), x_sums(1, i)
        for j in range(2):
            mean = sums[0][j] * per_box
            var = sums[1][j] * per_box - mean * mean + var_eps
            f_mean[i + j] = mean
            f_inv[i + j] = inverse(var)
            f_dev[i + j] = shifted(f_ext, (i + j + 2,), 5, FROWS) - mean

    if chips != 4:
        for e in range(1, chips):
            for h in range(2):
                take(e, h)
    loads[1].wait()
    for e in range(chips - 1):
        for h in range(2):
            passed(e, h).wait_recv()
    for h in range(2):
        resample(0, chips - 1, h)
        if chips == 4:
            take(3, h)
    for h in range(2):
        passed(chips - 1, h).wait_recv()
        resample(chips - 1, chips, h)

    last_row = lax.broadcasted_iota(jnp.int32, (SIDE, LANES), 0) == SIDE - 1

    @pl.loop(0, SIDE, unroll=4)
    def _(x):
        here = pl.ds(pl.multiple_of(x * SIDE, SIDE), SIDE)
        after = pl.ds(pl.multiple_of(jnp.minimum(x + 1, SIDE - 1) * SIDE, SIDE), SIDE)
        stay = acc[here, :LANES] + acc[after, LANES : 2 * LANES]
        move = acc[here, 2 * LANES : 3 * LANES] + acc[after, 3 * LANES :]
        moved = jnp.where(last_row, move, pltpu.roll(move, SIDE - 1, 0))
        warped = ((stay + moved) * share).astype(BF16).astype(F32)
        m_ext[HALO + x, FIRST : FIRST + SIDE, :] = warped

    pack_rims(m_ext, mx_send, mz_send)
    m_copies = rim_copies(mx_send, mz_send, mx_recv, mz_recv, mc_recv, m_ssem, m_rsem)
    start_all(m_copies)

    def y_pass(planes, rows, shape):
        count = shape[0] * shape[1]
        m_now = m_ext[planes, rows].reshape(count, LANES)
        f_now = f_ext[planes, rows].reshape(count, LANES)
        y_m = jnp.dot(m_now.astype(BF16), band_m[...], preferred_element_type=F32)
        products = jnp.concatenate([halves(m_now * m_now), halves(f_now * m_now)], axis=0)
        y_p = jnp.dot(products, band_2[...], preferred_element_type=F32)
        ybox[0, planes, rows] = y_m[:, :LANES].reshape(*shape, LANES)
        grad_y[planes, rows] = y_m[:, LANES:].reshape(*shape, LANES)
        ybox[1, planes, rows] = y_p[:count].reshape(*shape, LANES)
        ybox[2, planes, rows] = y_p[count:].reshape(*shape, LANES)

    @pl.loop(0, 4)
    def _(part):
        y_pass(pl.ds(HALO + part * 8, 8), slice(FIRST, FIRST + SIDE), (8, SIDE))

    edge = 3
    inner = slice(8, 32)
    outer = (slice(0, 8), slice(32, FROWS))

    def force_rows(now, rows):
        first, n = rows.start, rows.stop - rows.start
        i = 2 * now
        sums = [x_sums(q, i, first, n) for q in range(3)]
        for j in range(2):
            at = i + j
            mean = sums[0][j] * per_box
            var = sums[1][j] * per_box - mean * mean + var_eps
            cov = sums[2][j] * per_box - f_mean[at, rows] * mean
            slope = cov * inverse(var)
            center = shifted(m_ext, (at + 2,), 5 + first, n)
            term = slope * f_inv[at, rows] * (f_dev[at, rows] - slope * (center - mean))
            region = jnp.where(at >= SMOOTH_RADIUS, 1, 0) + jnp.where(
                at >= SMOOTH_RADIUS + SIDE, 1, 0
            )
            term = jnp.where(mask_pl[region, rows] > 0.5, term, 0.0)
            steps = (
                shifted(m_ext, (at + 3,), 5 + first, n) - shifted(m_ext, (at + 1,), 5 + first, n),
                shifted(m_ext, (at + 2,), 6 + first, n) - shifted(m_ext, (at + 2,), 4 + first, n),
                2.0 * shifted(grad_y, (at + 2,), 5 + first, n),
            )
            for c in range(3):
                base = (3 * j + c) * FROWS + first
                forces[now, base : base + n] = term * steps[c]

    @pl.loop(0, SIDE // 2)
    def _(step):
        for j in range(2):
            for q in range(3):
                z_sum(q, HALO + 2 * step + j, 8, 24)

    pairs = FPLANES // 2

    @pl.loop(edge, pairs - edge)
    def _(now):
        force_rows(now, inner)

    fill_rims(m_copies, m_ext, mx_recv, mz_recv, mc_recv)
    y_pass(slice(0, HALO), slice(None), (HALO, ROWS))
    y_pass(slice(HALO + SIDE, PLANES), slice(None), (HALO, ROWS))
    y_pass(slice(HALO, HALO + SIDE), slice(0, FIRST), (SIDE, FIRST))
    y_pass(slice(HALO, HALO + SIDE), slice(FIRST + SIDE, ROWS), (SIDE, ROWS - FIRST - SIDE))

    @pl.loop(0, HALO)
    def _(step):
        for at in (step, HALO + SIDE + step):
            for q in range(3):
                z_sum(q, at)

    @pl.loop(0, SIDE // 4)
    def _(step):
        for j in range(4):
            for q in range(3):
                for rows in outer:
                    z_sum(q, HALO + 4 * step + j, rows.start, 8)

    def bell_sum(values):
        total = taps[3] * values[3]
        for t in range(3):
            total = total + taps[t] * (values[t] + values[6 - t])
        return total

    def stages(step, row_sets):
        old = jnp.maximum(step - 2, 0)
        both = jnp.dot(halves(ysm[old]), band_s[...], preferred_element_type=F32)
        both = (both[:, :LANES] + both[:, LANES:]).reshape(6, SIDE, LANES)
        for j in range(2):
            for c in range(3):
                zsm[c, 2 * old + j] = both[3 * j + c]
        mid = jnp.minimum(jnp.maximum(step - 1, 0), pairs - 1)
        both = jnp.dot(band_z[...], forces[mid].astype(BF16), preferred_element_type=F32)
        ysm[mid] = both[: 6 * SIDE] + both[6 * SIDE :]
        for rows in row_sets:
            force_rows(step, rows)

    for begin, end, row_sets in (
        (0, edge, (slice(0, FROWS),)),
        (edge, pairs - edge, outer),
        (pairs - edge, pairs, (slice(0, FROWS),)),
        (pairs, pairs + 2, ()),
    ):

        @pl.loop(begin, end)
        def _(step):
            stages(step, row_sets)

    def last_pass(step, top):
        x = 2 * step
        squares = [jnp.zeros((SIDE, LANES), F32) for _ in range(2)]
        for c in range(3):
            values = [zsm[c, x + t] for t in range(8)]
            for j in range(2):
                value = bell_sum(values[j : j + 7])
                out_ref[c, x + j] = value
                squares[j] = squares[j] + value * value
        return jnp.maximum(top, jnp.maximum(squares[0], squares[1]))

    top = lax.fori_loop(0, SIDE // 2, last_pass, jnp.zeros((SIDE, LANES), F32))
    top = jnp.max(top.reshape(4, 8, LANES), axis=0)
    write = pltpu.make_async_copy(out_ref, out_hbm, out_sem)
    write.start()

    def all_peak(top, n, slots, ssem, rsem, device):
        pk = pk_send.at[0 if slots is pk_blk else 1]
        pk[...] = top
        copies = []
        for d in range(1, n):
            copies.append(
                pltpu.make_async_remote_copy(
                    src_ref=pk,
                    dst_ref=slots.at[d],
                    send_sem=ssem.at[d],
                    recv_sem=rsem.at[d],
                    device_id=device(d),
                    device_id_type=MESH,
                )
            )
        for copy in copies:
            copy.start()
        for d, copy in enumerate(copies):
            copy.wait_recv()
            top = jnp.maximum(top, slots[d + 1])
        return top, copies

    top, blk_copies = all_peak(
        top, n_blk, pk_blk, pb_ssem, pb_rsem, lambda d: (me_s, (me_b + d) % n_blk)
    )
    top, slab_copies = all_peak(
        top, n_slab, pk_slab, ps_ssem, ps_rsem, lambda d: ((me_s + d) % n_slab, me_b)
    )
    peak = jnp.sqrt(jnp.max(top, axis=(0, 1), keepdims=True))
    scale_ref[...] = jnp.broadcast_to(step_length / (peak + peak_eps), (1, LANES))

    for e in range(chips):
        for h in range(2):
            if e > 0:
                piece(e, h).wait_send()
            passed(e, h).wait_send()
    write.wait()
    finish_all(f_copies)
    finish_all(m_copies)
    for copy in blk_copies + slab_copies:
        copy.wait_send()


def scale_kernel(in_hbm, scale_hbm, out_hbm, held, scale_ref, in_sems, out_sems, scale_sem):
    chunks = [(c, pl.ds(h * (SIDE // 2), SIDE // 2)) for c in range(3) for h in range(2)]
    fetch = [
        pltpu.make_async_copy(in_hbm.at[chunk], held.at[chunk], in_sems.at[i])
        for i, chunk in enumerate(chunks)
    ]
    store = [
        pltpu.make_async_copy(held.at[chunk], out_hbm.at[chunk], out_sems.at[i])
        for i, chunk in enumerate(chunks)
    ]
    fetch_scale = pltpu.make_async_copy(scale_hbm, scale_ref, scale_sem)
    fetch_scale.start()
    for copy in fetch:
        copy.start()
    fetch_scale.wait()
    scale = scale_ref[...].reshape(1, 1, LANES)
    for chunk, came, goes in zip(chunks, fetch, store):
        came.wait()
        held[chunk] = held[chunk] * scale
        goes.start()
    for goes in store:
        goes.wait()


def per_device(
    n_slab,
    n_blk,
    fixed_image,
    moving_image,
    fetch_owner,
    fetch_block,
    fetch_count,
    interp_level,
    block_mask,
):
    chips = n_blk // 2
    interp_level = jnp.swapaxes(interp_level, 2, 3)
    vmem = pl.BlockSpec(memory_space=pltpu.VMEM)
    small = [fetch_owner, fetch_block, fetch_count, interp_level, block_mask]
    rim = lambda planes, rows, n: pltpu.VMEM((n, planes, rows, LANES), BF16)
    sems = lambda n: pltpu.SemaphoreType.DMA((n,))
    smoothed, scale = pl.pallas_call(
        functools.partial(kernel, n_slab, n_blk),
        out_shape=(
            jax.ShapeDtypeStruct((3, SIDE, SIDE, LANES), F32),
            jax.ShapeDtypeStruct((1, LANES), F32),
        ),
        in_specs=[pl.BlockSpec(memory_space=pltpu.HBM)] * 7,
        out_specs=(pl.BlockSpec(memory_space=pltpu.HBM), vmem),
        scratch_shapes=[
            pltpu.VMEM((3, SIDE, SIDE, LANES), F32),
            pltpu.SemaphoreType.DMA,
            pltpu.VMEM((SIDE, SIDE, LANES), BF16),
            *[pltpu.SMEM(one.shape, jnp.int32) for one in small],
            sems(7),
            pltpu.VMEM((n_blk, SIDE, SIDE, LANES), BF16),
            pltpu.VMEM((chips, 4 * LANES, 4 * LANES), BF16),
            pltpu.VMEM((SIDE * SIDE, 4 * LANES), F32),
            pltpu.VMEM((PLANES, ROWS, LANES), F32),
            pltpu.VMEM((PLANES, ROWS, LANES), F32),
            pltpu.VMEM((3, PLANES, ROWS, LANES), F32),
            pltpu.VMEM((3, PLANES, FROWS, LANES), F32),
            pltpu.VMEM((FPLANES, FROWS, LANES), F32),
            pltpu.VMEM((FPLANES, FROWS, LANES), F32),
            pltpu.VMEM((FPLANES, FROWS, LANES), F32),
            pltpu.VMEM((PLANES, ROWS, LANES), F32),
            pltpu.VMEM((FPLANES // 2, 2 * LANES, LANES), F32),
            pltpu.VMEM((FPLANES // 2, 6 * SIDE, LANES), F32),
            pltpu.VMEM((3, FPLANES, SIDE, LANES), F32),
            pltpu.VMEM((3, FROWS, LANES), F32),
            pltpu.VMEM((LANES, 2 * LANES), BF16),
            pltpu.VMEM((2 * LANES, LANES), BF16),
            pltpu.VMEM((2 * LANES, 2 * LANES), BF16),
            pltpu.VMEM((12 * SIDE, 2 * LANES), BF16),
            rim(HALO, SIDE, 2),
            rim(SIDE, 16, 2),
            rim(HALO, 16, 4),
            rim(HALO + 1, SIDE, 2),
            rim(HALO + 1, SIDE, 2),
            rim(HALO + 1, SIDE, 2),
            rim(HALO + 1, SIDE, 2),
            rim(HALO + 1, 16, 4),
            pltpu.VMEM((2, 8, LANES), F32),
            pltpu.VMEM((n_blk, 8, LANES), F32),
            pltpu.VMEM((n_slab, 8, LANES), F32),
            sems(2 * n_blk),
            sems(2 * n_blk),
            sems(8),
            sems(8),
            sems(8),
            sems(8),
            sems(n_blk),
            sems(n_blk),
            sems(n_slab),
            sems(n_slab),
        ],
        compiler_params=pltpu.CompilerParams(
            collective_id=0, has_side_effects=True, vmem_limit_bytes=64 * 1024 * 1024
        ),
        name="syn_step",
    )(
        fixed_image,
        moving_image,
        fetch_owner,
        fetch_block,
        fetch_count,
        interp_level,
        block_mask,
    )
    return pl.pallas_call(
        scale_kernel,
        out_shape=jax.ShapeDtypeStruct((3, SIDE, SIDE, LANES), F32),
        in_specs=[pl.BlockSpec(memory_space=pltpu.HBM)] * 2,
        out_specs=pl.BlockSpec(memory_space=pltpu.HBM),
        scratch_shapes=[
            pltpu.VMEM((3, SIDE, SIDE, LANES), F32),
            pltpu.VMEM((1, LANES), F32),
            sems(6),
            sems(6),
            pltpu.SemaphoreType.DMA,
        ],
        compiler_params=pltpu.CompilerParams(vmem_limit_bytes=64 * 1024 * 1024),
        name="scale_step",
    )(smoothed, scale)


def solution(mesh):
    in_specs = (
        P("blk", "slab", None),
        P("blk", "slab", None),
        P("blk", "slab", None, None),
        P("blk", "slab", None, None),
        P("blk", "slab", None),
        P("blk", "slab", None, None, None),
        P("blk", "slab", None),
    )
    out_specs = P(None, "blk", "slab", None)
    return jax.shard_map(
        functools.partial(per_device, mesh.shape["slab"], mesh.shape["blk"]),
        mesh=mesh,
        in_specs=in_specs,
        out_specs=out_specs,
        check_vma=False,
    )
```

```python
import functools
import math

import jax
import jax.numpy as jnp
from jax import lax
from jax.experimental import pallas as pl
from jax.experimental.pallas import tpu as pltpu
from jax.sharding import PartitionSpec as P

LEVELS = 8
BOX_RADIUS = 2
SMOOTH_RADIUS = 3
HALO = BOX_RADIUS + SMOOTH_RADIUS

sigma_smooth = 1.5
step_length = 2.0
var_eps = 1e-05
peak_eps = 1e-06

SIDE = 32
LANES = 128
PLANES = SIDE + 2 * HALO
ROWS = 48
FIRST = 8
FPLANES = SIDE + 2 * SMOOTH_RADIUS
FROWS = 40
F32 = jnp.float32
BF16 = jnp.bfloat16
MESH = pl.DeviceIdType.MESH
DIRECTIONS = ((1, 0), (-1, 0), (0, 1), (0, -1), (1, 1), (1, -1), (-1, 1), (-1, -1))


def smooth_weights(radius):
    weights_raw = [
        math.exp(-(offset * offset) / (2.0 * sigma_smooth * sigma_smooth))
        for offset in range(-radius, radius + 1)
    ]
    weights_total = sum(weights_raw)
    return [weight_one / weights_total for weight_one in weights_raw]


def kernel(
    n_slab,
    n_blk,
    fixed_hbm,
    moving_hbm,
    owner_hbm,
    block_hbm,
    count_hbm,
    level_hbm,
    mask_hbm,
    out_hbm,
    scale_ref,
    out_ref,
    out_sem,
    fixed_ref,
    owner_ref,
    block_ref,
    count_ref,
    level_ref,
    mask_ref,
    in_sem,
    gath,
    select,
    acc,
    f_ext,
    m_ext,
    ybox,
    zbox,
    f_mean,
    f_inv,
    f_dev,
    grad_y,
    forces,
    ysm,
    zsm,
    mask_pl,
    band_m,
    band_2,
    band_s,
    fx_recv,
    fz_recv,
    fc_recv,
    mx_send,
    mz_send,
    mx_recv,
    mz_recv,
    mc_recv,
    pk_send,
    pk_blk,
    pk_slab,
    ag_ssem,
    ag_rsem,
    f_ssem,
    f_rsem,
    m_ssem,
    m_rsem,
    pb_ssem,
    pb_rsem,
    ps_ssem,
    ps_rsem,
):
    me_s = lax.axis_index("slab")
    me_b = lax.axis_index("blk")
    chips = n_blk // 2
    chip = me_b // 2
    core = me_b % 2
    taps = smooth_weights(SMOOTH_RADIUS)

    def there(dx, dz):
        ok = None
        for d, me, n in ((dx, me_b, n_blk), (dz, me_s, n_slab)):
            if d == 0:
                continue
            now = me + d < n if d > 0 else me + d >= 0
            ok = now if ok is None else jnp.logical_and(ok, now)
        return ok

    loads = [
        pltpu.make_async_copy(src, dst, in_sem.at[i])
        for i, (src, dst) in enumerate(
            (
                (fixed_hbm, fixed_ref),
                (moving_hbm, gath.at[0]),
                (owner_hbm, owner_ref),
                (block_hbm, block_ref),
                (count_hbm, count_ref),
                (level_hbm, level_ref),
                (mask_hbm, mask_ref),
            )
        )
    ]
    for load in loads:
        load.start()

    barrier = pltpu.get_barrier_semaphore()
    for d in range(1, n_blk):
        pl.semaphore_signal(
            barrier, inc=1, device_id=(me_s, (me_b + d) % n_blk), device_id_type=MESH
        )
    for d in range(1, n_slab):
        pl.semaphore_signal(
            barrier, inc=1, device_id=((me_s + d) % n_slab, me_b), device_id_type=MESH
        )
    for dx, dz in DIRECTIONS[4:]:

        @pl.when(there(dx, dz))
        def _():
            pl.semaphore_signal(
                barrier, inc=1, device_id=(me_s + dz, me_b + dx), device_id_type=MESH
            )

    def rim_copies(x_send, z_send, x_recv, z_recv, c_recv, ssem, rsem):
        copies = []
        for i, (dx, dz) in enumerate(DIRECTIONS):
            if dz == 0:
                src, dst = x_send.at[(dx + 1) // 2], x_recv.at[(dx + 1) // 2]
            elif dx == 0:
                src, dst = z_send.at[(dz + 1) // 2], z_recv.at[(dz + 1) // 2]
            else:
                src = z_send.at[(dz + 1) // 2, :, pl.ds(16 if dx > 0 else 0, 16), :]
                dst = c_recv.at[i - 4]
            copies.append(
                pltpu.make_async_remote_copy(
                    src_ref=src,
                    dst_ref=dst,
                    send_sem=ssem.at[i],
                    recv_sem=rsem.at[i],
                    device_id=(me_s + dz, me_b + dx),
                    device_id_type=MESH,
                )
            )
        return copies

    def start_all(copies):
        for (dx, dz), copy in zip(DIRECTIONS, copies):
            pl.when(there(dx, dz))(copy.start)

    def finish_all(copies):
        for (dx, dz), copy in zip(DIRECTIONS, copies):
            pl.when(there(dx, dz))(copy.wait_send)

    def pack_rims(ext, x_send, z_send):
        flat = ext.reshape(PLANES * ROWS, LANES)
        for j in range(HALO):
            for side, at in ((0, j), (1, SIDE - HALO + j)):
                z_send[side, j] = flat[
                    pl.ds(HALO * ROWS + FIRST + at, SIDE, stride=ROWS), :
                ].astype(BF16)
                x_send[side, j] = ext[HALO + at, FIRST : FIRST + SIDE, :].astype(BF16)

    def fill_rims(copies, ext, x_recv, z_recv, c_recv):
        flat = ext.reshape(PLANES * ROWS, LANES)
        for i, (dx, dz) in enumerate(DIRECTIONS):
            at_x = 0 if dx > 0 else HALO + SIDE
            at_z = FIRST - HALO if dz > 0 else FIRST + SIDE
            region = {1: 0, 0: 1, -1: 2}[dx]
            row_at = {1: 0, 0: SMOOTH_RADIUS, -1: SMOOTH_RADIUS + SIDE}[dz]
            row_n = SIDE if dz == 0 else SMOOTH_RADIUS

            @pl.when(there(-dx, -dz))
            def _():
                copies[i].wait_recv()
                side_x, side_z = (dx + 1) // 2, (dz + 1) // 2
                for j in range(HALO):
                    if dz == 0:
                        ext[at_x + j, FIRST : FIRST + SIDE, :] = x_recv[side_x, j].astype(F32)
                    elif dx == 0:
                        flat[pl.ds(HALO * ROWS + at_z + j, SIDE, stride=ROWS), :] = z_recv[
                            side_z, j
                        ].astype(F32)
                    else:
                        rows = c_recv[i - 4, j].astype(F32)
                        rows = rows[16 - HALO :] if dx > 0 else rows[:HALO]
                        flat[pl.ds(at_x * ROWS + at_z + j, HALO, stride=ROWS), :] = rows
                if dz == 0:
                    plane = x_recv[side_x, HALO].astype(F32)
                elif dx == 0:
                    plane = z_recv[side_z, HALO].astype(F32)
                else:
                    plane = c_recv[i - 4, HALO].astype(F32)
                mask_pl[region, row_at : row_at + row_n, :] = plane[:row_n]

    lane = lax.broadcasted_iota(jnp.int32, (1, LANES), 1)

    def by_block(scalars):
        vec = jnp.full((1, LANES), scalars[3], jnp.int32)
        for g in range(3):
            vec = jnp.where(lane // SIDE == g, scalars[g], vec)
        return vec

    wide_x = jnp.where(me_b > 0, 1, 0) + jnp.where(me_b < n_blk - 1, 1, 0)
    wide_z = jnp.where(me_s > 0, 1, 0) + jnp.where(me_s < n_slab - 1, 1, 0)
    pl.semaphore_wait(barrier, n_blk - 1 + n_slab - 1 + wide_x * wide_z)

    f_copies = []
    for i, (dx, dz) in enumerate(DIRECTIONS):
        planes = pl.ds(0 if dx < 0 else SIDE - HALO, HALO)
        rows = pl.ds(0 if dz < 0 else SIDE - 16, 16)
        if dz == 0:
            src, dst = fixed_hbm.at[planes], fx_recv.at[(dx + 1) // 2]
        elif dx == 0:
            src, dst = fixed_hbm.at[:, rows], fz_recv.at[(dz + 1) // 2]
        else:
            src, dst = fixed_hbm.at[planes, rows], fc_recv.at[i - 4]
        f_copies.append(
            pltpu.make_async_remote_copy(
                src_ref=src,
                dst_ref=dst,
                send_sem=f_ssem.at[i],
                recv_sem=f_rsem.at[i],
                device_id=(me_s + dz, me_b + dx),
                device_id_type=MESH,
            )
        )
    start_all(f_copies)

    if chips == 4:
        flip_x = chip + 1 - 2 * (chip % 2)
        flip_y = chip + 2 - 4 * (chip // 2)
        away = [chip, flip_x, flip_y, 3 - chip]
    else:
        away = [(chip + chips - e) % chips for e in range(chips)]
    half = SIDE // 2

    def remote(src, dst, at, device):
        return pltpu.make_async_remote_copy(
            src_ref=src,
            dst_ref=dst,
            send_sem=ag_ssem.at[at],
            recv_sem=ag_rsem.at[at],
            device_id=device,
            device_id_type=MESH,
        )

    def piece(e, h):
        rows = pl.ds(h * half, half)
        at = 4 * e + 2 * h
        if chips != 4:
            target = (chip + e) % chips
            src = moving_hbm.at[rows]
        elif e < 3:
            target = away[e]
            src = moving_hbm.at[rows]
        else:
            target = away[2 - h]
            src = gath.at[2 * (1 + h), rows]
        return remote(src, gath.at[2 * e, rows], at, (me_s, 2 * target + core))

    def passed(e, h):
        rows = pl.ds(h * half, half)
        src = moving_hbm.at[rows] if e == 0 else gath.at[2 * e, rows]
        return remote(
            src, gath.at[2 * e + 1, rows], 4 * e + 2 * h + 1, (me_s, 2 * chip + 1 - core)
        )

    if chips == 4:
        for e, h in ((1, 0), (2, 1), (1, 1), (2, 0)):
            piece(e, h).start()
    else:
        for e in range(1, chips):
            for h in range(2):
                piece(e, h).start()
    for h in range(2):
        passed(0, h).start()

    def take(e, h):
        piece(e, h).wait_recv()
        if chips == 4 and (e, h) in ((1, 0), (2, 1)):
            piece(3, h).start()
        passed(e, h).start()

    nought = me_b // n_blk
    for ext in (f_ext, m_ext):

        @pl.loop(0, PLANES // 7)
        def _(x):
            ext[pl.ds(x * 7, 7)] = jnp.zeros((7, ROWS, LANES), F32)

    loads[0].wait()
    loads[6].wait()

    mask_pl[...] = jnp.zeros_like(mask_pl)
    own_mask = by_block([mask_ref[0, 0, g] for g in range(4)]).astype(F32)
    mask_rows = jnp.broadcast_to(own_mask, (SIDE, LANES))
    mask_pl[1, SMOOTH_RADIUS : SMOOTH_RADIUS + SIDE, :] = mask_rows

    @pl.loop(0, SIDE // 4)
    def _(x):
        at = pl.ds(HALO + x * 4, 4)
        f_ext[at, FIRST : FIRST + SIDE, :] = fixed_ref[pl.ds(x * 4, 4)].astype(F32)

    for side in range(2):
        mx_send[side, HALO] = mask_rows.astype(BF16)
        mz_send[side, HALO] = mask_rows.astype(BF16)
    for load in loads[2:6]:
        load.wait()
    places, mixes = [], []
    counts = by_block([count_ref[0, 0, g] for g in range(4)])
    at_end = lane % SIDE == SIDE - 1
    for k in range(4):
        f_x, f_z, f_y = [
            by_block([level_ref[0, 0, a, g, k] for g in range(4)]).astype(F32) / LEVELS
            for a in range(3)
        ]
        places.append(
            by_block([owner_ref[0, 0, g, k] for g in range(4)]) * LANES
            + by_block([block_ref[0, 0, g, k] for g in range(4)]) * SIDE
            + lane % SIDE
        )
        listed = jnp.where(counts > k, 1.0, 0.0)
        mixes.append(
            (
                jnp.where(at_end, 1.0, 1.0 - f_y),
                jnp.where(at_end, 0.0, f_y),
                [
                    listed * (f_x if mx else 1.0 - f_x) * (f_z if mz else 1.0 - f_z)
                    for mx, mz in ((0, 0), (1, 0), (0, 1), (1, 1))
                ],
            )
        )
    share = 1.0 / counts.astype(F32)
    sub = lax.broadcasted_iota(jnp.int32, (LANES, LANES), 0)

    @pl.loop(0, LANES // SIDE)
    def _(part):
        row = lax.broadcasted_iota(jnp.int32, (SIDE, LANES), 0) + part * SIDE
        for e in range(chips):
            for p in range(2):
                base = (2 * away[e] + (core if p == 0 else 1 - core)) * LANES
                totals = [None] * 4
                for k in range(4):
                    first = places[k] - base
                    y_stay, y_move, mix = mixes[k]
                    taken = jnp.where(
                        row == first, y_stay, jnp.where(row == first + 1, y_move, 0.0)
                    )
                    for c in range(4):
                        term = taken * mix[c]
                        totals[c] = term if k == 0 else totals[c] + term
                for c in range(4):
                    cols = slice(c * LANES, (c + 1) * LANES)
                    high = totals[c].astype(BF16)
                    low = (totals[c] - high.astype(F32)).astype(BF16)
                    at = pl.multiple_of(p * LANES + part * SIDE, SIDE)
                    select[e, pl.ds(at, SIDE), cols] = high
                    select[e, pl.ds(at + 2 * LANES, SIDE), cols] = low

    off = sub - lax.broadcasted_iota(jnp.int32, (LANES, LANES), 1)
    band = jnp.where(jnp.abs(off) <= BOX_RADIUS, 1.0, 0.0).astype(BF16)
    band_m[:, :LANES] = band
    band_m[:, LANES:] = (
        jnp.where(off == 1, 0.5, 0.0) - jnp.where(off == -1, 0.5, 0.0)
    ).astype(BF16)
    band_2[:LANES] = band
    band_2[LANES:] = band
    bell = jnp.zeros((LANES, LANES), F32)
    for t in range(2 * SMOOTH_RADIUS + 1):
        bell = jnp.where(off == t - SMOOTH_RADIUS, taps[t], bell)
    bell_hi = bell.astype(BF16)
    band_s[:, :LANES] = bell_hi
    band_s[:, LANES:] = (bell - bell_hi.astype(F32)).astype(BF16)

    def halves(product):
        high = product.astype(BF16)
        return jnp.concatenate([high, (product - high.astype(F32)).astype(BF16)], axis=1)

    def shifted(ref, lead, start, rows):
        return ref[(*lead, pl.ds(nought + start, rows), slice(None))]

    def z_sum(q, j, first=0, rows=FROWS):
        total = shifted(ybox, (q, j), first + 3, rows)
        for t in range(1, 5):
            total = total + shifted(ybox, (q, j), first + 3 + t, rows)
        zbox[q, j, first : first + rows] = total

    def x_sums(q, i, first=0, rows=FROWS):
        v = [zbox[q, i + t, first : first + rows] for t in range(6)]
        shared = (v[1] + v[2]) + (v[3] + v[4])
        return v[0] + shared, shared + v[5]

    def inverse(value):
        guess = pltpu.reciprocal(value, approx=True)
        return guess * (2.0 - value * guess)

    per_box = 1.0 / float((2 * BOX_RADIUS + 1) ** 3)

    def resample(first_e, last_e, h):
        at = slice(h * half, (h + 1) * half)
        rows = slice(h * half * SIDE, (h + 1) * half * SIDE)
        blocks = []
        for e in range(first_e, last_e):
            pair = [gath[2 * e + p, at].reshape(half * SIDE, LANES) for p in range(2)]
            blocks += pair + pair
        got = jnp.dot(
            jnp.concatenate(blocks, axis=1),
            select[first_e:last_e].reshape((last_e - first_e) * 4 * LANES, 4 * LANES),
            preferred_element_type=F32,
        )
        acc[rows, :] = got if first_e == 0 else acc[rows, :] + got

    if chips == 4:
        take(1, 0)
        take(2, 1)

    for i, (dx, dz) in enumerate(DIRECTIONS):
        planes = {1: slice(0, HALO), 0: slice(HALO, HALO + SIDE), -1: slice(HALO + SIDE, PLANES)}[dx]

        @pl.when(there(-dx, -dz))
        def _():
            f_copies[i].wait_recv()
            if dz == 0:
                f_ext[planes, FIRST : FIRST + SIDE] = fx_recv[(dx + 1) // 2].astype(F32)
            else:
                slab = fz_recv[(dz + 1) // 2] if dx == 0 else fc_recv[i - 4]
                slab = slab.astype(F32)
                if dz > 0:
                    f_ext[planes, :FIRST] = slab[:, 8:]
                else:
                    f_ext[planes, FIRST + SIDE :] = slab[:, :8]


    @pl.loop(0, PLANES // 7)
    def _(step):
        at = pl.ds(step * 7, 7)
        planes = f_ext[at].reshape(7 * ROWS, LANES)
        y_f = jnp.dot(planes.astype(BF16), band, preferred_element_type=F32)
        y_ff = jnp.dot(halves(planes * planes), band_2[...], preferred_element_type=F32)
        ybox[0, at] = y_f.reshape(7, ROWS, LANES)
        ybox[1, at] = y_ff.reshape(7, ROWS, LANES)

    if chips == 4:
        take(1, 1)
        take(2, 0)

    @pl.loop(0, PLANES // 2)
    def _(step):
        for j in range(2):
            for q in range(2):
                z_sum(q, 2 * step + j)

    @pl.loop(0, FPLANES // 2)
    def _(step):
        i = 2 * step
        sums = x_sums(0, i), x_sums(1, i)
        for j in range(2):
            mean = sums[0][j] * per_box
            var = sums[1][j] * per_box - mean * mean + var_eps
            f_mean[i + j] = mean
            f_inv[i + j] = inverse(var)
            f_dev[i + j] = shifted(f_ext, (i + j + 2,), 5, FROWS) - mean

    if chips != 4:
        for e in range(1, chips):
            for h in range(2):
                take(e, h)
    loads[1].wait()
    for e in range(chips - 1):
        for h in range(2):
            passed(e, h).wait_recv()
    for h in range(2):
        resample(0, chips - 1, h)
        if chips == 4:
            take(3, h)
    for h in range(2):
        passed(chips - 1, h).wait_recv()
        resample(chips - 1, chips, h)

    last_row = lax.broadcasted_iota(jnp.int32, (SIDE, LANES), 0) == SIDE - 1

    @pl.loop(0, SIDE, unroll=4)
    def _(x):
        here = pl.ds(pl.multiple_of(x * SIDE, SIDE), SIDE)
        after = pl.ds(pl.multiple_of(jnp.minimum(x + 1, SIDE - 1) * SIDE, SIDE), SIDE)
        stay = acc[here, :LANES] + acc[after, LANES : 2 * LANES]
        move = acc[here, 2 * LANES : 3 * LANES] + acc[after, 3 * LANES :]
        moved = jnp.where(last_row, move, pltpu.roll(move, SIDE - 1, 0))
        warped = ((stay + moved) * share).astype(BF16).astype(F32)
        m_ext[HALO + x, FIRST : FIRST + SIDE, :] = warped

    pack_rims(m_ext, mx_send, mz_send)
    m_copies = rim_copies(mx_send, mz_send, mx_recv, mz_recv, mc_recv, m_ssem, m_rsem)
    start_all(m_copies)

    def y_pass(planes, rows, shape):
        count = shape[0] * shape[1]
        m_now = m_ext[planes, rows].reshape(count, LANES)
        f_now = f_ext[planes, rows].reshape(count, LANES)
        y_m = jnp.dot(m_now.astype(BF16), band_m[...], preferred_element_type=F32)
        products = jnp.concatenate([halves(m_now * m_now), halves(f_now * m_now)], axis=0)
        y_p = jnp.dot(products, band_2[...], preferred_element_type=F32)
        ybox[0, planes, rows] = y_m[:, :LANES].reshape(*shape, LANES)
        grad_y[planes, rows] = y_m[:, LANES:].reshape(*shape, LANES)
        ybox[1, planes, rows] = y_p[:count].reshape(*shape, LANES)
        ybox[2, planes, rows] = y_p[count:].reshape(*shape, LANES)

    @pl.loop(0, 4)
    def _(part):
        y_pass(pl.ds(HALO + part * 8, 8), slice(FIRST, FIRST + SIDE), (8, SIDE))

    edge = 3
    inner = slice(8, 32)
    outer = (slice(0, 8), slice(32, FROWS))

    def force_rows(now, rows):
        first, n = rows.start, rows.stop - rows.start
        i = 2 * now
        sums = [x_sums(q, i, first, n) for q in range(3)]
        for j in range(2):
            at = i + j
            mean = sums[0][j] * per_box
            var = sums[1][j] * per_box - mean * mean + var_eps
            cov = sums[2][j] * per_box - f_mean[at, rows] * mean
            slope = cov * inverse(var)
            center = shifted(m_ext, (at + 2,), 5 + first, n)
            term = slope * f_inv[at, rows] * (f_dev[at, rows] - slope * (center - mean))
            region = jnp.where(at >= SMOOTH_RADIUS, 1, 0) + jnp.where(
                at >= SMOOTH_RADIUS + SIDE, 1, 0
            )
            term = jnp.where(mask_pl[region, rows] > 0.5, term, 0.0)
            steps = (
                shifted(m_ext, (at + 3,), 5 + first, n) - shifted(m_ext, (at + 1,), 5 + first, n),
                shifted(m_ext, (at + 2,), 6 + first, n) - shifted(m_ext, (at + 2,), 4 + first, n),
                2.0 * shifted(grad_y, (at + 2,), 5 + first, n),
            )
            for c in range(3):
                base = (3 * j + c) * FROWS + first
                forces[now, base : base + n] = term * steps[c]

    @pl.loop(0, SIDE // 2)
    def _(step):
        for j in range(2):
            for q in range(3):
                z_sum(q, HALO + 2 * step + j, 8, 24)

    pairs = FPLANES // 2

    @pl.loop(edge, pairs - edge - 1, unroll=2)
    def _(now):
        force_rows(now, inner)

    force_rows(pairs - edge - 1, inner)

    fill_rims(m_copies, m_ext, mx_recv, mz_recv, mc_recv)
    y_pass(slice(0, HALO), slice(None), (HALO, ROWS))
    y_pass(slice(HALO + SIDE, PLANES), slice(None), (HALO, ROWS))
    y_pass(slice(HALO, HALO + SIDE), slice(0, FIRST), (SIDE, FIRST))
    y_pass(slice(HALO, HALO + SIDE), slice(FIRST + SIDE, ROWS), (SIDE, ROWS - FIRST - SIDE))

    @pl.loop(0, HALO)
    def _(step):
        for at in (step, HALO + SIDE + step):
            for q in range(3):
                z_sum(q, at)

    @pl.loop(0, SIDE // 4)
    def _(step):
        for j in range(4):
            for q in range(3):
                for rows in outer:
                    z_sum(q, HALO + 4 * step + j, rows.start, 8)

    def bell_sum(values):
        total = taps[3] * values[3]
        for t in range(3):
            total = total + taps[t] * (values[t] + values[6 - t])
        return total

    def stages(step, row_sets):
        old = jnp.maximum(step - 2, 0)
        for j in range(2):
            for c in range(3):
                zsm[c, 2 * old + j] = bell_sum(
                    [shifted(ysm, (old, 3 * j + c), t, SIDE) for t in range(7)]
                )
        mid = jnp.minimum(jnp.maximum(step - 1, 0), pairs - 1)
        both = jnp.dot(forces[mid].astype(BF16), band_s[...], preferred_element_type=F32)
        ysm[mid] = (both[:, :LANES] + both[:, LANES:]).reshape(6, FROWS, LANES)
        for rows in row_sets:
            force_rows(step, rows)

    for begin, end, unroll, row_sets in (
        (0, edge, edge, (slice(0, FROWS),)),
        (edge, pairs - edge - 1, 4, outer),
        (pairs - edge - 1, pairs - edge, 1, outer),
        (pairs - edge, pairs, edge, (slice(0, FROWS),)),
        (pairs, pairs + 2, 2, ()),
    ):

        @pl.loop(begin, end, unroll=unroll)
        def _(step):
            stages(step, row_sets)

    def last_pass(step, top):
        x = 2 * step
        squares = [jnp.zeros((SIDE, LANES), F32) for _ in range(2)]
        for c in range(3):
            values = [zsm[c, x + t] for t in range(8)]
            for j in range(2):
                value = bell_sum(values[j : j + 7])
                out_ref[c, x + j] = value
                squares[j] = squares[j] + value * value
        return jnp.maximum(top, jnp.maximum(squares[0], squares[1]))

    top = lax.fori_loop(
        0, SIDE // 2, last_pass, jnp.zeros((SIDE, LANES), F32), unroll=2
    )
    top = jnp.max(top.reshape(4, 8, LANES), axis=0)
    write = pltpu.make_async_copy(out_ref, out_hbm, out_sem)
    write.start()

    def all_peak(top, n, slots, ssem, rsem, device):
        pk = pk_send.at[0 if slots is pk_blk else 1]
        pk[...] = top
        copies = []
        for d in range(1, n):
            copies.append(
                pltpu.make_async_remote_copy(
                    src_ref=pk,
                    dst_ref=slots.at[d],
                    send_sem=ssem.at[d],
                    recv_sem=rsem.at[d],
                    device_id=device(d),
                    device_id_type=MESH,
                )
            )
        for copy in copies:
            copy.start()
        for d, copy in enumerate(copies):
            copy.wait_recv()
            top = jnp.maximum(top, slots[d + 1])
        return top, copies

    top, blk_copies = all_peak(
        top, n_blk, pk_blk, pb_ssem, pb_rsem, lambda d: (me_s, (me_b + d) % n_blk)
    )
    top, slab_copies = all_peak(
        top, n_slab, pk_slab, ps_ssem, ps_rsem, lambda d: ((me_s + d) % n_slab, me_b)
    )
    peak = jnp.sqrt(jnp.max(top, axis=(0, 1), keepdims=True))
    scale_ref[...] = jnp.broadcast_to(step_length / (peak + peak_eps), (1, LANES))

    for e in range(chips):
        for h in range(2):
            if e > 0:
                piece(e, h).wait_send()
            passed(e, h).wait_send()
    write.wait()
    finish_all(f_copies)
    finish_all(m_copies)
    for copy in blk_copies + slab_copies:
        copy.wait_send()


def scale_kernel(in_hbm, scale_hbm, out_hbm, held, scale_ref, in_sems, out_sems, scale_sem):
    chunks = [(c, pl.ds(h * (SIDE // 2), SIDE // 2)) for c in range(3) for h in range(2)]
    fetch = [
        pltpu.make_async_copy(in_hbm.at[chunk], held.at[chunk], in_sems.at[i])
        for i, chunk in enumerate(chunks)
    ]
    store = [
        pltpu.make_async_copy(held.at[chunk], out_hbm.at[chunk], out_sems.at[i])
        for i, chunk in enumerate(chunks)
    ]
    fetch_scale = pltpu.make_async_copy(scale_hbm, scale_ref, scale_sem)
    fetch_scale.start()
    for copy in fetch:
        copy.start()
    fetch_scale.wait()
    scale = scale_ref[...].reshape(1, 1, LANES)
    for chunk, came, goes in zip(chunks, fetch, store):
        came.wait()
        held[chunk] = held[chunk] * scale
        goes.start()
    for goes in store:
        goes.wait()


def per_device(
    n_slab,
    n_blk,
    fixed_image,
    moving_image,
    fetch_owner,
    fetch_block,
    fetch_count,
    interp_level,
    block_mask,
):
    chips = n_blk // 2
    interp_level = jnp.swapaxes(interp_level, 2, 3)
    vmem = pl.BlockSpec(memory_space=pltpu.VMEM)
    small = [fetch_owner, fetch_block, fetch_count, interp_level, block_mask]
    rim = lambda planes, rows, n: pltpu.VMEM((n, planes, rows, LANES), BF16)
    sems = lambda n: pltpu.SemaphoreType.DMA((n,))
    smoothed, scale = pl.pallas_call(
        functools.partial(kernel, n_slab, n_blk),
        out_shape=(
            jax.ShapeDtypeStruct((3, SIDE, SIDE, LANES), F32),
            jax.ShapeDtypeStruct((1, LANES), F32),
        ),
        in_specs=[pl.BlockSpec(memory_space=pltpu.HBM)] * 7,
        out_specs=(pl.BlockSpec(memory_space=pltpu.HBM), vmem),
        scratch_shapes=[
            pltpu.VMEM((3, SIDE, SIDE, LANES), F32),
            pltpu.SemaphoreType.DMA,
            pltpu.VMEM((SIDE, SIDE, LANES), BF16),
            *[pltpu.SMEM(one.shape, jnp.int32) for one in small],
            sems(7),
            pltpu.VMEM((n_blk, SIDE, SIDE, LANES), BF16),
            pltpu.VMEM((chips, 4 * LANES, 4 * LANES), BF16),
            pltpu.VMEM((SIDE * SIDE, 4 * LANES), F32),
            pltpu.VMEM((PLANES, ROWS, LANES), F32),
            pltpu.VMEM((PLANES, ROWS, LANES), F32),
            pltpu.VMEM((3, PLANES, ROWS, LANES), F32),
            pltpu.VMEM((3, PLANES, FROWS, LANES), F32),
            pltpu.VMEM((FPLANES, FROWS, LANES), F32),
            pltpu.VMEM((FPLANES, FROWS, LANES), F32),
            pltpu.VMEM((FPLANES, FROWS, LANES), F32),
            pltpu.VMEM((PLANES, ROWS, LANES), F32),
            pltpu.VMEM((FPLANES // 2, 6 * FROWS, LANES), F32),
            pltpu.VMEM((FPLANES // 2, 6, FROWS, LANES), F32),
            pltpu.VMEM((3, FPLANES, SIDE, LANES), F32),
            pltpu.VMEM((3, FROWS, LANES), F32),
            pltpu.VMEM((LANES, 2 * LANES), BF16),
            pltpu.VMEM((2 * LANES, LANES), BF16),
            pltpu.VMEM((LANES, 2 * LANES), BF16),
            rim(HALO, SIDE, 2),
            rim(SIDE, 16, 2),
            rim(HALO, 16, 4),
            rim(HALO + 1, SIDE, 2),
            rim(HALO + 1, SIDE, 2),
            rim(HALO + 1, SIDE, 2),
            rim(HALO + 1, SIDE, 2),
            rim(HALO + 1, 16, 4),
            pltpu.VMEM((2, 8, LANES), F32),
            pltpu.VMEM((n_blk, 8, LANES), F32),
            pltpu.VMEM((n_slab, 8, LANES), F32),
            sems(2 * n_blk),
            sems(2 * n_blk),
            sems(8),
            sems(8),
            sems(8),
            sems(8),
            sems(n_blk),
            sems(n_blk),
            sems(n_slab),
            sems(n_slab),
        ],
        compiler_params=pltpu.CompilerParams(
            collective_id=0, has_side_effects=True, vmem_limit_bytes=64 * 1024 * 1024
        ),
        name="syn_step",
    )(
        fixed_image,
        moving_image,
        fetch_owner,
        fetch_block,
        fetch_count,
        interp_level,
        block_mask,
    )
    return pl.pallas_call(
        scale_kernel,
        out_shape=jax.ShapeDtypeStruct((3, SIDE, SIDE, LANES), F32),
        in_specs=[pl.BlockSpec(memory_space=pltpu.HBM)] * 2,
        out_specs=pl.BlockSpec(memory_space=pltpu.HBM),
        scratch_shapes=[
            pltpu.VMEM((3, SIDE, SIDE, LANES), F32),
            pltpu.VMEM((1, LANES), F32),
            sems(6),
            sems(6),
            pltpu.SemaphoreType.DMA,
        ],
        compiler_params=pltpu.CompilerParams(vmem_limit_bytes=64 * 1024 * 1024),
        name="scale_step",
    )(smoothed, scale)


def solution(mesh):
    in_specs = (
        P("blk", "slab", None),
        P("blk", "slab", None),
        P("blk", "slab", None, None),
        P("blk", "slab", None, None),
        P("blk", "slab", None),
        P("blk", "slab", None, None, None),
        P("blk", "slab", None),
    )
    out_specs = P(None, "blk", "slab", None)
    return jax.shard_map(
        functools.partial(per_device, mesh.shape["slab"], mesh.shape["blk"]),
        mesh=mesh,
        in_specs=in_specs,
        out_specs=out_specs,
        check_vma=False,
    )
```
